32 devices in a mesh: dp: 8 (over z, x), tensor: 4 (over y, core).
Axes of the slice: x: 2, y: 2, z: 4, core: 2. Of those that a mesh axis runs over, the one named last changes fastest.
Arguments:
- tokens: bfloat16 [2048, 1024], P(('dp', 'tensor')), may hold values from -6 to 6
- segments: int32 [2048], P('dp'), may hold values from 0 to 2, as said below
- zx_weight: bfloat16 [2, 1024, 1536], P(None, 'dp', 'tensor'), may hold values from -0.1875 to 0.1875
- dt_weight: bfloat16 [1024, 24], P('dp', 'tensor'), may hold values from -0.1875 to 0.1875
- query_weight: bfloat16 [1024, 512], P('dp', 'tensor'), may hold values from -0.1875 to 0.1875
- ssm_out_weight: bfloat16 [1536, 1024], P('tensor', 'dp'), may hold values from -0.3125 to 0.3125
- attn_out_weight: bfloat16 [512, 1024], P('tensor', 'dp'), may hold values from -2 to 2
- gate_up_weight: bfloat16 [2, 1024, 2048], P(None, 'dp', 'tensor'), may hold values from -0.1875 to 0.1875
- down_weight: bfloat16 [2048, 1024], P('tensor', 'dp'), may hold values from -0.125 to 0.125
- shared_weight: bfloat16 [1024, 512], P(('dp', 'tensor')), may hold values from -0.1875 to 0.1875
- norm_gains: float32 [2, 1024], replicated, may hold values from 0.25 to 1.75
- conv_params: float32 [5, 1792], replicated, may hold values from -3 to 3
- head_params: float32 [3, 24], replicated, may hold values from -7 to 2.7, as said below
- cotangent: bfloat16 [2048, 1024], P(('dp', 'tensor')), may hold values from -6 to 6
Outputs:
- output: bfloat16 [2048, 1024], P(('dp', 'tensor'))
- tokens_grad: float32 [2048, 1024], P(('dp', 'tensor'))
- zx_grad: float32 [2, 1024, 1536], P(None, 'dp', 'tensor')
- dt_grad: float32 [1024, 24], P('dp', 'tensor')
- query_grad: float32 [1024, 512], P('dp', 'tensor')
- ssm_out_grad: float32 [1536, 1024], P('tensor', 'dp')
- attn_out_grad: float32 [512, 1024], P('tensor', 'dp')
- gate_up_grad: float32 [2, 1024, 2048], P(None, 'dp', 'tensor')
- down_grad: float32 [2048, 1024], P('tensor', 'dp')
- shared_grad: float32 [1024, 512], P(('dp', 'tensor'))
- gains_grad: float32 [2, 1024], replicated
- conv_grad: float32 [5, 1792], replicated
- head_grad: float32 [3, 24], replicated
The draws below stay inside these ranges and needn't reach their ends.
Inputs may be any that keep to these rules, and one draw needn't show every extreme that they name: `segments`: each sequence of 256 tokens holds three documents numbered 0, 1, 2 in order; the first and the last hold at least min(60, 32) tokens each; the middle one runs at least from the last token of the sequence's first quarter to the first token of its last quarter. `head_params`: row 0 holds step biases, row 1 logarithms of decay rates, row 2 skip gains.
All inputs are finite; a program needn't handle non-finite values.
Results may differ from the reference program's by a relative error of at most 0.014.
Values may be sent and summed in bfloat16 or wider, within the bound.
No kernel may reach another device: no remote copies, remote signals or barrier semaphores. Data moves between devices by JAX's collectives and lax.ppermute only.
A program may use at most 128 MiB of HBM per device.

```python
import math
import jax
import jax.numpy as jnp
from jax import lax

D = 1024
MH = 24
HDM = 64
NSTATE = 128
CONV = 4
QH = 8
KVH = 2
HD = 64
FF = 2048
SEQ = 256
DSSM = 1536
KVBC = 512
TOKENS = 2048
N_DP = 8
N_TENSOR = 4


def draw_segments(key, part):
    key = jax.random.fold_in(key, 11)
    first_key, second_key = jax.random.split(key)
    seq_count = TOKENS // SEQ
    least_doc = max(1, min(60, SEQ // (2 * N_TENSOR)))
    first_cut = jax.random.randint(first_key, (seq_count, 1), least_doc, SEQ // N_TENSOR)
    second_cut = jax.random.randint(second_key, (seq_count, 1), SEQ - SEQ // N_TENSOR + 1, SEQ - least_doc + 1)
    places = lax.broadcasted_iota(jnp.int32, (seq_count, SEQ), 1)
    numbers = (places >= first_cut).astype(jnp.int32) + (places >= second_cut).astype(jnp.int32)
    return numbers.reshape(TOKENS)


def draw_head_params(key, part):
    key = jax.random.fold_in(key, 23)
    unit_draw = jax.random.uniform(key, (3, MH), jnp.float32)
    bottom = jnp.array([-6.0, 0.0, 0.5], jnp.float32)
    upper = jnp.array([-2.0, 2.7, 1.5], jnp.float32)
    return bottom[:, None] + (upper - bottom)[:, None] * unit_draw


def spiked(entries, key, source, target, shards_of, factor):
    def block_of(position):
        return (jnp.arange(entries.shape[position]) // (entries.shape[position] // shards_of)).reshape((-1,) + (1,) * (entries.ndim - 1 - position))

    near = jax.random.permutation(key, shards_of)[block_of(target)]
    far = (block_of(target) + shards_of // 2) % shards_of
    return jnp.where((block_of(source) == near) | (block_of(source) == far), factor * entries, entries)


def levels(key, shape, cuts, low, largest):
    def one(dim, blocks):
        steps = jax.random.uniform(jax.random.fold_in(jax.random.fold_in(key, 6), dim), (blocks,), jnp.float32, low / len(cuts), largest / len(cuts))
        return jnp.repeat(jnp.exp(steps), shape[dim] // blocks).reshape((-1,) + (1,) * (len(shape) - dim - 1))

    gain = one(*cuts[0])
    for cut in cuts[1:]:
        gain = gain * one(*cut)
    return gain


def bell_draw(own_key, extent, width, limit, shards=(), kind=jnp.bfloat16):
    values = jax.random.normal(own_key, extent, jnp.float32) * width
    if len(shards) > 0:
        values = levels(own_key, extent, shards, -0.22, 0.18) * values
    return jnp.clip(values, min=-limit, max=limit).astype(kind)


def gaussian_with(rng, shape, width, limit, cuts, heavy, kind=jnp.bfloat16):
    values = width * jax.random.normal(rng, shape, jnp.float32)
    if cuts:
        values = values * levels(rng, shape, cuts, -0.22, 0.18)
    return jnp.clip(spiked(values, jax.random.fold_in(rng, 3), *heavy), -limit, limit).astype(kind)


def setup_inputs(seed: int = 0) -> dict:
    streams_of = jax.random.split(jax.random.key(seed), 15)
    return {
        "tokens": gaussian_with(streams_of[0], (TOKENS, D), 1.0, 6.0, ((0, 32),), (0, 1, 32, 2.75)),
        "segments": draw_segments(jax.random.fold_in(streams_of[14], 71), 0),
        "zx_weight": bell_draw(streams_of[2], (2, D, DSSM), D ** -0.5, 0.1875, ((1, 8), (2, 4))),
        "dt_weight": bell_draw(streams_of[3], (D, MH), D ** -0.5, 0.1875, ((0, 8), (1, 4))),
        "query_weight": bell_draw(streams_of[4], (D, QH * HD), D ** -0.5, 0.1875, ((0, 8), (1, 4))),
        "ssm_out_weight": bell_draw(streams_of[5], (DSSM, D), (DSSM // 4) ** -0.5, 0.3125, ((0, 4), (1, 8))),
        "attn_out_weight": bell_draw(streams_of[6], (QH * HD, D), (QH * HD // 64) ** -0.5, 2.0, ((0, 4), (1, 8))),
        "gate_up_weight": bell_draw(streams_of[7], (2, D, FF), D ** -0.5, 0.1875, ((1, 8), (2, 4))),
        "down_weight": bell_draw(streams_of[8], (FF, D), FF ** -0.5, 0.125, ((0, 4), (1, 8))),
        "shared_weight": bell_draw(streams_of[9], (D, KVBC), D ** -0.5, 0.1875, ((0, 32),)),
        "norm_gains": jnp.clip(1.0 + 0.15 * jax.random.normal(streams_of[10], (2, D), jnp.float32), 0.25, 1.75),
        "conv_params": bell_draw(streams_of[11], (CONV + 1, DSSM + 2 * NSTATE), 0.5, 3.0, (), jnp.float32),
        "head_params": draw_head_params(jax.random.fold_in(streams_of[14], 71), 0),
        "cotangent": gaussian_with(streams_of[13], (TOKENS, D), 1.0, 6.0, ((0, 32),), (0, 1, 32, 2.75)),
    }


@jax.custom_vjp
def low(v):
    return lax.optimization_barrier(v.astype(jnp.bfloat16)).astype(jnp.float32)

@jax.custom_vjp
def low_back(v):
    return v

def low_keep(v):
    return (low(v), None)

def low_pass(kept, grad):
    return (grad,)

def back_keep(v):
    return (v, None)

def back_low(kept, grad):
    return (low(grad),)
low.defvjp(low_keep, low_pass)
low_back.defvjp(back_keep, back_low)
EPSILON = 1e-05
HIGHEST = lax.Precision.HIGHEST

def matmul(op_left, op_right):
    return jnp.dot(op_left, op_right, precision=HIGHEST)

def rms_norm(values, scale_vec):
    return values * lax.rsqrt(lax.optimization_barrier(jnp.mean(values * values, axis=-1, keepdims=True)) + EPSILON) * scale_vec

def causal_conv(values, segment, taps_all):
    running = taps_all[-1] + taps_all[-2] * values
    for offset in range(1, taps_all.shape[0] - 1):
        shifted = jnp.concatenate([jnp.zeros_like(values[..., :offset, :]), values[..., :-offset, :]], axis=-2)
        same_doc = (segment[..., offset:] == segment[..., :-offset]).astype(values.dtype)
        same_doc = jnp.concatenate([jnp.zeros_like(same_doc[..., :offset]), same_doc], axis=-1)
        running = running + taps_all[-2 - offset] * shifted * same_doc[..., None]
    return running

def doc_mask(segment):
    length = segment.shape[0]
    row_index = lax.broadcasted_iota(jnp.int32, (length, length), 0)
    col_index = lax.broadcasted_iota(jnp.int32, (length, length), 1)
    return jnp.logical_and(row_index >= col_index, segment[:, None] == segment[None, :])

def mix_sequence(x_conv, b_state, c_state, step_size, decay_sum, gate_z, queries, key_rows, value_rows, segment, skip_gain):
    length = x_conv.shape[0]
    head_count = step_size.shape[1]
    mask_bool = doc_mask(segment)
    mask_float = mask_bool.astype(x_conv.dtype)
    gram_mat = matmul(c_state, b_state.T)
    gram_heads = low_back(jnp.broadcast_to(gram_mat, (head_count, length, length)))
    log_gap = decay_sum.T[:, :, None] - decay_sum.T[:, None, :]
    decay_mat = jnp.exp(jnp.where(mask_bool, log_gap, 0.0)) * mask_float
    mix_weights = low(gram_heads * decay_mat * step_size.T[:, None, :])
    x_heads = x_conv.reshape(length, head_count, HDM)
    y_heads = low_back(jnp.einsum('hij,jhp->ihp', mix_weights, x_heads, precision=HIGHEST))
    out_heads = y_heads + skip_gain[None, :, None] * x_heads
    gated_out = low(out_heads.reshape(length, -1) * jax.nn.silu(gate_z))
    q_heads = queries.reshape(length, QH, HD)
    k_heads = jnp.repeat(key_rows.reshape(length, KVH, HD), QH // KVH, axis=1)
    v_heads = jnp.repeat(value_rows.reshape(length, KVH, HD), QH // KVH, axis=1)
    scores = low_back(jnp.einsum('ihd,jhd->hij', q_heads, k_heads, precision=HIGHEST) * (1.0 / math.sqrt(HD)))
    masked = jnp.where(mask_bool, scores, -1000000000.0)
    row_max = lax.optimization_barrier(jnp.max(masked, axis=-1, keepdims=True))
    exp_scores = jnp.exp(masked - row_max)
    attn_probs = low(exp_scores / lax.optimization_barrier(jnp.sum(exp_scores, axis=-1, keepdims=True)))
    attn_out = low_back(low(jnp.einsum('hij,jhd->ihd', attn_probs, v_heads, precision=HIGHEST).reshape(length, QH * HD)))
    return (gated_out, attn_out)

def forward_group(token_rows, segment_rows, weight_set):
    zx_weight, dt_weight, query_weight, ssm_out_weight, attn_out_weight, gate_up_weight, down_weight, shared_weight, gain_set, conv_set, head_set = weight_set
    seq_count, length = segment_rows.shape
    kv_width = KVH * HD
    normed_one = low(rms_norm(token_rows, gain_set[0]))
    shared_proj = low_back(low(matmul(normed_one, shared_weight)))
    gate_z = low_back(matmul(normed_one, zx_weight[0]))
    x_raw = low_back(matmul(normed_one, zx_weight[1]))
    step_raw = low_back(matmul(normed_one, dt_weight))
    queries = low_back(low(matmul(normed_one, query_weight)))
    conv_input = jnp.concatenate([x_raw, shared_proj[:, 2 * kv_width:]], axis=1).reshape(seq_count, length, -1)
    conv_act = jax.nn.silu(causal_conv(conv_input, segment_rows, conv_set))
    x_conv = low(conv_act[..., :DSSM])
    b_state = low(conv_act[..., DSSM:DSSM + NSTATE])
    c_state = low(conv_act[..., DSSM + NSTATE:])
    step_size = jax.nn.softplus(step_raw.reshape(seq_count, length, MH) + head_set[0])
    decay_sum = jnp.cumsum(step_size * -jnp.exp(head_set[1]), axis=1)
    checked = jax.checkpoint(mix_sequence)
    gated_out, attn_out = lax.map(lambda seq_items: checked(*seq_items, head_set[2]), (x_conv, b_state, c_state, step_size, decay_sum, gate_z.reshape(seq_count, length, DSSM), queries.reshape(seq_count, length, QH * HD), shared_proj[:, :kv_width].reshape(seq_count, length, kv_width), shared_proj[:, kv_width:2 * kv_width].reshape(seq_count, length, kv_width), segment_rows))
    mixer_sum = low_back(matmul(gated_out.reshape(-1, DSSM), ssm_out_weight) + matmul(attn_out.reshape(-1, QH * HD), attn_out_weight))
    hidden = token_rows + mixer_sum
    normed_two = low(rms_norm(hidden, gain_set[1]))
    gate_proj = low_back(matmul(normed_two, gate_up_weight[0]))
    up_proj = low_back(matmul(normed_two, gate_up_weight[1]))
    ffn_act = low(jax.nn.silu(gate_proj) * up_proj)
    return hidden + matmul(ffn_act, down_weight)

def reference(tokens, segments, zx_weight, dt_weight, query_weight, ssm_out_weight, attn_out_weight, gate_up_weight, down_weight, shared_weight, norm_gains, conv_params, head_params, cotangent):
    per_block = math.gcd(N_DP, max(1, 4096 // SEQ))
    block_count = N_DP // per_block
    weight_set = (zx_weight.astype(jnp.float32), dt_weight.astype(jnp.float32), query_weight.astype(jnp.float32), ssm_out_weight.astype(jnp.float32), attn_out_weight.astype(jnp.float32), gate_up_weight.astype(jnp.float32), down_weight.astype(jnp.float32), shared_weight.astype(jnp.float32), norm_gains.astype(jnp.float32), conv_params.astype(jnp.float32), head_params.astype(jnp.float32))
    token_blocks = tokens.astype(jnp.float32).reshape(block_count, per_block * SEQ, D)
    segment_blocks = segments.reshape(block_count, per_block, SEQ)
    cot_blocks = cotangent.astype(jnp.float32).reshape(block_count, per_block * SEQ, D)

    def accumulate(grad_sums, block_item):
        token_block, segment_block, cot_block = block_item
        block_out, pullback = jax.vjp(lambda token_rows, weights_now: forward_group(token_rows, segment_block, weights_now), token_block, weight_set)
        token_grad, weight_grads = pullback(cot_block)
        return (jax.tree.map(jnp.add, grad_sums, weight_grads), (block_out, token_grad))
    zero_sums = jax.tree.map(jnp.zeros_like, weight_set)
    grad_sums, (outputs, token_grads) = lax.scan(accumulate, zero_sums, (token_blocks, segment_blocks, cot_blocks))
    return (outputs.reshape(TOKENS, D).astype(jnp.bfloat16), token_grads.reshape(TOKENS, D), grad_sums[0], grad_sums[1], grad_sums[2], grad_sums[3], grad_sums[4], grad_sums[5], grad_sums[6], grad_sums[7], grad_sums[8], grad_sums[9], grad_sums[10])
```

```python
import math

import jax
import jax.numpy as jnp
from jax import lax
from jax.sharding import PartitionSpec as P

HDM = 64
NSTATE = 128
QH = 8
KVH = 2
HD = 64


EPSILON = 1e-05
FLOAT = jnp.float32
BFLOAT = jnp.bfloat16


def rms_norm(values, scale_vec):
    return (
        values * lax.rsqrt(jnp.mean(values * values, axis=-1, keepdims=True) + EPSILON) * scale_vec
    )


def causal_conv(values, segment, taps_all):
    running = taps_all[-1] + taps_all[-2] * values
    for offset in range(1, taps_all.shape[0] - 1):
        shifted = jnp.concatenate(
            [jnp.zeros_like(values[..., :offset, :]), values[..., :-offset, :]], axis=-2
        )
        same_doc = (segment[..., offset:] == segment[..., :-offset]).astype(values.dtype)
        same_doc = jnp.concatenate([jnp.zeros_like(same_doc[..., :offset]), same_doc], axis=-1)
        running = running + taps_all[-2 - offset] * shifted * same_doc[..., None]
    return running


def doc_mask(segment):
    length = segment.shape[0]
    row_index = lax.broadcasted_iota(jnp.int32, (length, length), 0)
    col_index = lax.broadcasted_iota(jnp.int32, (length, length), 1)
    return jnp.logical_and(row_index >= col_index, segment[:, None] == segment[None, :])


def einsum_f32(pattern, op_left, op_right):
    return jnp.einsum(pattern, op_left, op_right, preferred_element_type=jnp.float32)


def silu_gate(gate_proj, up_proj):
    return jax.nn.silu(gate_proj) * up_proj


def swap(values, axis, count, bits):
    return lax.ppermute(values, axis, [(i, i ^ bits) for i in range(count)])


def stages_of(count):
    top = count.bit_length() - 1
    groups = []
    while top > 0:
        low = max(0, top - 2)
        groups.append([m << low for m in range(1, 1 << (top - low))])
        top = low
    return groups


def block_order(count):
    order = [0]
    for group in stages_of(count):
        order = order + [r ^ m for m in group for r in order]
    return order


def reorder(values, index, count):
    blocks = values.reshape(values.shape[0], count, -1)
    for bit in range(count.bit_length() - 1):
        halves = blocks.reshape(values.shape[0], -1, 2, 1 << bit, blocks.shape[-1])
        flipped = jnp.flip(halves, axis=2)
        blocks = jnp.where((index >> bit) & 1 == 1, flipped, halves).reshape(blocks.shape)
    return blocks


def to_relative(values, index, count):
    blocks = reorder(values, index, count)
    return jnp.concatenate([blocks[:, r] for r in block_order(count)], axis=1)


def from_relative(values, index, count):
    order = block_order(count)
    blocks = values.reshape(values.shape[0], count, -1)
    plain = jnp.concatenate([blocks[:, order.index(r)] for r in range(count)], axis=1)
    return reorder(plain, index, count).reshape(values.shape)


def gather_dp(piece, count):
    parts = [piece]
    for group in stages_of(count):
        parts = parts + [swap(p, "dp", count, m) for m in group for p in parts]
    return jnp.concatenate(parts, axis=0)


def scatter_dp(left, right, count):
    groups = stages_of(count)
    size = left.shape[1]
    total = None
    for group in reversed(groups):
        share = size // (len(group) + 1)
        if total is None:
            kept = einsum_f32("ld,lc->dc", left[:, :share], right)
            sent = [
                einsum_f32("ld,lc->dc", left[:, k * share : (k + 1) * share], right).astype(BFLOAT)
                for k in range(1, len(group) + 1)
            ]
        else:
            kept = total[:share]
            sent = [
                total[k * share : (k + 1) * share].astype(BFLOAT) for k in range(1, len(group) + 1)
            ]
        for m, part in zip(group, sent):
            kept = kept + swap(part, "dp", count, m).astype(FLOAT)
        total = kept
        size = share
    return total


def sum_tensor(partial, index, axis):
    size = partial.shape[axis] // 4
    core, half = index & 1, index >> 1
    blocks = [lax.slice_in_dim(partial, k * size, (k + 1) * size, axis=axis) for k in range(4)]
    at_core = core == 0
    keep = [jnp.where(at_core, blocks[2 * y], blocks[2 * y + 1]) for y in range(2)]
    give = [jnp.where(at_core, blocks[2 * y + 1], blocks[2 * y]) for y in range(2)]
    got = swap(jnp.stack(give), "tensor", 4, 1)
    sums = [keep[y] + got[y] for y in range(2)]
    mine = jnp.where(half == 0, sums[0], sums[1])
    other = jnp.where(half == 0, sums[1], sums[0])
    return mine + swap(other.astype(BFLOAT), "tensor", 4, 2).astype(FLOAT)


def gather_tensor(values):
    return lax.all_gather(values, "tensor", axis=0, tiled=True)


def sum_all(values, count):
    def group_sum(items, axis, axis_count, bits):
        parts = [items] + [swap(items, axis, axis_count, m) for m in bits]
        while len(parts) > 1:
            parts = [parts[k] + parts[k + 1] for k in range(0, len(parts), 2)]
        return parts[0]

    total = group_sum(values, "tensor", 4, [1, 2, 3])
    for group in stages_of(count):
        total = group_sum(total, "dp", count, group)
    return total


def per_device(
    count,
    tokens,
    segments,
    zx_weight,
    dt_weight,
    query_weight,
    ssm_out_weight,
    attn_out_weight,
    gate_up_weight,
    down_weight,
    shared_weight,
    norm_gains,
    conv_params,
    head_params,
    cotangent,
):
    shard_index = lax.axis_index("tensor")
    dp_index = lax.axis_index("dp")
    length = segments.shape[0]
    rows = zx_weight.shape[1]
    head_local = dt_weight.shape[1]
    width_local = zx_weight.shape[2]
    query_cols = query_weight.shape[1]
    query_local = query_cols // HD
    ff_local = down_weight.shape[0]
    kv_width = KVH * HD
    score_scale = 1.0 / math.sqrt(HD)
    share_rows = shared_weight.shape[0]
    share_cols = shared_weight.shape[1]

    shared_pack = shared_weight.reshape(share_rows, 4, share_cols // 4)
    shared_pack = jnp.concatenate([shared_pack[:, k] for k in range(4)], axis=0)
    dt_pad = jnp.pad(dt_weight, ((0, 0), (0, 128 - head_local)))
    shared_got = gather_dp(shared_pack, count)
    in_full = gather_dp(
        jnp.concatenate([zx_weight[0], zx_weight[1], query_weight, dt_pad], axis=1), count
    )
    out_full = gather_dp(
        jnp.concatenate([ssm_out_weight, attn_out_weight], axis=0).T, count
    )
    gu_full = gather_dp(jnp.concatenate([gate_up_weight[0], gate_up_weight[1]], axis=1), count)
    down_full = gather_dp(down_weight.T, count)
    shared_got = shared_got.reshape(count, 4, share_rows, share_cols // 4)
    shared_got = jnp.concatenate([shared_got[:, k] for k in range(4)], axis=-1)
    near = jnp.stack([shared_got, swap(shared_got, "tensor", 4, 2)])
    both = jnp.stack([near, swap(near, "tensor", 4, 1)])
    both = jnp.where(shard_index & 1 == 1, both[::-1], both)
    both = jnp.where(shard_index >> 1 == 1, both[:, ::-1], both)
    shared_full = both.transpose(2, 1, 0, 3, 4).reshape(count * rows, share_cols)

    token_f = to_relative(tokens, dp_index, count).astype(FLOAT)
    cot_local = to_relative(cotangent, dp_index, count)
    gains = to_relative(norm_gains, dp_index, count)

    head_mine = lax.dynamic_slice_in_dim(head_params, shard_index * head_local, head_local, 1)
    bc_start = conv_params.shape[1] - 2 * NSTATE
    conv_mine = jnp.concatenate(
        [
            lax.dynamic_slice_in_dim(conv_params, shard_index * width_local, width_local, 1),
            conv_params[:, bc_start:],
        ],
        axis=1,
    )
    normed_one, norm_one_back = jax.vjp(rms_norm, token_f, gains[0])
    normed_rows = gather_tensor(normed_one.astype(BFLOAT))
    shared_proj = einsum_f32("ld,dk->lk", normed_rows, shared_full).astype(BFLOAT)
    projected = einsum_f32("ld,dc->lc", normed_rows, in_full)
    gate_z = projected[:, :width_local]
    x_raw = projected[:, width_local : 2 * width_local]
    queries = projected[:, 2 * width_local : 2 * width_local + query_cols].astype(BFLOAT)
    dt_start = 2 * width_local + query_cols
    step_raw = projected[:, dt_start : dt_start + head_local]
    mask_bool = doc_mask(segments)
    mask_float = mask_bool.astype(FLOAT)

    def conv_piece(x_part, bc_part, taps_all):
        return jax.nn.silu(
            causal_conv(jnp.concatenate([x_part, bc_part], axis=1), segments, taps_all)
        )

    conv_act, conv_back = jax.vjp(
        conv_piece, x_raw, shared_proj[:, 2 * kv_width :].astype(FLOAT), conv_mine
    )
    x_conv = conv_act[:, :width_local].astype(BFLOAT)
    b_state = conv_act[:, width_local : width_local + NSTATE].astype(BFLOAT)
    c_state = conv_act[:, width_local + NSTATE :].astype(BFLOAT)
    lower = (
        lax.broadcasted_iota(jnp.int32, (length, length), 0)
        >= lax.broadcasted_iota(jnp.int32, (length, length), 1)
    ).astype(FLOAT)

    def decay_piece(raw_steps, bias_vec, log_rate):
        step_vals = jax.nn.softplus(raw_steps + bias_vec)
        sums = jnp.dot(lower, step_vals * -jnp.exp(log_rate), precision=lax.Precision.HIGHEST)
        return (step_vals, sums)

    (step_size, decay_sum), decay_back = jax.vjp(decay_piece, step_raw, head_mine[0], head_mine[1])
    gram_mat = einsum_f32("in,jn->ij", c_state, b_state)

    def weight_piece(gram_heads, step_vals, sum_vals):
        log_gap = sum_vals.T[:, :, None] - sum_vals.T[:, None, :]
        decay_mat = jnp.exp(jnp.where(mask_bool, log_gap, 0.0)) * mask_float
        return gram_heads * decay_mat * step_vals.T[:, None, :]

    mix_weights, weight_back = jax.vjp(
        weight_piece, jnp.broadcast_to(gram_mat, (head_local, length, length)), step_size, decay_sum
    )
    weights_low = mix_weights.astype(BFLOAT)
    x_heads = x_conv.reshape(length, head_local, HDM)
    y_heads = einsum_f32("hij,jhp->ihp", weights_low, x_heads)

    def gate_piece(y_part, x_part, z_part, skip_gain):
        return (y_part + skip_gain[None, :, None] * x_part).reshape(length, -1) * jax.nn.silu(
            z_part
        )

    gated_out, gate_back = jax.vjp(gate_piece, y_heads, x_heads.astype(FLOAT), gate_z, head_mine[2])
    gated_low = gated_out.astype(BFLOAT)
    kv_owner = (shard_index * query_local) // (QH // KVH)
    key_rows = lax.dynamic_slice_in_dim(shared_proj, kv_owner * HD, HD, 1)
    value_rows = lax.dynamic_slice_in_dim(shared_proj, kv_width + kv_owner * HD, HD, 1)
    query_heads = queries.reshape(length, query_local, HD)
    scores = einsum_f32("ihd,jd->hij", query_heads, key_rows) * score_scale
    masked = jnp.where(mask_bool, scores, -1000000000.0)
    row_max = jnp.max(masked, axis=-1, keepdims=True)
    exp_scores = jnp.exp(masked - row_max)
    softmax_rows = exp_scores / jnp.sum(exp_scores, axis=-1, keepdims=True)
    probs_low = softmax_rows.astype(BFLOAT)
    attn_low = einsum_f32("hij,jd->ihd", probs_low, value_rows).reshape(length, -1).astype(BFLOAT)
    mixed_low = jnp.concatenate([gated_low, attn_low], axis=1)
    mixer_terms = einsum_f32("lc,dc->ld", mixed_low, out_full)
    hidden = token_f + sum_tensor(mixer_terms, shard_index, 0)
    normed_two, norm_two_back = jax.vjp(rms_norm, hidden, gains[1])
    ffn_rows = gather_tensor(normed_two.astype(BFLOAT))
    cot_rows = gather_tensor(cot_local)
    gate_up = einsum_f32("ld,df->lf", ffn_rows, gu_full)
    ffn_act, act_back = jax.vjp(silu_gate, gate_up[:, :ff_local], gate_up[:, ff_local:])
    act_low = ffn_act.astype(BFLOAT)
    act_grad = einsum_f32("ld,df->lf", cot_rows, down_full)
    gate_grad, up_grad = act_back(act_grad)
    gu_low = jnp.concatenate([gate_grad.astype(BFLOAT), up_grad.astype(BFLOAT)], axis=1)
    ffn_input_grad = einsum_f32("lf,df->ld", gu_low, gu_full)
    normed_two_grad = sum_tensor(ffn_input_grad, shard_index, 0)
    hidden_norm_grad, gain_two_grad = norm_two_back(normed_two_grad)
    hidden_grad = cot_local.astype(FLOAT) + hidden_norm_grad
    mix_grad_rows = gather_tensor(hidden_grad.astype(BFLOAT))
    gu_sum = scatter_dp(ffn_rows, gu_low, count)
    down_sum = scatter_dp(cot_rows, act_low, count)
    ffn_sum = sum_tensor(einsum_f32("lf,df->ld", act_low, down_full), shard_index, 0)
    output = (hidden + ffn_sum).astype(BFLOAT)

    mixed_grad = einsum_f32("ld,dc->lc", mix_grad_rows, out_full)
    gated_grad = mixed_grad[:, :width_local]
    attn_grad = mixed_grad[:, width_local:]
    out_sum = scatter_dp(mix_grad_rows, mixed_low, count)
    y_grad, x_skip_grad, z_grad, skip_grad = gate_back(gated_grad)
    y_low = y_grad.astype(BFLOAT)
    z_low = z_grad.astype(BFLOAT)
    weights_grad = einsum_f32("ihp,jhp->hij", y_low, x_heads)
    x_conv_grad = x_skip_grad + einsum_f32("hij,ihp->jhp", weights_low, y_low)
    gram_grad, step_grad, sum_grad = weight_back(weights_grad)
    gram_low = gram_grad.astype(BFLOAT)
    c_grad = einsum_f32("hij,jn->in", gram_low, b_state)
    b_grad = einsum_f32("hij,in->jn", gram_low, c_state)
    raw_step_grad, bias_grad, rate_grad = decay_back((step_grad, sum_grad))
    x_raw_grad, bc_raw_grad, taps_grad = conv_back(
        jnp.concatenate([x_conv_grad.reshape(length, -1), b_grad, c_grad], axis=1)
    )
    out_low = attn_grad.astype(BFLOAT).reshape(length, query_local, HD)
    value_grad = einsum_f32("hij,ihd->jd", probs_low, out_low)
    prob_grad = einsum_f32("ihd,jd->hij", out_low, value_rows)
    score_grad = softmax_rows * (
        prob_grad - jnp.sum(softmax_rows * prob_grad, axis=-1, keepdims=True)
    )
    score_low = score_grad.astype(BFLOAT)
    query_grad_rows = (
        (einsum_f32("hij,jd->ihd", score_low, key_rows) * score_scale)
        .reshape(length, -1)
        .astype(BFLOAT)
    )
    key_grad = einsum_f32("hij,ihd->jd", score_low, query_heads) * score_scale
    at_first = kv_owner == 0
    key_terms = jnp.concatenate(
        [jnp.where(at_first, key_grad, 0.0), jnp.where(at_first, 0.0, key_grad)], axis=1
    )
    value_terms = jnp.concatenate(
        [jnp.where(at_first, value_grad, 0.0), jnp.where(at_first, 0.0, value_grad)], axis=1
    )
    x_raw_low = x_raw_grad.astype(BFLOAT)
    step_low = raw_step_grad.astype(BFLOAT)
    shared_terms = jnp.concatenate([key_terms, value_terms, bc_raw_grad], axis=1)
    block_low = sum_tensor(shared_terms, shard_index, 1).astype(BFLOAT)
    block_width = share_cols // 4
    shared_mine = lax.dynamic_slice_in_dim(shared_full, shard_index * block_width, block_width, 1)
    step_pad = jnp.pad(step_low, ((0, 0), (0, 128 - head_local)))
    in_low = jnp.concatenate([z_low, x_raw_low, query_grad_rows, step_pad], axis=1)
    in_sum = scatter_dp(normed_rows, in_low, count)
    block_sum = scatter_dp(normed_rows, block_low, count)
    normed_one_terms = einsum_f32("lc,dc->ld", in_low, in_full) + einsum_f32(
        "lk,dk->ld", block_low, shared_mine
    )
    normed_one_grad = sum_tensor(normed_one_terms, shard_index, 0)
    token_norm_grad, gain_one_grad = norm_one_back(normed_one_grad)
    tokens_grad = from_relative(hidden_grad + token_norm_grad, dp_index, count)
    shared_sum = lax.all_to_all(
        block_sum, "tensor", split_axis=0, concat_axis=1, tiled=True
    )

    conv_full = lax.dynamic_update_slice_in_dim(
        jnp.zeros_like(conv_params), taps_grad[:, :width_local], shard_index * width_local, 1
    )
    conv_full = conv_full.at[:, bc_start:].set(taps_grad[:, width_local:])
    head_full = lax.dynamic_update_slice_in_dim(
        jnp.zeros_like(head_params),
        jnp.stack([bias_grad, rate_grad, skip_grad]),
        shard_index * head_local,
        1,
    )
    gains_grad = from_relative(jnp.stack([gain_one_grad, gain_two_grad]), dp_index, count)
    pieces = (gains_grad, conv_full, head_full)
    flat = jnp.concatenate([p.reshape(-1) for p in pieces])
    wide = -(-flat.shape[0] // 1024) * 1024
    summed = sum_all(jnp.pad(flat, (0, wide - flat.shape[0])).reshape(-1, 128), count).reshape(-1)
    small = []
    start = 0
    for p in pieces:
        small.append(summed[start : start + p.size].reshape(p.shape))
        start += p.size
    return (
        from_relative(output, dp_index, count),
        tokens_grad,
        jnp.stack([in_sum[:, :width_local], in_sum[:, width_local : 2 * width_local]]),
        in_sum[:, dt_start : dt_start + head_local],
        in_sum[:, 2 * width_local : dt_start],
        out_sum[:, :width_local].T,
        out_sum[:, width_local:].T,
        jnp.stack([gu_sum[:, :ff_local], gu_sum[:, ff_local:]]),
        down_sum.T,
        shared_sum,
        small[0],
        small[1],
        small[2],
    )


def solution(mesh):
    count = mesh.shape["dp"]
    placed = (
        P(("dp", "tensor"), None),
        P("dp"),
        P(None, "dp", "tensor"),
        P("dp", "tensor"),
        P("dp", "tensor"),
        P("tensor", "dp"),
        P("tensor", "dp"),
        P(None, "dp", "tensor"),
        P("tensor", "dp"),
        P(("dp", "tensor"), None),
        P(),
        P(),
        P(),
        P(("dp", "tensor"), None),
    )

    def body(*arrays):
        return per_device(count, *arrays)

    return jax.shard_map(
        body,
        mesh=mesh,
        in_specs=placed,
        out_specs=(
            P(("dp", "tensor"), None),
            P(("dp", "tensor"), None),
            P(None, "dp", "tensor"),
            P("dp", "tensor"),
            P("dp", "tensor"),
            P("tensor", "dp"),
            P("tensor", "dp"),
            P(None, "dp", "tensor"),
            P("tensor", "dp"),
            P(("dp", "tensor"), None),
            P(),
            P(),
            P(),
        ),
        check_vma=False,
    )
```

```python
import functools
import math

import jax
import jax.numpy as jnp
from jax import lax
from jax.experimental import pallas as pl
from jax.experimental.pallas import tpu as pltpu
from jax.sharding import PartitionSpec as P

HDM = 64
NSTATE = 128
QH = 8
KVH = 2
HD = 64


EPSILON = 1e-05
FLOAT = jnp.float32
BFLOAT = jnp.bfloat16
WHOLE = pl.BlockSpec()


def rms_norm(values, scale_vec):
    return (
        values * lax.rsqrt(jnp.mean(values * values, axis=-1, keepdims=True) + EPSILON) * scale_vec
    )


def einsum_f32(pattern, op_left, op_right):
    return jnp.einsum(pattern, op_left, op_right, preferred_element_type=jnp.float32)


def silu_gate(gate_proj, up_proj):
    return jax.nn.silu(gate_proj) * up_proj


def swap(values, axis, count, bits):
    return lax.ppermute(values, axis, [(i, i ^ bits) for i in range(count)])


def stages_of(count):
    top = count.bit_length() - 1
    groups = []
    while top > 0:
        low = max(0, top - 2)
        groups.append([m << low for m in range(1, 1 << (top - low))])
        top = low
    return groups


def block_order(count):
    order = [0]
    for group in stages_of(count):
        order = order + [r ^ m for m in group for r in order]
    return order


def relocate_kernel(order, to_relative, index_ref, *refs):
    for source, target in zip(refs[: len(refs) // 2], refs[len(refs) // 2 :]):
        block = source.shape[1] // len(order)
        for k, r in enumerate(order):
            here = slice(k * block, (k + 1) * block)
            there = pl.ds(pl.multiple_of((index_ref[0] ^ r) * block, block), block)
            if to_relative:
                target[:, here] = source[:, there]
            else:
                target[:, there] = source[:, here]


def relocate(arrays, index, count, to_relative):
    order = block_order(count)
    if arrays[0].shape[1] // count % 128 == 0:
        return call(
            functools.partial(relocate_kernel, order, to_relative),
            [(a.shape, a.dtype) for a in arrays],
            index[None],
            *arrays,
        )
    places = jnp.array(order, jnp.int32) ^ index
    if not to_relative:
        places = jnp.argsort(places)
    moved = [a.reshape(a.shape[0], count, -1)[:, places].reshape(a.shape) for a in arrays]
    return moved


def together(*values):
    return lax.optimization_barrier(values)


def stack_kernel(*refs):
    *parts, out_ref = refs
    start = 0
    for part in parts:
        out_ref[start : start + part.shape[0], :] = part[...]
        start += part.shape[0]


def stacked(parts):
    rows = sum(p.shape[0] for p in parts)
    return pl.pallas_call(
        stack_kernel,
        out_shape=jax.ShapeDtypeStruct((rows, parts[0].shape[1]), parts[0].dtype),
        in_specs=[WHOLE] * len(parts),
        out_specs=WHOLE,
        compiler_params=pltpu.CompilerParams(vmem_limit_bytes=16 * 1024 * 1024),
        cost_estimate=pl.CostEstimate(flops=1000, bytes_accessed=1000, transcendentals=0),
    )(*parts)


def gather(stack, have, groups, count):
    parts, places = [stack], [have]
    for k, group in enumerate(groups):
        if k > 0:
            stack = stacked(parts)
            have = [r for p in places for r in p]
        parts = [stack] + [swap(stack, "dp", count, m) for m in group]
        places = [have] + [[r ^ m for r in have] for m in group]
    return parts, places


def joined(parts, places):
    return stacked(parts), [r for p in places for r in p]


def two(parts, places):
    far = parts[1] if len(parts) == 2 else stacked(parts[1:])
    return (parts[0], far), places


def column_runs(places, order):
    found = []
    for have in places:
        runs = []
        for row, r in enumerate(have):
            col = order.index(r)
            if runs and runs[-1][0] + runs[-1][2] == col:
                runs[-1] = (runs[-1][0], runs[-1][1], runs[-1][2] + 1)
            else:
                runs.append((col, row, 1))
        found.append(runs)
    return found


def products_kernel(runs_of, block, widths, *refs):
    lefts, rights, outs = refs[: len(widths)], refs[len(widths) : 2 * len(widths)], refs[2 * len(widths) :]
    start = 0
    for left, right, width in zip(lefts, rights, widths):
        right_now = right[...]
        for out, runs in zip(outs, runs_of):
            row = 0
            for col, n in runs:
                found = dot(left[:, col * block : (col + n) * block], right_now, 0, 0)
                out[row * block : (row + n) * block, start : start + width] = found.astype(out.dtype)
                row += n
        start += width


def parted(pairs, order, group):
    block = pairs[0][0].shape[1] // len(order)
    span = 0
    for m in group:
        span |= m
    stay = [r for r in order if r & span == 0]
    runs_of = []
    for blocks in [stay] + [[r ^ m for r in stay] for m in group]:
        runs = []
        for r in blocks:
            col = order.index(r)
            if runs and sum(runs[-1]) == col:
                runs[-1] = (runs[-1][0], runs[-1][1] + 1)
            else:
                runs.append((col, 1))
        runs_of.append(runs)
    widths = [right.shape[1] for _, right in pairs]
    shape = (len(stay) * block, sum(widths))
    kept, *sent = pl.pallas_call(
        functools.partial(products_kernel, runs_of, block, widths),
        out_shape=[jax.ShapeDtypeStruct(shape, FLOAT)]
        + [jax.ShapeDtypeStruct(shape, BFLOAT)] * len(group),
        in_specs=[WHOLE] * (2 * len(pairs)),
        out_specs=[WHOLE] * (1 + len(group)),
        compiler_params=pltpu.CompilerParams(vmem_limit_bytes=16 * 1024 * 1024),
        cost_estimate=pl.CostEstimate(flops=1000, bytes_accessed=1000, transcendentals=0),
    )(*[left for left, _ in pairs], *[right for _, right in pairs])
    return kept, sent, stay


def send(sent, group, count):
    return [swap(part, "dp", count, m) for m, part in zip(group, sent)]


def add(kept, got):
    for part in got:
        kept = kept + part.astype(FLOAT)
    return kept


def split(total, order, group, sizes):
    span = 0
    for m in group:
        span |= m
    stay = [r for r in order if r & span == 0]

    def rows(blocks):
        parts = []
        start = 0
        for size in sizes:
            parts += [total[start + order.index(r) * size :][:size] for r in blocks]
            start += size * len(order)
        return jnp.concatenate(parts, axis=0)

    return rows(stay), [rows([r ^ m for r in stay]).astype(BFLOAT) for m in group], stay


def finish(total, order, groups, count, sizes=None):
    if sizes is None:
        sizes = [total.shape[0] // len(order)]
    kept, got = total, []
    for group in groups:
        kept, sent, order = split(add(kept, got), order, group, sizes)
        got = send(sent, group, count)
    return kept, got


def dot(left, right, left_dim=1, right_dim=0):
    return lax.dot_general(
        left, right, (((left_dim,), (right_dim,)), ((), ())), preferred_element_type=FLOAT
    )


def exact_dot(left, right):
    return jnp.dot(left, right, precision=lax.Precision.HIGHEST, preferred_element_type=FLOAT)


def sigmoid(values):
    return 1.0 / (1.0 + jnp.exp(-values))


def softplus(values):
    return jnp.maximum(values, 0.0) + jnp.log1p(jnp.exp(-jnp.abs(values)))


def lanes_of(shape):
    return lax.broadcasted_iota(jnp.int32, shape, 1)


def same_document(seg_wide, offset):
    if offset == 0:
        return None
    row = lax.broadcasted_iota(jnp.int32, seg_wide.shape, 0)
    same = jnp.logical_and(pltpu.roll(seg_wide, offset, 0) == seg_wide, row >= offset)
    return jnp.where(same, 1.0, 0.0)


def square_mask(seg_wide, seg_row):
    length = seg_wide.shape[0]
    row = lax.broadcasted_iota(jnp.int32, (length, length), 0)
    col = lax.broadcasted_iota(jnp.int32, (length, length), 1)
    wide = jnp.concatenate([seg_wide] * (length // 128), axis=1)
    return jnp.logical_and(row >= col, wide == seg_row[0:1, :])


def triangle(length, flip):
    row = lax.broadcasted_iota(jnp.int32, (length, length), 0)
    col = lax.broadcasted_iota(jnp.int32, (length, length), 1)
    return jnp.where(row <= col if flip else row >= col, 1.0, 0.0)


def head_lanes(values, head, lane):
    return jnp.where((lane >= HDM) == (head == 1), values, jnp.zeros_like(values))


def softmax_of(queries, keys, mask, head, lane):
    scores = dot(head_lanes(queries, head, lane), keys, 1, 1) * (1.0 / math.sqrt(HD))
    masked = jnp.where(mask, scores, -1000000000.0)
    grown = jnp.exp(masked - jnp.max(masked, axis=-1, keepdims=True))
    return grown / jnp.sum(grown, axis=-1, keepdims=True)


def views(ref, widths):
    found = []
    start = 0
    for width in widths:
        found.append(ref.at[:, start : start + width])
        start += width
    return found


def kept_views(ref, width):
    return views(ref, (width + 256, width + 256, 128, 128, ref.shape[0]))


def low_views(ref, width):
    return views(ref, (width + 256, 128, 256))


def mixer_kernel(
    heads, owner_ref, normed_ref, near_ref, far_ref, shared_ref, taps_ref, head_ref, seg_ref, seg_row_ref,
    kept_ref, low_ref, pre_gate_ref, attn_ref,
):
    conv_in_ref, conv_pre_ref, step_ref, decay_ref, gram_ref = kept_views(kept_ref, pre_gate_ref.shape[1])
    conv_low_ref, query_ref, kv_ref = low_views(low_ref, pre_gate_ref.shape[1])
    length = normed_ref.shape[0]
    half = near_ref.shape[0]
    width = pre_gate_ref.shape[1]
    conv_width = conv_in_ref.shape[1]
    normed = normed_ref[...]
    taps = taps_ref[...]
    seg = seg_ref[...]
    mask = square_mask(seg, seg_row_ref[...])
    lead = dot(normed[:, :half], near_ref[:, 128:]) + dot(normed[:, half:], far_ref[:, 128:])
    x_raw = lead[:, 256:]
    shared = dot(normed, shared_ref[...]).astype(BFLOAT)
    queries = lead[:, :128].astype(BFLOAT)
    query_ref[...] = queries
    lane = lanes_of((length, 128))
    keep_half = (lane >= HD) == (owner_ref[0] == 1)
    shared_f = shared.astype(FLOAT)
    keys = jnp.where(keep_half, shared_f[:, :128], pltpu.roll(shared_f[:, :128], HD, 1)).astype(BFLOAT)
    values = jnp.where(keep_half, shared_f[:, 128:256], pltpu.roll(shared_f[:, 128:256], HD, 1)).astype(BFLOAT)
    kv_ref[:, :128] = keys
    kv_ref[:, 128:] = values
    outs = [dot(softmax_of(queries, keys, mask, h, lane).astype(BFLOAT), values) for h in range(2)]
    attn_ref[...] = jnp.where(lane < HD, outs[0], outs[1]).astype(BFLOAT)
    step_pre = lead[:, 128:256] + head_ref[0:1, :]
    step_ref[...] = step_pre
    step_size = softplus(step_pre)
    decay = exact_dot(triangle(length, False), step_size * -jnp.exp(head_ref[1:2, :]))
    decay_ref[...] = decay
    sames = [same_document(seg, o) for o in range(4)]
    for start in range(0, conv_width, 128):
        cols = slice(start, start + 128)
        if start < width:
            u = x_raw[:, cols]
        else:
            u = shared_f[:, 256 + start - width : 256 + start - width + 128]
        conv_in_ref[:, cols] = u
        pre = taps[4:5, cols] + taps[3:4, cols] * u
        for o in range(1, 4):
            pre = pre + taps[3 - o : 4 - o, cols] * (pltpu.roll(u, o, 0) * sames[o])
        conv_pre_ref[:, cols] = pre
        conv_low_ref[:, cols] = (pre * sigmoid(pre)).astype(BFLOAT)
    b_state = conv_low_ref[:, width : width + 128]
    c_state = conv_low_ref[:, width + 128 :]
    gram = dot(c_state, b_state, 1, 1)
    gram_ref[...] = gram
    step_rows, decay_rows = step_size.T, decay.T
    for pair in range(heads // 2):
        cols = slice(128 * pair, 128 * pair + 128)
        x_pair = conv_low_ref[:, cols]
        found = []
        for h in (2 * pair, 2 * pair + 1):
            gap = decay[:, h : h + 1] - decay_rows[h : h + 1, :]
            grown = jnp.where(mask, jnp.exp(jnp.where(mask, gap, 0.0)), 0.0)
            found.append(dot((gram * grown * step_rows[h : h + 1, :]).astype(BFLOAT), x_pair))
        y_pair = jnp.where(lane < HDM, found[0], found[1])
        pre_gate_ref[:, cols] = y_pair + taps[5:6, cols] * x_pair.astype(FLOAT)


def pieces_of(terms, at_core, axis):
    size = terms.shape[axis] // 4
    blocks = [lax.slice_in_dim(terms, k * size, (k + 1) * size, axis=axis) for k in range(4)]
    keep = [jnp.where(at_core, blocks[2 * y], blocks[2 * y + 1]) for y in range(2)]
    give = [jnp.where(at_core, blocks[2 * y + 1], blocks[2 * y]) for y in range(2)]
    return keep, give


def gate_kernel(
    core_ref, normed_ref, near_ref, far_ref, pre_gate_ref, attn_ref, gates_ref, mixed_ref, keep_ref, give_ref
):
    half = near_ref.shape[0]
    width = pre_gate_ref.shape[1]
    normed = normed_ref[...]
    gate_z = dot(normed[:, :half], near_ref[:, :width]) + dot(normed[:, half:], far_ref[:, :width])
    gates_ref[:, :width] = gate_z
    gates_ref[:, width:] = pre_gate_ref[...]
    gated = (pre_gate_ref[...] * (gate_z * sigmoid(gate_z))).astype(BFLOAT)
    mixed_ref[:, :width] = gated
    mixed_ref[:, width:] = attn_ref[...]
    mixed = mixed_ref[...]
    at_core = core_ref[0] == 0
    start = 0
    for part in (near_ref, far_ref):
        terms = dot(mixed, part[:, width:], 1, 1)
        cols = slice(start, start + part.shape[0])
        start += part.shape[0]
        keep, give = pieces_of(terms, at_core, 0)
        for y in range(2):
            keep_ref[y, :, cols] = keep[y]
            give_ref[y, :, cols] = give[y]


def input_back_kernel(
    core_ref, in_low_ref, zq_ref, block_ref, early_near_ref, early_far_ref, near_ref, far_ref,
    shared_ref, keep_ref, give_ref,
):
    width = zq_ref.shape[1] - 128
    x_low, step_low = in_low_ref[:, :width], in_low_ref[:, width:]
    z_low, query_low = zq_ref[:, :width], zq_ref[:, width:]
    block = block_ref[...]
    at_core = core_ref[0] == 0
    start = 0
    for early, part in ((early_near_ref, near_ref), (early_far_ref, far_ref)):
        cols = slice(start, start + part.shape[0])
        start += part.shape[0]
        terms = (
            dot(x_low, early[:, 384:], 1, 1)
            + dot(query_low, early[:, 128:256], 1, 1)
            + dot(step_low, early[:, 256:384], 1, 1)
            + dot(z_low, part[:, :width], 1, 1)
            + dot(block, shared_ref[cols, :], 1, 1)
        )
        keep, give = pieces_of(terms, at_core, 0)
        for y in range(2):
            keep_ref[y, :, cols] = keep[y]
            give_ref[y, :, cols] = give[y]


def gate_back_kernel(
    owner_ref, grad_ref, near_ref, far_ref, gates_ref, low_ref, seg_ref, seg_row_ref,
    zq_ref, pre_grad_ref, skip_ref, kv_grad_ref,
):
    half = near_ref.shape[0]
    width = pre_grad_ref.shape[1]
    conv_low_ref, query_ref, kv_ref = low_views(low_ref, width)
    grad = grad_ref[...]
    mixed_grad = dot(grad[:, :half], near_ref[:, width:]) + dot(grad[:, half:], far_ref[:, width:])
    gated_grad = mixed_grad[:, :width]
    gate_z = gates_ref[:, :width]
    s = sigmoid(gate_z)
    pre_grad = gated_grad * (gate_z * s)
    pre_grad_ref[...] = pre_grad
    zq_ref[:, :width] = (gated_grad * gates_ref[:, width:] * (s * (1.0 + gate_z * (1.0 - s)))).astype(BFLOAT)
    skip = jnp.sum(pre_grad * conv_low_ref[:, :width].astype(FLOAT), axis=0, keepdims=True)
    row = lax.broadcasted_iota(jnp.int32, (width, 128), 0)
    col = lax.broadcasted_iota(jnp.int32, (width, 128), 1)
    of_head = jnp.where(jnp.logical_and(row >= col * HDM, row < (col + 1) * HDM), 1.0, 0.0)
    skip_ref[...] = exact_dot(jnp.broadcast_to(skip, (8, width)), of_head)
    lane = lanes_of((grad.shape[0], 128))
    out_low = mixed_grad[:, width:].astype(BFLOAT)
    mask = square_mask(seg_ref[...], seg_row_ref[...])
    queries, keys, values = query_ref[...], kv_ref[:, :128], kv_ref[:, 128:]
    query_grads, key_sum, value_sum = [], 0.0, 0.0
    for h in range(2):
        probs = softmax_of(queries, keys, mask, h, lane)
        out_head = head_lanes(out_low, h, lane)
        prob_grad = dot(out_head, values, 1, 1)
        score = probs * (prob_grad - jnp.sum(probs * prob_grad, axis=-1, keepdims=True))
        score_low = score.astype(BFLOAT)
        query_grads.append(dot(score_low, keys))
        key_sum = key_sum + dot(score_low, head_lanes(queries, h, lane), 0, 0)
        value_sum = value_sum + dot(probs.astype(BFLOAT), out_head, 0, 0)
    scale = 1.0 / math.sqrt(HD)
    zq_ref[:, width:] = (jnp.where(lane < HD, query_grads[0], query_grads[1]) * scale).astype(BFLOAT)
    mine = (lane >= HD) == (owner_ref[0] == 1)
    for k, total in enumerate((key_sum * scale, value_sum)):
        both = total + pltpu.roll(total, HD, 1)
        kv_grad_ref[:, 128 * k : 128 * k + 128] = jnp.where(mine, both, 0.0)


def mixer_back_kernel(
    heads, owner_ref, pre_grad_ref, kept_ref, low_ref, kv_grad_ref, taps_ref, head_ref, seg_ref, seg_row_ref,
    in_low_ref, taps_grad_ref, head_grad_ref, share_ref, act_grad_ref,
):
    conv_in_ref, conv_pre_ref, step_ref, decay_ref, gram_ref = kept_views(kept_ref, pre_grad_ref.shape[1])
    conv_low_ref = low_views(low_ref, pre_grad_ref.shape[1])[0]
    length = pre_grad_ref.shape[0]
    width = pre_grad_ref.shape[1]
    conv_width = conv_in_ref.shape[1]
    taps = taps_ref[...]
    seg = seg_ref[...]
    mask = square_mask(seg, seg_row_ref[...])
    lane = lanes_of((length, 128))
    step_pre = step_ref[...]
    step_size = softplus(step_pre)
    decay = decay_ref[...]
    step_rows, decay_rows = step_size.T, decay.T
    gram = gram_ref[...]
    b_state = conv_low_ref[:, width : width + 128]
    c_state = conv_low_ref[:, width + 128 :]
    b_grad, c_grad = 0.0, 0.0
    step_grad_rows, row_sums = [], jnp.zeros((length, 128), FLOAT)
    for pair in range(heads // 2):
        cols = slice(128 * pair, 128 * pair + 128)
        x_pair = conv_low_ref[:, cols]
        pre_grad = pre_grad_ref[:, cols]
        y_pair = pre_grad.astype(BFLOAT)
        found = []
        for k in range(2):
            h = 2 * pair + k
            gap = decay[:, h : h + 1] - decay_rows[h : h + 1, :]
            grown = jnp.where(mask, jnp.exp(jnp.where(mask, gap, 0.0)), 0.0)
            step_row = step_rows[h : h + 1, :]
            y_head = head_lanes(y_pair, k, lane)
            weights_grad = dot(y_head, x_pair, 1, 1)
            shaped = weights_grad * grown
            gram_grad = (shaped * step_row).astype(BFLOAT)
            c_grad = c_grad + dot(gram_grad, b_state)
            b_grad = b_grad + dot(gram_grad, c_state, 0, 0)
            terms = shaped * gram
            step_grad_rows.append(jnp.sum(terms, axis=0, keepdims=True))
            sums = jnp.sum(terms * step_row, axis=1, keepdims=True)
            row_sums = jnp.where(lane == h, sums, row_sums)
            weights_low = (gram * grown * step_row).astype(BFLOAT)
            found.append(dot(weights_low, y_head, 0, 0))
        x_grad = pre_grad * taps[5:6, cols] + jnp.where(lane < HDM, found[0], found[1])
        act_grad_ref[:, cols] = x_grad
    act_grad_ref[:, width : width + 128] = b_grad
    act_grad_ref[:, width + 128 :] = c_grad
    step_grad = jnp.concatenate(
        step_grad_rows + [jnp.zeros((128 - heads, length), FLOAT)], axis=0
    ).T
    rate = -jnp.exp(head_ref[1:2, :])
    back_sum = exact_dot(triangle(length, True), row_sums - step_grad * step_size)
    raw_grad = (step_grad + rate * back_sum) * sigmoid(step_pre)
    raw_grad = jnp.where(lane < heads, raw_grad, 0.0)
    in_low_ref[:, width:] = raw_grad.astype(BFLOAT)
    head_grad_ref[0:1, :] = jnp.sum(raw_grad, axis=0, keepdims=True)
    head_grad_ref[1:2, :] = jnp.sum(rate * step_size * back_sum, axis=0, keepdims=True)
    head_grad_ref[2:8, :] = jnp.zeros((6, 128), FLOAT)
    sames = [same_document(seg, o) for o in range(4)]
    share_ref[:, :256] = kv_grad_ref[...]
    for start in range(0, conv_width, 128):
        cols = slice(start, start + 128)
        pre = conv_pre_ref[:, cols]
        s = sigmoid(pre)
        a = act_grad_ref[:, cols] * (s * (1.0 + pre * (1.0 - s)))
        u = conv_in_ref[:, cols]
        raw = taps[3:4, cols] * a
        taps_grad_ref[3:4, cols] = jnp.sum(a * u, axis=0, keepdims=True)
        taps_grad_ref[4:5, cols] = jnp.sum(a, axis=0, keepdims=True)
        for o in range(1, 4):
            masked = a * sames[o]
            raw = raw + taps[3 - o : 4 - o, cols] * pltpu.roll(masked, length - o, 0)
            taps_grad_ref[3 - o : 4 - o, cols] = jnp.sum(
                masked * pltpu.roll(u, o, 0), axis=0, keepdims=True
            )
        if start < width:
            in_low_ref[:, cols] = raw.astype(BFLOAT)
        else:
            share_ref[:, 256 + start - width : 256 + start - width + 128] = raw
    taps_grad_ref[5:8, :] = jnp.zeros((3, conv_width), FLOAT)


def call(kernel, outs, scalar, *arrays, scratch=()):
    return pl.pallas_call(
        kernel,
        out_shape=[jax.ShapeDtypeStruct(shape, dtype) for shape, dtype in outs],
        in_specs=[pl.BlockSpec(memory_space=pltpu.SMEM)]
        + [WHOLE] * len(arrays),
        out_specs=[WHOLE] * len(outs),
        scratch_shapes=list(scratch),
        compiler_params=pltpu.CompilerParams(vmem_limit_bytes=16 * 1024 * 1024),
        cost_estimate=pl.CostEstimate(flops=1000, bytes_accessed=1000, transcendentals=0),
    )(scalar, *arrays)


def finish_tensor(keep, give, index):
    sums = keep + swap(give, "tensor", 4, 1)
    half = index >> 1
    mine = jnp.where(half == 0, sums[0], sums[1])
    other = jnp.where(half == 0, sums[1], sums[0])
    return mine + swap(other.astype(BFLOAT), "tensor", 4, 2).astype(FLOAT)


def sum_tensor(partial, index):
    keep, give = pieces_of(partial, index & 1 == 0, 0)
    return finish_tensor(jnp.stack(keep), jnp.stack(give), index)


def ffn_kernel(
    gu_runs, down_runs, core_ref, rows_ref, cot_ref, *refs
):
    gu_refs, refs = refs[: len(gu_runs)], refs[len(gu_runs) :]
    down_refs, refs = refs[: len(down_runs)], refs[len(down_runs) :]
    gu_low_ref, act_ref, keep_ref, give_ref, out_keep_ref, out_give_ref = refs
    width = act_ref.shape[1]
    block = sum(n for runs in gu_runs for _, _, n in runs)
    block = rows_ref.shape[1] // block

    def inner(left_ref, parts, found):
        total = 0.0
        for part, runs in zip(parts, found):
            for col, row, n in runs:
                total = total + dot(
                    left_ref[:, col * block : (col + n) * block], part[row * block : (row + n) * block, :]
                )
        return total

    def outer(left, parts, found, to_keep, to_give):
        for part, runs in zip(parts, found):
            for col, row, n in runs:
                terms = dot(left, part[row * block : (row + n) * block, :], 1, 1)
                keep, give = pieces_of(terms, at_core, 0)
                for y in range(2):
                    to_keep[y, :, col * block : (col + n) * block] = keep[y]
                    to_give[y, :, col * block : (col + n) * block] = give[y]

    at_core = core_ref[0] == 0
    gate_up = inner(rows_ref, gu_refs, gu_runs)
    gate_proj, up_proj = gate_up[:, :width], gate_up[:, width:]
    s = sigmoid(gate_proj)
    silu = gate_proj * s
    act = (silu * up_proj).astype(BFLOAT)
    act_ref[...] = act
    act_grad = inner(cot_ref, down_refs, down_runs)
    gu_low_ref[:, :width] = (act_grad * up_proj * (s * (1.0 + gate_proj * (1.0 - s)))).astype(BFLOAT)
    gu_low_ref[:, width:] = (act_grad * silu).astype(BFLOAT)
    outer(gu_low_ref[...], gu_refs, gu_runs, keep_ref, give_ref)
    outer(act, down_refs, down_runs, out_keep_ref, out_give_ref)


def gather_tensor(values):
    return lax.all_gather(values, "tensor", axis=0, tiled=True)


def group_sum(values, axis, axis_count, bits):
    parts = [values] + [swap(values, axis, axis_count, m) for m in bits]
    while len(parts) > 1:
        parts = [parts[k] + parts[k + 1] for k in range(0, len(parts), 2)]
    return parts[0]


def per_device(
    count,
    tokens,
    segments,
    zx_weight,
    dt_weight,
    query_weight,
    ssm_out_weight,
    attn_out_weight,
    gate_up_weight,
    down_weight,
    shared_weight,
    norm_gains,
    conv_params,
    head_params,
    cotangent,
):
    shard_index = lax.axis_index("tensor")
    dp_index = lax.axis_index("dp")
    length = segments.shape[0]
    rows = zx_weight.shape[1]
    head_local = dt_weight.shape[1]
    width_local = zx_weight.shape[2]
    query_cols = query_weight.shape[1]
    query_local = query_cols // HD
    ff_local = down_weight.shape[0]
    share_rows = shared_weight.shape[0]
    share_cols = shared_weight.shape[1]

    token_rel, cot_local = relocate([tokens, cotangent], dp_index, count, True)
    token_f = token_rel.astype(FLOAT)
    gains = relocate([norm_gains], dp_index, count, True)[0]
    normed_one, norm_one_back = jax.vjp(rms_norm, token_f, gains[0])
    normed_rows = gather_tensor(normed_one.astype(BFLOAT))
    cot_rows = gather_tensor(cot_local)

    shared_pack = shared_weight.reshape(share_rows, 4, share_cols // 4)
    shared_pack = jnp.concatenate([shared_pack[:, k] for k in range(4)], axis=0)
    dt_pad = jnp.pad(dt_weight, ((0, 0), (0, 128 - head_local)))
    groups = stages_of(count)
    first, last = groups[:-1], groups[-1:]
    order = block_order(count)
    lead_piece = jnp.concatenate([shared_pack, query_weight, dt_pad, zx_weight[1]], axis=1)
    mid_piece = jnp.concatenate([zx_weight[0], ssm_out_weight.T, attn_out_weight.T], axis=1)
    gu_piece = jnp.concatenate([gate_up_weight[0], gate_up_weight[1]], axis=1)
    down_half, down_have = joined(*gather(down_weight.T, [0], last, count))
    early_half, have = joined(*gather(lead_piece, [0], first, count))
    early_half, down_half, mid_piece, normed_rows = lax.optimization_barrier(
        (early_half, down_half, mid_piece, normed_rows)
    )
    (early_near, early_far), _ = two(*gather(early_half, have, last, count))
    mid_half, _ = joined(*gather(mid_piece, [0], first, count))
    mid_half, early_far, gu_piece, cot_rows = lax.optimization_barrier(
        (mid_half, early_far, gu_piece, cot_rows)
    )
    (mid_near, mid_far), _ = two(*gather(mid_half, have, last, count))
    gu_half, _ = joined(*gather(gu_piece, [0], first, count))
    gu_half, mid_far, down_half = lax.optimization_barrier((gu_half, mid_far, down_half))
    gu_parts, gu_places = gather(gu_half, have, last, count)
    down_parts, down_places = gather(down_half, down_have, first, count)
    shared_got = jnp.concatenate([early_near[:, :128], early_far[:, :128]], axis=0)
    shared_got = shared_got.reshape(count, 4, share_rows, share_cols // 4)
    shared_got = jnp.concatenate([shared_got[:, k] for k in range(4)], axis=-1)
    near = jnp.stack([shared_got, swap(shared_got, "tensor", 4, 2)])
    both = jnp.stack([near, swap(near, "tensor", 4, 1)])
    both = jnp.where(shard_index & 1 == 1, both[::-1], both)
    both = jnp.where(shard_index >> 1 == 1, both[:, ::-1], both)
    shared_full = both.transpose(2, 1, 0, 3, 4).reshape(count * rows, share_cols)

    head_mine = lax.dynamic_slice_in_dim(head_params, shard_index * head_local, head_local, 1)
    bc_start = conv_params.shape[1] - 2 * NSTATE
    conv_mine = jnp.concatenate(
        [
            lax.dynamic_slice_in_dim(conv_params, shard_index * width_local, width_local, 1),
            conv_params[:, bc_start:],
        ],
        axis=1,
    )
    conv_width = width_local + 2 * NSTATE
    taps = jnp.concatenate([conv_mine, jnp.pad(jnp.repeat(head_mine[2], HDM), (0, 2 * NSTATE))[None]], axis=0)
    taps = jnp.pad(taps, ((0, 8 - taps.shape[0]), (0, 0)))
    head_pack = jnp.pad(head_mine, ((0, 5), (0, 128 - head_local)))
    seg_wide = jnp.broadcast_to(segments.astype(FLOAT)[:, None], (length, 128))
    seg_row = jnp.broadcast_to(segments.astype(FLOAT)[None], (8, length))
    core = (shard_index & 1)[None]
    owner = ((shard_index * query_local) // (QH // KVH))[None]
    width_full = count * rows
    kept_width = 2 * conv_width + 256 + length
    low_width = conv_width + 128 + 256
    mixer_kept, mixer_low, pre_gate, attn_low = call(
        functools.partial(mixer_kernel, head_local),
        [
            ((length, kept_width), FLOAT),
            ((length, low_width), BFLOAT),
            ((length, width_local), FLOAT),
            ((length, 128), BFLOAT),
        ],
        owner,
        normed_rows,
        early_near,
        early_far,
        shared_full,
        taps,
        head_pack,
        seg_wide,
        seg_row,
    )
    halves = ((2, length // 4, width_full), FLOAT)
    gates, mixed_low, keep, give = call(
        gate_kernel,
        [((length, 2 * width_local), FLOAT), ((length, width_local + 128), BFLOAT), halves, halves],
        core,
        normed_rows,
        mid_near,
        mid_far,
        pre_gate,
        attn_low,
    )
    hidden = token_f + finish_tensor(keep, give, shard_index)
    normed_two, norm_two_back = jax.vjp(rms_norm, hidden, gains[1])
    ffn_rows = gather_tensor(normed_two.astype(BFLOAT))
    gu_low, act_low, keep, give, out_keep, out_give = call(
        functools.partial(ffn_kernel, column_runs(gu_places, order), column_runs(down_places, order)),
        [((length, 2 * ff_local), BFLOAT), ((length, ff_local), BFLOAT), halves, halves, halves, halves],
        core,
        ffn_rows,
        cot_rows,
        *gu_parts,
        *down_parts,
    )
    normed_two_grad = finish_tensor(keep, give, shard_index)
    hidden_norm_grad, gain_two_grad = norm_two_back(normed_two_grad)
    hidden_grad = cot_local.astype(FLOAT) + hidden_norm_grad
    mix_grad_rows = gather_tensor(hidden_grad.astype(BFLOAT))
    last_group = last[0]
    back = groups[:-1][::-1]
    down_kept, down_sent, down_stay = parted([(cot_rows, act_low)], order, back[0])
    gu_kept, gu_sent, stay = parted([(ffn_rows, gu_low)], order, last_group)
    gu_sent, down_sent = together(gu_sent, down_sent)
    gu_half_sum = add(gu_kept, send(gu_sent, last_group, count))
    down_half_sum = add(down_kept, send(down_sent, back[0], count))
    gu_half_sum, down_half_sum, mix_grad_rows = lax.optimization_barrier(
        (gu_half_sum, down_half_sum, mix_grad_rows)
    )
    gu_kept, gu_got = finish(gu_half_sum, stay, back, count)
    zq_low, pre_grad, skip_lanes, kv_grad = call(
        gate_back_kernel,
        [
            ((length, width_local + 128), BFLOAT),
            ((length, width_local), FLOAT),
            ((8, 128), FLOAT),
            ((length, 256), FLOAT),
        ],
        owner,
        mix_grad_rows,
        mid_near,
        mid_far,
        gates,
        mixer_low,
        seg_wide,
        seg_row,
    )
    dt_start = width_local + query_cols
    pre_grad, *gu_got = together(pre_grad, *gu_got)
    gu_sum = add(gu_kept, gu_got)
    in_low, taps_grad, head_grad, share_terms = call(
        functools.partial(mixer_back_kernel, head_local),
        [
            ((length, width_local + 128), BFLOAT),
            ((8, conv_width), FLOAT),
            ((8, 128), FLOAT),
            ((length, share_cols), FLOAT),
        ],
        owner,
        pre_grad,
        mixer_kept,
        mixer_low,
        kv_grad,
        taps,
        head_pack,
        seg_wide,
        seg_row,
        scratch=[pltpu.VMEM((length, conv_width), FLOAT)],
    )
    share_terms = share_terms + swap(share_terms, "tensor", 4, 1)
    share_terms = share_terms + swap(share_terms.astype(BFLOAT), "tensor", 4, 2).astype(FLOAT)
    share_low = share_terms.astype(BFLOAT)
    block_width = share_cols // 4
    shared_mine = lax.dynamic_slice_in_dim(shared_full, shard_index * block_width, block_width, 1)
    block_low = lax.dynamic_slice_in_dim(share_low, shard_index * block_width, block_width, 1)
    share_grad = einsum_f32("ld,lk->dk", normed_rows, share_low).reshape(count, 4, share_rows, share_cols)
    share_grad = lax.dynamic_index_in_dim(share_grad, shard_index, 1, keepdims=False)
    share_grad = share_grad.reshape(count * share_rows, share_cols)
    mid_kept, mid_sent, _ = parted(
        [(normed_rows, zq_low), (mix_grad_rows, mixed_low)], order, last_group
    )
    mid_half_sum = add(mid_kept, send(mid_sent, last_group, count))
    in_kept, in_sent, _ = parted([(normed_rows, in_low)], order, last_group)
    share_kept, share_sent, _ = split(share_grad, order, last_group, [share_rows])
    in_kept = jnp.concatenate([in_kept, share_kept], axis=0)
    in_sent = [jnp.concatenate(pair, axis=0) for pair in zip(in_sent, share_sent)]
    mid_half_sum, gu_sum, block_low, *in_sent = lax.optimization_barrier(
        (mid_half_sum, gu_sum, block_low, *in_sent)
    )
    mid_sum = add(*finish(mid_half_sum, stay, back, count))
    in_half_sum = add(in_kept, send(in_sent, last_group, count))
    keep, give = call(
        input_back_kernel,
        [halves, halves],
        core,
        in_low,
        zq_low,
        block_low,
        early_near,
        early_far,
        mid_near,
        mid_far,
        shared_mine,
    )
    normed_one_grad = finish_tensor(keep, give, shard_index)
    token_norm_grad, gain_one_grad = norm_one_back(normed_one_grad)
    conv_full = lax.dynamic_update_slice_in_dim(
        jnp.zeros_like(conv_params), taps_grad[:5, :width_local], shard_index * width_local, 1
    )
    conv_full = conv_full.at[:, bc_start:].set(taps_grad[:5, width_local:])
    head_full = lax.dynamic_update_slice_in_dim(
        jnp.zeros_like(head_params),
        jnp.concatenate([head_grad[:2, :head_local], skip_lanes[:1, :head_local]], axis=0),
        shard_index * head_local,
        1,
    )
    wide = conv_params.shape[1]
    features, head_count = gains.shape[1], head_params.shape[1]
    gains_grad = relocate([jnp.stack([gain_one_grad, gain_two_grad])], dp_index, count, False)[0]
    small = jnp.concatenate(
        [
            jnp.pad(
                jnp.concatenate([gains_grad, head_full[:2]], axis=1),
                ((0, 0), (0, wide - features - head_count)),
            ),
            conv_full,
            jnp.pad(head_full[2:], ((0, 0), (0, wide - head_count))),
        ],
        axis=0,
    )
    for bits in (1, 2):
        small = group_sum(small, "tensor", 4, [bits])
    in_half_sum, mid_sum, down_half_sum, out_give, small = together(
        in_half_sum, mid_sum, down_half_sum, out_give, small
    )
    in_sum = add(*finish(in_half_sum, stay, back, count, [rows, share_rows]))
    down_sum = add(*finish(down_half_sum, down_stay, back[1:] + last, count))
    ffn_sum = finish_tensor(out_keep, out_give, shard_index)
    output = (hidden + ffn_sum).astype(BFLOAT)
    z_sum = mid_sum[:, :dt_start]
    out_sum = mid_sum[:, dt_start:]
    small = group_sum(small, "dp", count, last_group)
    small, in_sum = together(small, in_sum)
    for group in first:
        small = group_sum(small, "dp", count, group)
    shared_sum = in_sum[rows:]
    in_sum = in_sum[:rows]
    return (
        *relocate([output, hidden_grad + token_norm_grad], dp_index, count, False),
        jnp.stack([z_sum[:, :width_local], in_sum[:, :width_local]]),
        in_sum[:, width_local : width_local + head_local],
        z_sum[:, width_local:],
        out_sum[:, :width_local].T,
        out_sum[:, width_local:].T,
        jnp.stack([gu_sum[:, :ff_local], gu_sum[:, ff_local:]]),
        down_sum.T,
        shared_sum,
        small[:2, :features],
        small[2:7],
        jnp.concatenate(
            [small[:2, features : features + head_count], small[7:, :head_count]], axis=0
        ),
    )


def solution(mesh):
    count = mesh.shape["dp"]
    placed = (
        P(("dp", "tensor"), None),
        P("dp"),
        P(None, "dp", "tensor"),
        P("dp", "tensor"),
        P("dp", "tensor"),
        P("tensor", "dp"),
        P("tensor", "dp"),
        P(None, "dp", "tensor"),
        P("tensor", "dp"),
        P(("dp", "tensor"), None),
        P(),
        P(),
        P(),
        P(("dp", "tensor"), None),
    )

    def body(*arrays):
        return per_device(count, *arrays)

    return jax.shard_map(
        body,
        mesh=mesh,
        in_specs=placed,
        out_specs=(
            P(("dp", "tensor"), None),
            P(("dp", "tensor"), None),
            P(None, "dp", "tensor"),
            P("dp", "tensor"),
            P("dp", "tensor"),
            P("tensor", "dp"),
            P("tensor", "dp"),
            P(None, "dp", "tensor"),
            P("tensor", "dp"),
            P(("dp", "tensor"), None),
            P(),
            P(),
            P(),
        ),
        check_vma=False,
    )
```

```python
import functools
import math

import jax
import jax.numpy as jnp
from jax import lax
from jax.experimental import pallas as pl
from jax.experimental.pallas import tpu as pltpu
from jax.sharding import PartitionSpec as P

HDM = 64
NSTATE = 128
QH = 8
KVH = 2
HD = 64


EPSILON = 1e-05
FLOAT = jnp.float32
BFLOAT = jnp.bfloat16
WHOLE = pl.BlockSpec()


def rms_norm(values, scale_vec):
    return (
        values * lax.rsqrt(jnp.mean(values * values, axis=-1, keepdims=True) + EPSILON) * scale_vec
    )


def einsum_f32(pattern, op_left, op_right):
    return jnp.einsum(pattern, op_left, op_right, preferred_element_type=jnp.float32)


def silu_gate(gate_proj, up_proj):
    return jax.nn.silu(gate_proj) * up_proj


def swap(values, axis, count, bits):
    return lax.ppermute(values, axis, [(i, i ^ bits) for i in range(count)])


def stages_of(count):
    top = count.bit_length() - 1
    groups = []
    while top > 0:
        low = max(0, top - 2)
        groups.append([m << low for m in range(1, 1 << (top - low))])
        top = low
    return groups


def block_order(count):
    order = [0]
    for group in stages_of(count):
        order = order + [r ^ m for m in group for r in order]
    return order


def relocate_kernel(order, to_relative, index_ref, *refs):
    for source, target in zip(refs[: len(refs) // 2], refs[len(refs) // 2 :]):
        block = source.shape[1] // len(order)
        for k, r in enumerate(order):
            here = slice(k * block, (k + 1) * block)
            there = pl.ds(pl.multiple_of((index_ref[0] ^ r) * block, block), block)
            if to_relative:
                target[:, here] = source[:, there]
            else:
                target[:, there] = source[:, here]


def relocate(arrays, index, count, to_relative):
    order = block_order(count)
    if arrays[0].shape[1] // count % 128 == 0:
        return call(
            functools.partial(relocate_kernel, order, to_relative),
            [(a.shape, a.dtype) for a in arrays],
            index[None],
            *arrays,
        )
    places = jnp.array(order, jnp.int32) ^ index
    if not to_relative:
        places = jnp.argsort(places)
    moved = [a.reshape(a.shape[0], count, -1)[:, places].reshape(a.shape) for a in arrays]
    return moved


def together(*values):
    return lax.optimization_barrier(values)


def stack_kernel(*refs):
    *parts, out_ref = refs
    start = 0
    for part in parts:
        out_ref[start : start + part.shape[0], :] = part[...]
        start += part.shape[0]


def stacked(parts):
    rows = sum(p.shape[0] for p in parts)
    return pl.pallas_call(
        stack_kernel,
        out_shape=jax.ShapeDtypeStruct((rows, parts[0].shape[1]), parts[0].dtype),
        in_specs=[WHOLE] * len(parts),
        out_specs=WHOLE,
        compiler_params=pltpu.CompilerParams(vmem_limit_bytes=16 * 1024 * 1024),
        cost_estimate=pl.CostEstimate(flops=1000, bytes_accessed=1000, transcendentals=0),
    )(*parts)


def gather(stack, have, groups, count):
    parts, places = [stack], [have]
    for k, group in enumerate(groups):
        if k > 0:
            stack = stacked(parts)
            have = [r for p in places for r in p]
        parts = [stack] + [swap(stack, "dp", count, m) for m in group]
        places = [have] + [[r ^ m for r in have] for m in group]
    return parts, places


def joined(parts, places):
    return stacked(parts), [r for p in places for r in p]


def two(parts, places):
    far = parts[1] if len(parts) == 2 else stacked(parts[1:])
    return (parts[0], far), places


def column_runs(places, order):
    found = []
    for have in places:
        runs = []
        for row, r in enumerate(have):
            col = order.index(r)
            if runs and runs[-1][0] + runs[-1][2] == col:
                runs[-1] = (runs[-1][0], runs[-1][1], runs[-1][2] + 1)
            else:
                runs.append((col, row, 1))
        found.append(runs)
    return found


def products_kernel(runs_of, block, widths, *refs):
    lefts, rights, outs = refs[: len(widths)], refs[len(widths) : 2 * len(widths)], refs[2 * len(widths) :]
    start = 0
    for left, right, width in zip(lefts, rights, widths):
        right_now = right[...]
        for out, runs in zip(outs, runs_of):
            row = 0
            for col, n in runs:
                found = dot(left[:, col * block : (col + n) * block], right_now, 0, 0)
                out[row * block : (row + n) * block, start : start + width] = found.astype(out.dtype)
                row += n
        start += width


def parted(pairs, order, group):
    block = pairs[0][0].shape[1] // len(order)
    span = 0
    for m in group:
        span |= m
    stay = [r for r in order if r & span == 0]
    runs_of = []
    for blocks in [stay] + [[r ^ m for r in stay] for m in group]:
        runs = []
        for r in blocks:
            col = order.index(r)
            if runs and sum(runs[-1]) == col:
                runs[-1] = (runs[-1][0], runs[-1][1] + 1)
            else:
                runs.append((col, 1))
        runs_of.append(runs)
    widths = [right.shape[1] for _, right in pairs]
    shape = (len(stay) * block, sum(widths))
    kept, *sent = pl.pallas_call(
        functools.partial(products_kernel, runs_of, block, widths),
        out_shape=[jax.ShapeDtypeStruct(shape, FLOAT)]
        + [jax.ShapeDtypeStruct(shape, BFLOAT)] * len(group),
        in_specs=[WHOLE] * (2 * len(pairs)),
        out_specs=[WHOLE] * (1 + len(group)),
        compiler_params=pltpu.CompilerParams(vmem_limit_bytes=16 * 1024 * 1024),
        cost_estimate=pl.CostEstimate(flops=1000, bytes_accessed=1000, transcendentals=0),
    )(*[left for left, _ in pairs], *[right for _, right in pairs])
    return kept, sent, stay


def send(sent, group, count):
    return [swap(part, "dp", count, m) for m, part in zip(group, sent)]


def add(kept, got):
    for part in got:
        kept = kept + part.astype(FLOAT)
    return kept


def split(total, order, group, sizes):
    span = 0
    for m in group:
        span |= m
    stay = [r for r in order if r & span == 0]

    def rows(blocks):
        parts = []
        start = 0
        for size in sizes:
            parts += [total[start + order.index(r) * size :][:size] for r in blocks]
            start += size * len(order)
        return jnp.concatenate(parts, axis=0)

    return rows(stay), [rows([r ^ m for r in stay]).astype(BFLOAT) for m in group], stay


def add_split_kernel(spans, kept_ref, *refs):
    got, outs = refs[: len(refs) - len(spans)], refs[len(refs) - len(spans) :]
    for out, found in zip(outs, spans):
        row = 0
        for start, size in found:
            total = kept_ref[start : start + size, :]
            for part in got:
                total = total + part[start : start + size, :].astype(FLOAT)
            out[row : row + size, :] = total.astype(out.dtype)
            row += size


def add_split(kept, got, order, group, sizes):
    span = 0
    for m in group:
        span |= m
    stay = [r for r in order if r & span == 0]
    spans = []
    for blocks in [stay] + [[r ^ m for r in stay] for m in group]:
        start, found = 0, []
        for size in sizes:
            found += [(start + order.index(r) * size, size) for r in blocks]
            start += size * len(order)
        spans.append(found)
    shape = (sum(sizes) * len(stay), kept.shape[1])
    kept, *sent = pl.pallas_call(
        functools.partial(add_split_kernel, spans),
        out_shape=[jax.ShapeDtypeStruct(shape, FLOAT)]
        + [jax.ShapeDtypeStruct(shape, BFLOAT)] * len(group),
        in_specs=[WHOLE] * (1 + len(got)),
        out_specs=[WHOLE] * (1 + len(group)),
        compiler_params=pltpu.CompilerParams(vmem_limit_bytes=16 * 1024 * 1024),
        cost_estimate=pl.CostEstimate(flops=1000, bytes_accessed=1000, transcendentals=0),
    )(kept, *got)
    return kept, sent, stay


def finish(kept, got, order, groups, count, sizes=None):
    if sizes is None:
        sizes = [kept.shape[0] // len(order)]
    for group in groups:
        if min(sizes) % 16 == 0:
            kept, sent, order = add_split(kept, got, order, group, sizes)
        else:
            kept, sent, order = split(add(kept, got), order, group, sizes)
        got = send(sent, group, count)
    return kept, got


def dot(left, right, left_dim=1, right_dim=0):
    return lax.dot_general(
        left, right, (((left_dim,), (right_dim,)), ((), ())), preferred_element_type=FLOAT
    )


def exact_dot(left, right):
    return jnp.dot(left, right, precision=lax.Precision.HIGHEST, preferred_element_type=FLOAT)


def sigmoid(values):
    return 1.0 / (1.0 + jnp.exp(-values))


def softplus(values):
    return jnp.maximum(values, 0.0) + jnp.log1p(jnp.exp(-jnp.abs(values)))


def lanes_of(shape):
    return lax.broadcasted_iota(jnp.int32, shape, 1)


def same_document(seg_wide, offset):
    if offset == 0:
        return None
    row = lax.broadcasted_iota(jnp.int32, seg_wide.shape, 0)
    same = jnp.logical_and(pltpu.roll(seg_wide, offset, 0) == seg_wide, row >= offset)
    return jnp.where(same, 1.0, 0.0)


def square_mask(seg_wide, seg_row):
    length = seg_wide.shape[0]
    row = lax.broadcasted_iota(jnp.int32, (length, length), 0)
    col = lax.broadcasted_iota(jnp.int32, (length, length), 1)
    wide = jnp.concatenate([seg_wide] * (length // 128), axis=1)
    return jnp.logical_and(row >= col, wide == seg_row[0:1, :])


def triangle(length, flip):
    row = lax.broadcasted_iota(jnp.int32, (length, length), 0)
    col = lax.broadcasted_iota(jnp.int32, (length, length), 1)
    return jnp.where(row <= col if flip else row >= col, 1.0, 0.0)


def head_lanes(values, head, lane):
    return jnp.where((lane >= HDM) == (head == 1), values, jnp.zeros_like(values))


def softmax_of(queries, keys, mask, head, lane):
    scores = dot(head_lanes(queries, head, lane), keys, 1, 1) * (1.0 / math.sqrt(HD))
    masked = jnp.where(mask, scores, -1000000000.0)
    grown = jnp.exp(masked - jnp.max(masked, axis=-1, keepdims=True))
    return grown / jnp.sum(grown, axis=-1, keepdims=True)


def views(ref, widths):
    found = []
    start = 0
    for width in widths:
        found.append(ref.at[:, start : start + width])
        start += width
    return found


def kept_views(ref, width):
    return views(ref, (width + 256, width + 256, 128, 128, ref.shape[0]))


def low_views(ref, width):
    return views(ref, (width + 256, 128, 256))


def mixer_kernel(
    heads, owner_ref, normed_ref, near_ref, far_ref, shared_ref, taps_ref, head_ref, seg_ref, seg_row_ref,
    kept_ref, low_ref, pre_gate_ref, attn_ref,
):
    conv_in_ref, conv_pre_ref, step_ref, decay_ref, gram_ref = kept_views(kept_ref, pre_gate_ref.shape[1])
    conv_low_ref, query_ref, kv_ref = low_views(low_ref, pre_gate_ref.shape[1])
    length = normed_ref.shape[0]
    half = near_ref.shape[0]
    width = pre_gate_ref.shape[1]
    conv_width = conv_in_ref.shape[1]
    normed = normed_ref[...]
    taps = taps_ref[...]
    seg = seg_ref[...]
    mask = square_mask(seg, seg_row_ref[...])
    lead = dot(normed[:, :half], near_ref[:, 128:]) + dot(normed[:, half:], far_ref[:, 128:])
    x_raw = lead[:, 256:]
    shared = dot(normed, shared_ref[...]).astype(BFLOAT)
    queries = lead[:, :128].astype(BFLOAT)
    query_ref[...] = queries
    lane = lanes_of((length, 128))
    keep_half = (lane >= HD) == (owner_ref[0] == 1)
    shared_f = shared.astype(FLOAT)
    keys = jnp.where(keep_half, shared_f[:, :128], pltpu.roll(shared_f[:, :128], HD, 1)).astype(BFLOAT)
    values = jnp.where(keep_half, shared_f[:, 128:256], pltpu.roll(shared_f[:, 128:256], HD, 1)).astype(BFLOAT)
    kv_ref[:, :128] = keys
    kv_ref[:, 128:] = values
    outs = [dot(softmax_of(queries, keys, mask, h, lane).astype(BFLOAT), values) for h in range(2)]
    attn_ref[...] = jnp.where(lane < HD, outs[0], outs[1]).astype(BFLOAT)
    step_pre = lead[:, 128:256] + head_ref[0:1, :]
    step_ref[...] = step_pre
    step_size = softplus(step_pre)
    decay = exact_dot(triangle(length, False), step_size * -jnp.exp(head_ref[1:2, :]))
    decay_ref[...] = decay
    sames = [same_document(seg, o) for o in range(4)]
    for start in range(0, conv_width, 128):
        cols = slice(start, start + 128)
        if start < width:
            u = x_raw[:, cols]
        else:
            u = shared_f[:, 256 + start - width : 256 + start - width + 128]
        conv_in_ref[:, cols] = u
        pre = taps[4:5, cols] + taps[3:4, cols] * u
        for o in range(1, 4):
            pre = pre + taps[3 - o : 4 - o, cols] * (pltpu.roll(u, o, 0) * sames[o])
        conv_pre_ref[:, cols] = pre
        conv_low_ref[:, cols] = (pre * sigmoid(pre)).astype(BFLOAT)
    b_state = conv_low_ref[:, width : width + 128]
    c_state = conv_low_ref[:, width + 128 :]
    gram = dot(c_state, b_state, 1, 1)
    gram_ref[...] = gram
    step_rows, decay_rows = step_size.T, decay.T
    for pair in range(heads // 2):
        cols = slice(128 * pair, 128 * pair + 128)
        x_pair = conv_low_ref[:, cols]
        found = []
        for h in (2 * pair, 2 * pair + 1):
            gap = decay[:, h : h + 1] - decay_rows[h : h + 1, :]
            grown = jnp.where(mask, jnp.exp(jnp.where(mask, gap, 0.0)), 0.0)
            found.append(dot((gram * grown * step_rows[h : h + 1, :]).astype(BFLOAT), x_pair))
        y_pair = jnp.where(lane < HDM, found[0], found[1])
        pre_gate_ref[:, cols] = y_pair + taps[5:6, cols] * x_pair.astype(FLOAT)


def pieces_of(terms, at_core, axis):
    size = terms.shape[axis] // 4
    blocks = [lax.slice_in_dim(terms, k * size, (k + 1) * size, axis=axis) for k in range(4)]
    keep = [jnp.where(at_core, blocks[2 * y], blocks[2 * y + 1]) for y in range(2)]
    give = [jnp.where(at_core, blocks[2 * y + 1], blocks[2 * y]) for y in range(2)]
    return keep, give


def gate_kernel(
    core_ref, normed_ref, near_ref, far_ref, pre_gate_ref, attn_ref, gates_ref, mixed_ref, keep_ref, give_ref
):
    half = near_ref.shape[0]
    width = pre_gate_ref.shape[1]
    normed = normed_ref[...]
    gate_z = dot(normed[:, :half], near_ref[:, :width]) + dot(normed[:, half:], far_ref[:, :width])
    gates_ref[:, :width] = gate_z
    gates_ref[:, width:] = pre_gate_ref[...]
    gated = (pre_gate_ref[...] * (gate_z * sigmoid(gate_z))).astype(BFLOAT)
    mixed_ref[:, :width] = gated
    mixed_ref[:, width:] = attn_ref[...]
    mixed = mixed_ref[...]
    at_core = core_ref[0] == 0
    start = 0
    for part in (near_ref, far_ref):
        terms = dot(mixed, part[:, width:], 1, 1)
        cols = slice(start, start + part.shape[0])
        start += part.shape[0]
        keep, give = pieces_of(terms, at_core, 0)
        for y in range(2):
            keep_ref[y, :, cols] = keep[y]
            give_ref[y, :, cols] = give[y]


def input_back_kernel(
    core_ref, in_low_ref, zq_ref, block_ref, early_near_ref, early_far_ref, near_ref, far_ref,
    shared_ref, keep_ref, give_ref,
):
    width = zq_ref.shape[1] - 128
    x_low, step_low = in_low_ref[:, :width], in_low_ref[:, width:]
    z_low, query_low = zq_ref[:, :width], zq_ref[:, width:]
    block = block_ref[...]
    at_core = core_ref[0] == 0
    start = 0
    for early, part in ((early_near_ref, near_ref), (early_far_ref, far_ref)):
        cols = slice(start, start + part.shape[0])
        start += part.shape[0]
        terms = (
            dot(x_low, early[:, 384:], 1, 1)
            + dot(query_low, early[:, 128:256], 1, 1)
            + dot(step_low, early[:, 256:384], 1, 1)
            + dot(z_low, part[:, :width], 1, 1)
            + dot(block, shared_ref[cols, :], 1, 1)
        )
        keep, give = pieces_of(terms, at_core, 0)
        for y in range(2):
            keep_ref[y, :, cols] = keep[y]
            give_ref[y, :, cols] = give[y]


def gate_back_kernel(
    owner_ref, grad_ref, near_ref, far_ref, gates_ref, low_ref, seg_ref, seg_row_ref,
    zq_ref, pre_grad_ref, skip_ref, kv_grad_ref,
):
    half = near_ref.shape[0]
    width = pre_grad_ref.shape[1]
    conv_low_ref, query_ref, kv_ref = low_views(low_ref, width)
    grad = grad_ref[...]
    mixed_grad = dot(grad[:, :half], near_ref[:, width:]) + dot(grad[:, half:], far_ref[:, width:])
    gated_grad = mixed_grad[:, :width]
    gate_z = gates_ref[:, :width]
    s = sigmoid(gate_z)
    pre_grad = gated_grad * (gate_z * s)
    pre_grad_ref[...] = pre_grad
    zq_ref[:, :width] = (gated_grad * gates_ref[:, width:] * (s * (1.0 + gate_z * (1.0 - s)))).astype(BFLOAT)
    skip = jnp.sum(pre_grad * conv_low_ref[:, :width].astype(FLOAT), axis=0, keepdims=True)
    row = lax.broadcasted_iota(jnp.int32, (width, 128), 0)
    col = lax.broadcasted_iota(jnp.int32, (width, 128), 1)
    of_head = jnp.where(jnp.logical_and(row >= col * HDM, row < (col + 1) * HDM), 1.0, 0.0)
    skip_ref[...] = exact_dot(jnp.broadcast_to(skip, (8, width)), of_head)
    lane = lanes_of((grad.shape[0], 128))
    out_low = mixed_grad[:, width:].astype(BFLOAT)
    mask = square_mask(seg_ref[...], seg_row_ref[...])
    queries, keys, values = query_ref[...], kv_ref[:, :128], kv_ref[:, 128:]
    query_grads, key_sum, value_sum = [], 0.0, 0.0
    for h in range(2):
        probs = softmax_of(queries, keys, mask, h, lane)
        out_head = head_lanes(out_low, h, lane)
        prob_grad = dot(out_head, values, 1, 1)
        score = probs * (prob_grad - jnp.sum(probs * prob_grad, axis=-1, keepdims=True))
        score_low = score.astype(BFLOAT)
        query_grads.append(dot(score_low, keys))
        key_sum = key_sum + dot(score_low, head_lanes(queries, h, lane), 0, 0)
        value_sum = value_sum + dot(probs.astype(BFLOAT), out_head, 0, 0)
    scale = 1.0 / math.sqrt(HD)
    zq_ref[:, width:] = (jnp.where(lane < HD, query_grads[0], query_grads[1]) * scale).astype(BFLOAT)
    mine = (lane >= HD) == (owner_ref[0] == 1)
    for k, total in enumerate((key_sum * scale, value_sum)):
        both = total + pltpu.roll(total, HD, 1)
        kv_grad_ref[:, 128 * k : 128 * k + 128] = jnp.where(mine, both, 0.0)


def mixer_back_kernel(
    heads, owner_ref, pre_grad_ref, kept_ref, low_ref, kv_grad_ref, taps_ref, head_ref, seg_ref, seg_row_ref,
    in_low_ref, taps_grad_ref, head_grad_ref, share_ref, act_grad_ref,
):
    conv_in_ref, conv_pre_ref, step_ref, decay_ref, gram_ref = kept_views(kept_ref, pre_grad_ref.shape[1])
    conv_low_ref = low_views(low_ref, pre_grad_ref.shape[1])[0]
    length = pre_grad_ref.shape[0]
    width = pre_grad_ref.shape[1]
    conv_width = conv_in_ref.shape[1]
    taps = taps_ref[...]
    seg = seg_ref[...]
    mask = square_mask(seg, seg_row_ref[...])
    lane = lanes_of((length, 128))
    step_pre = step_ref[...]
    step_size = softplus(step_pre)
    decay = decay_ref[...]
    step_rows, decay_rows = step_size.T, decay.T
    gram = gram_ref[...]
    b_state = conv_low_ref[:, width : width + 128]
    c_state = conv_low_ref[:, width + 128 :]
    b_grad, c_grad = 0.0, 0.0
    step_grad_rows, row_sums = [], jnp.zeros((length, 128), FLOAT)
    for pair in range(heads // 2):
        cols = slice(128 * pair, 128 * pair + 128)
        x_pair = conv_low_ref[:, cols]
        pre_grad = pre_grad_ref[:, cols]
        y_pair = pre_grad.astype(BFLOAT)
        found = []
        for k in range(2):
            h = 2 * pair + k
            gap = decay[:, h : h + 1] - decay_rows[h : h + 1, :]
            grown = jnp.where(mask, jnp.exp(jnp.where(mask, gap, 0.0)), 0.0)
            step_row = step_rows[h : h + 1, :]
            y_head = head_lanes(y_pair, k, lane)
            weights_grad = dot(y_head, x_pair, 1, 1)
            shaped = weights_grad * grown
            gram_grad = (shaped * step_row).astype(BFLOAT)
            c_grad = c_grad + dot(gram_grad, b_state)
            b_grad = b_grad + dot(gram_grad, c_state, 0, 0)
            terms = shaped * gram
            step_grad_rows.append(jnp.sum(terms, axis=0, keepdims=True))
            sums = jnp.sum(terms * step_row, axis=1, keepdims=True)
            row_sums = jnp.where(lane == h, sums, row_sums)
            weights_low = (gram * grown * step_row).astype(BFLOAT)
            found.append(dot(weights_low, y_head, 0, 0))
        x_grad = pre_grad * taps[5:6, cols] + jnp.where(lane < HDM, found[0], found[1])
        act_grad_ref[:, cols] = x_grad
    act_grad_ref[:, width : width + 128] = b_grad
    act_grad_ref[:, width + 128 :] = c_grad
    step_grad = jnp.concatenate(
        step_grad_rows + [jnp.zeros((128 - heads, length), FLOAT)], axis=0
    ).T
    rate = -jnp.exp(head_ref[1:2, :])
    back_sum = exact_dot(triangle(length, True), row_sums - step_grad * step_size)
    raw_grad = (step_grad + rate * back_sum) * sigmoid(step_pre)
    raw_grad = jnp.where(lane < heads, raw_grad, 0.0)
    in_low_ref[:, width:] = raw_grad.astype(BFLOAT)
    head_grad_ref[0:1, :] = jnp.sum(raw_grad, axis=0, keepdims=True)
    head_grad_ref[1:2, :] = jnp.sum(rate * step_size * back_sum, axis=0, keepdims=True)
    head_grad_ref[2:8, :] = jnp.zeros((6, 128), FLOAT)
    sames = [same_document(seg, o) for o in range(4)]
    share_ref[:, :256] = kv_grad_ref[...]
    for start in range(0, conv_width, 128):
        cols = slice(start, start + 128)
        pre = conv_pre_ref[:, cols]
        s = sigmoid(pre)
        a = act_grad_ref[:, cols] * (s * (1.0 + pre * (1.0 - s)))
        u = conv_in_ref[:, cols]
        raw = taps[3:4, cols] * a
        taps_grad_ref[3:4, cols] = jnp.sum(a * u, axis=0, keepdims=True)
        taps_grad_ref[4:5, cols] = jnp.sum(a, axis=0, keepdims=True)
        for o in range(1, 4):
            masked = a * sames[o]
            raw = raw + taps[3 - o : 4 - o, cols] * pltpu.roll(masked, length - o, 0)
            taps_grad_ref[3 - o : 4 - o, cols] = jnp.sum(
                masked * pltpu.roll(u, o, 0), axis=0, keepdims=True
            )
        if start < width:
            in_low_ref[:, cols] = raw.astype(BFLOAT)
        else:
            share_ref[:, 256 + start - width : 256 + start - width + 128] = raw
    taps_grad_ref[5:8, :] = jnp.zeros((3, conv_width), FLOAT)


def call(kernel, outs, scalar, *arrays, scratch=()):
    return pl.pallas_call(
        kernel,
        out_shape=[jax.ShapeDtypeStruct(shape, dtype) for shape, dtype in outs],
        in_specs=[pl.BlockSpec(memory_space=pltpu.SMEM)]
        + [WHOLE] * len(arrays),
        out_specs=[WHOLE] * len(outs),
        scratch_shapes=list(scratch),
        compiler_params=pltpu.CompilerParams(vmem_limit_bytes=16 * 1024 * 1024),
        cost_estimate=pl.CostEstimate(flops=1000, bytes_accessed=1000, transcendentals=0),
    )(scalar, *arrays)


def finish_tensor(keep, give, index):
    sums = keep + swap(give, "tensor", 4, 1)
    half = index >> 1
    mine = jnp.where(half == 0, sums[0], sums[1])
    other = jnp.where(half == 0, sums[1], sums[0])
    return mine + swap(other.astype(BFLOAT), "tensor", 4, 2).astype(FLOAT)


def sum_tensor(partial, index):
    keep, give = pieces_of(partial, index & 1 == 0, 0)
    return finish_tensor(jnp.stack(keep), jnp.stack(give), index)


def ffn_kernel(
    gu_runs, down_runs, core_ref, rows_ref, cot_ref, *refs
):
    gu_refs, refs = refs[: len(gu_runs)], refs[len(gu_runs) :]
    down_refs, refs = refs[: len(down_runs)], refs[len(down_runs) :]
    gu_low_ref, act_ref, keep_ref, give_ref, out_keep_ref, out_give_ref = refs
    width = act_ref.shape[1]
    block = sum(n for runs in gu_runs for _, _, n in runs)
    block = rows_ref.shape[1] // block

    def inner(left_ref, parts, found):
        total = 0.0
        for part, runs in zip(parts, found):
            for col, row, n in runs:
                total = total + dot(
                    left_ref[:, col * block : (col + n) * block], part[row * block : (row + n) * block, :]
                )
        return total

    def outer(left, parts, found, to_keep, to_give):
        for part, runs in zip(parts, found):
            for col, row, n in runs:
                terms = dot(left, part[row * block : (row + n) * block, :], 1, 1)
                keep, give = pieces_of(terms, at_core, 0)
                for y in range(2):
                    to_keep[y, :, col * block : (col + n) * block] = keep[y]
                    to_give[y, :, col * block : (col + n) * block] = give[y]

    at_core = core_ref[0] == 0
    gate_up = inner(rows_ref, gu_refs, gu_runs)
    gate_proj, up_proj = gate_up[:, :width], gate_up[:, width:]
    s = sigmoid(gate_proj)
    silu = gate_proj * s
    act = (silu * up_proj).astype(BFLOAT)
    act_ref[...] = act
    act_grad = inner(cot_ref, down_refs, down_runs)
    gu_low_ref[:, :width] = (act_grad * up_proj * (s * (1.0 + gate_proj * (1.0 - s)))).astype(BFLOAT)
    gu_low_ref[:, width:] = (act_grad * silu).astype(BFLOAT)
    outer(gu_low_ref[...], gu_refs, gu_runs, keep_ref, give_ref)
    outer(act, down_refs, down_runs, out_keep_ref, out_give_ref)


def gather_tensor(values):
    return lax.all_gather(values, "tensor", axis=0, tiled=True)


def group_sum(values, axis, axis_count, bits):
    parts = [values] + [swap(values, axis, axis_count, m) for m in bits]
    while len(parts) > 1:
        parts = [parts[k] + parts[k + 1] for k in range(0, len(parts), 2)]
    return parts[0]


def per_device(
    count,
    tokens,
    segments,
    zx_weight,
    dt_weight,
    query_weight,
    ssm_out_weight,
    attn_out_weight,
    gate_up_weight,
    down_weight,
    shared_weight,
    norm_gains,
    conv_params,
    head_params,
    cotangent,
):
    shard_index = lax.axis_index("tensor")
    dp_index = lax.axis_index("dp")
    length = segments.shape[0]
    rows = zx_weight.shape[1]
    head_local = dt_weight.shape[1]
    width_local = zx_weight.shape[2]
    query_cols = query_weight.shape[1]
    query_local = query_cols // HD
    ff_local = down_weight.shape[0]
    share_rows = shared_weight.shape[0]
    share_cols = shared_weight.shape[1]

    token_rel, cot_local = relocate([tokens, cotangent], dp_index, count, True)
    token_f = token_rel.astype(FLOAT)
    gains = relocate([norm_gains], dp_index, count, True)[0]
    normed_one, norm_one_back = jax.vjp(rms_norm, token_f, gains[0])
    normed_rows = gather_tensor(normed_one.astype(BFLOAT))

    seg_wide = jnp.broadcast_to(segments.astype(FLOAT)[:, None], (length, 128))
    seg_row = jnp.broadcast_to(segments.astype(FLOAT)[None], (8, length))

    shared_pack = shared_weight.reshape(share_rows, 4, share_cols // 4)
    shared_pack = jnp.concatenate([shared_pack[:, k] for k in range(4)], axis=0)
    dt_pad = jnp.pad(dt_weight, ((0, 0), (0, 128 - head_local)))
    groups = stages_of(count)
    first, last = groups[:-1], groups[-1:]
    order = block_order(count)
    lead_piece = jnp.concatenate([shared_pack, query_weight, dt_pad, zx_weight[1]], axis=1)
    mid_piece = jnp.concatenate([zx_weight[0], ssm_out_weight.T, attn_out_weight.T], axis=1)
    gu_piece = jnp.concatenate([gate_up_weight[0], gate_up_weight[1]], axis=1)
    down_half, down_have = joined(*gather(down_weight.T, [0], last, count))
    early_half, have = joined(*gather(lead_piece, [0], first, count))
    early_half, down_half, mid_piece, normed_rows, seg_row = together(
        early_half, down_half, mid_piece, normed_rows, seg_row
    )
    cot_rows = gather_tensor(cot_local)
    (early_near, early_far), _ = two(*gather(early_half, have, last, count))
    mid_half, _ = joined(*gather(mid_piece, [0], first, count))
    mid_half, early_far, gu_piece, cot_rows, seg_row = together(
        mid_half, early_far, gu_piece, cot_rows, seg_row
    )
    (mid_near, mid_far), _ = two(*gather(mid_half, have, last, count))
    gu_first, gu_first_places = gather(gu_piece, [0], first, count)
    shared_got = jnp.concatenate([early_near[:, :128], early_far[:, :128]], axis=0)
    shared_got = shared_got.reshape(count, 4, share_rows, share_cols // 4)
    shared_got = jnp.concatenate([shared_got[:, k] for k in range(4)], axis=-1)
    near = jnp.stack([shared_got, swap(shared_got, "tensor", 4, 1)])
    both = jnp.stack([near, swap(near, "tensor", 4, 2)])
    both = jnp.where(shard_index >> 1 == 1, both[::-1], both)
    both = jnp.where(shard_index & 1 == 1, both[:, ::-1], both)
    shared_full = both.transpose(2, 0, 1, 3, 4).reshape(count * rows, share_cols)

    head_mine = lax.dynamic_slice_in_dim(head_params, shard_index * head_local, head_local, 1)
    bc_start = conv_params.shape[1] - 2 * NSTATE
    conv_mine = jnp.concatenate(
        [
            lax.dynamic_slice_in_dim(conv_params, shard_index * width_local, width_local, 1),
            conv_params[:, bc_start:],
        ],
        axis=1,
    )
    conv_width = width_local + 2 * NSTATE
    taps = jnp.concatenate([conv_mine, jnp.pad(jnp.repeat(head_mine[2], HDM), (0, 2 * NSTATE))[None]], axis=0)
    taps = jnp.pad(taps, ((0, 8 - taps.shape[0]), (0, 0)))
    head_pack = jnp.pad(head_mine, ((0, 5), (0, 128 - head_local)))
    core = (shard_index & 1)[None]
    owner = ((shard_index * query_local) // (QH // KVH))[None]
    width_full = count * rows
    kept_width = 2 * conv_width + 256 + length
    low_width = conv_width + 128 + 256
    mixer_kept, mixer_low, pre_gate, attn_low = call(
        functools.partial(mixer_kernel, head_local),
        [
            ((length, kept_width), FLOAT),
            ((length, low_width), BFLOAT),
            ((length, width_local), FLOAT),
            ((length, 128), BFLOAT),
        ],
        owner,
        normed_rows,
        early_near,
        early_far,
        shared_full,
        taps,
        head_pack,
        seg_wide,
        seg_row,
    )
    pre_gate, gu_first = together(pre_gate, gu_first)
    gu_half, _ = joined(gu_first, gu_first_places)
    gu_half, mid_far, down_half, seg_row = together(gu_half, mid_far, down_half, seg_row)
    gu_parts, gu_places = gather(gu_half, have, last, count)
    down_parts, down_places = gather(down_half, down_have, first, count)
    halves = ((2, length // 4, width_full), FLOAT)
    gates, mixed_low, keep, give = call(
        gate_kernel,
        [((length, 2 * width_local), FLOAT), ((length, width_local + 128), BFLOAT), halves, halves],
        core,
        normed_rows,
        mid_near,
        mid_far,
        pre_gate,
        attn_low,
    )
    hidden = token_f + finish_tensor(keep, give, shard_index)
    normed_two, norm_two_back = jax.vjp(rms_norm, hidden, gains[1])
    ffn_rows = gather_tensor(normed_two.astype(BFLOAT))
    gu_low, act_low, keep, give, out_keep, out_give = call(
        functools.partial(ffn_kernel, column_runs(gu_places, order), column_runs(down_places, order)),
        [((length, 2 * ff_local), BFLOAT), ((length, ff_local), BFLOAT), halves, halves, halves, halves],
        core,
        ffn_rows,
        cot_rows,
        *gu_parts,
        *down_parts,
    )
    last_group = last[0]
    back = groups[:-1][::-1]
    down_kept, down_sent, down_stay = parted([(cot_rows, act_low)], order, back[0])
    gu_kept, gu_sent, stay = parted([(ffn_rows, gu_low)], order, last_group)
    gu_sent, down_sent, seg_row = together(gu_sent, down_sent, seg_row)
    gu_got = send(gu_sent, last_group, count)
    down_got = send(down_sent, back[0], count)
    normed_two_grad = finish_tensor(keep, give, shard_index)
    hidden_norm_grad, gain_two_grad = norm_two_back(normed_two_grad)
    hidden_grad = cot_local.astype(FLOAT) + hidden_norm_grad
    mix_grad_rows = gather_tensor(hidden_grad.astype(BFLOAT))
    gu_got, down_got, mix_grad_rows, seg_row = together(gu_got, down_got, mix_grad_rows, seg_row)
    if len(back) == 1 and rows % 16 == 0:
        gu_kept, gu_sent, _ = add_split(gu_kept, gu_got, stay, back[0], [rows])
        gu_sent, mix_grad_rows = together(gu_sent, mix_grad_rows)
        gu_got = send(gu_sent, back[0], count)
    else:
        gu_kept, gu_got = finish(gu_kept, gu_got, stay, back, count)
    zq_low, pre_grad, skip_lanes, kv_grad = call(
        gate_back_kernel,
        [
            ((length, width_local + 128), BFLOAT),
            ((length, width_local), FLOAT),
            ((8, 128), FLOAT),
            ((length, 256), FLOAT),
        ],
        owner,
        mix_grad_rows,
        mid_near,
        mid_far,
        gates,
        mixer_low,
        seg_wide,
        seg_row,
    )
    dt_start = width_local + query_cols
    mid_kept, mid_sent, _ = parted(
        [(normed_rows, zq_low), (mix_grad_rows, mixed_low)], order, last_group
    )
    mid_sent, seg_row = together(mid_sent, seg_row)
    mid_got = send(mid_sent, last_group, count)
    in_low, taps_grad, head_grad, share_terms = call(
        functools.partial(mixer_back_kernel, head_local),
        [
            ((length, width_local + 128), BFLOAT),
            ((8, conv_width), FLOAT),
            ((8, 128), FLOAT),
            ((length, share_cols), FLOAT),
        ],
        owner,
        pre_grad,
        mixer_kept,
        mixer_low,
        kv_grad,
        taps,
        head_pack,
        seg_wide,
        seg_row,
        scratch=[pltpu.VMEM((length, conv_width), FLOAT)],
    )
    share_terms = share_terms + swap(share_terms, "tensor", 4, 1)
    share_terms = share_terms + swap(share_terms.astype(BFLOAT), "tensor", 4, 2).astype(FLOAT)
    share_low = share_terms.astype(BFLOAT)
    block_width = share_cols // 4
    shared_mine = lax.dynamic_slice_in_dim(shared_full, shard_index * block_width, block_width, 1)
    block_low = lax.dynamic_slice_in_dim(share_low, shard_index * block_width, block_width, 1)
    share_grad = einsum_f32("ld,lk->dk", normed_rows, share_low).reshape(count, 4, share_rows, share_cols)
    share_grad = lax.dynamic_index_in_dim(share_grad, shard_index, 1, keepdims=False)
    share_grad = share_grad.reshape(count * share_rows, share_cols)
    in_kept, in_sent, _ = parted([(normed_rows, in_low)], order, last_group)
    share_kept, share_sent, _ = split(share_grad, order, last_group, [share_rows])
    in_kept = jnp.concatenate([in_kept, share_kept], axis=0)
    in_sent = [jnp.concatenate(pair, axis=0) for pair in zip(in_sent, share_sent)]
    mid_got, gu_got, block_low, in_sent = together(mid_got, gu_got, block_low, in_sent)
    gu_sum = add(gu_kept, gu_got)
    mid_kept, mid_got = finish(mid_kept, mid_got, stay, back, count)
    in_got = send(in_sent, last_group, count)
    keep, give = call(
        input_back_kernel,
        [halves, halves],
        core,
        in_low,
        zq_low,
        block_low,
        early_near,
        early_far,
        mid_near,
        mid_far,
        shared_mine,
    )
    normed_one_grad = finish_tensor(keep, give, shard_index)
    token_norm_grad, gain_one_grad = norm_one_back(normed_one_grad)
    conv_full = lax.dynamic_update_slice_in_dim(
        jnp.zeros_like(conv_params), taps_grad[:5, :width_local], shard_index * width_local, 1
    )
    conv_full = conv_full.at[:, bc_start:].set(taps_grad[:5, width_local:])
    head_full = lax.dynamic_update_slice_in_dim(
        jnp.zeros_like(head_params),
        jnp.concatenate([head_grad[:2, :head_local], skip_lanes[:1, :head_local]], axis=0),
        shard_index * head_local,
        1,
    )
    wide = conv_params.shape[1]
    features, head_count = gains.shape[1], head_params.shape[1]
    gains_grad = relocate([jnp.stack([gain_one_grad, gain_two_grad])], dp_index, count, False)[0]
    small = jnp.concatenate(
        [
            jnp.pad(
                jnp.concatenate([gains_grad, head_full[:2]], axis=1),
                ((0, 0), (0, wide - features - head_count)),
            ),
            conv_full,
            jnp.pad(head_full[2:], ((0, 0), (0, wide - head_count))),
        ],
        axis=0,
    )
    for bits in (1, 2):
        small = group_sum(small, "tensor", 4, [bits])
    in_got, mid_got, down_got, out_give, small = together(in_got, mid_got, down_got, out_give, small)
    mid_sum = add(mid_kept, mid_got)
    in_sum = add(*finish(in_kept, in_got, stay, back, count, [rows, share_rows]))
    down_sum = add(*finish(down_kept, down_got, down_stay, back[1:] + last, count))
    ffn_sum = finish_tensor(out_keep, out_give, shard_index)
    output = (hidden + ffn_sum).astype(BFLOAT)
    z_sum = mid_sum[:, :dt_start]
    out_sum = mid_sum[:, dt_start:]
    small = group_sum(small, "dp", count, last_group)
    small, in_sum, output = together(small, in_sum, output)
    for group in first:
        small = group_sum(small, "dp", count, group)
    shared_sum = in_sum[rows:]
    in_sum = in_sum[:rows]
    return (
        *relocate([output, hidden_grad + token_norm_grad], dp_index, count, False),
        jnp.stack([z_sum[:, :width_local], in_sum[:, :width_local]]),
        in_sum[:, width_local : width_local + head_local],
        z_sum[:, width_local:],
        out_sum[:, :width_local].T,
        out_sum[:, width_local:].T,
        jnp.stack([gu_sum[:, :ff_local], gu_sum[:, ff_local:]]),
        down_sum.T,
        shared_sum,
        small[:2, :features],
        small[2:7],
        jnp.concatenate(
            [small[:2, features : features + head_count], small[7:, :head_count]], axis=0
        ),
    )


def solution(mesh):
    count = mesh.shape["dp"]
    placed = (
        P(("dp", "tensor"), None),
        P("dp"),
        P(None, "dp", "tensor"),
        P("dp", "tensor"),
        P("dp", "tensor"),
        P("tensor", "dp"),
        P("tensor", "dp"),
        P(None, "dp", "tensor"),
        P("tensor", "dp"),
        P(("dp", "tensor"), None),
        P(),
        P(),
        P(),
        P(("dp", "tensor"), None),
    )

    def body(*arrays):
        return per_device(count, *arrays)

    return jax.shard_map(
        body,
        mesh=mesh,
        in_specs=placed,
        out_specs=(
            P(("dp", "tensor"), None),
            P(("dp", "tensor"), None),
            P(None, "dp", "tensor"),
            P("dp", "tensor"),
            P("dp", "tensor"),
            P("tensor", "dp"),
            P("tensor", "dp"),
            P(None, "dp", "tensor"),
            P("tensor", "dp"),
            P(("dp", "tensor"), None),
            P(),
            P(),
            P(),
        ),
        check_vma=False,
    )
```

```python
import functools
import math

import jax
import jax.numpy as jnp
from jax import lax
from jax.experimental import pallas as pl
from jax.experimental.pallas import tpu as pltpu
from jax.sharding import PartitionSpec as P

HDM = 64
NSTATE = 128
QH = 8
KVH = 2
HD = 64


EPSILON = 1e-05
FLOAT = jnp.float32
BFLOAT = jnp.bfloat16
WHOLE = pl.BlockSpec()


def rms_norm(values, scale_vec):
    return (
        values * lax.rsqrt(jnp.mean(values * values, axis=-1, keepdims=True) + EPSILON) * scale_vec
    )


def einsum_f32(pattern, op_left, op_right):
    return jnp.einsum(pattern, op_left, op_right, preferred_element_type=jnp.float32)


def silu_gate(gate_proj, up_proj):
    return jax.nn.silu(gate_proj) * up_proj


def swap(values, axis, count, bits):
    return lax.ppermute(values, axis, [(i, i ^ bits) for i in range(count)])


def stages_of(count):
    top = count.bit_length() - 1
    groups = []
    while top > 0:
        low = max(0, top - 2)
        groups.append([m << low for m in range(1, 1 << (top - low))])
        top = low
    return groups


def block_order(count):
    order = [0]
    for group in stages_of(count):
        order = order + [r ^ m for m in group for r in order]
    return order


def relocate_kernel(order, to_relative, index_ref, *refs):
    for source, target in zip(refs[: len(refs) // 2], refs[len(refs) // 2 :]):
        block = source.shape[1] // len(order)
        for k, r in enumerate(order):
            here = slice(k * block, (k + 1) * block)
            there = pl.ds(pl.multiple_of((index_ref[0] ^ r) * block, block), block)
            if to_relative:
                target[:, here] = source[:, there]
            else:
                target[:, there] = source[:, here]


def relocate(arrays, index, count, to_relative):
    order = block_order(count)
    if arrays[0].shape[1] // count % 128 == 0:
        return call(
            functools.partial(relocate_kernel, order, to_relative),
            [(a.shape, a.dtype) for a in arrays],
            index[None],
            *arrays,
        )
    places = jnp.array(order, jnp.int32) ^ index
    if not to_relative:
        places = jnp.argsort(places)
    moved = [a.reshape(a.shape[0], count, -1)[:, places].reshape(a.shape) for a in arrays]
    return moved


def together(*values):
    return lax.optimization_barrier(values)


def stack_kernel(*refs):
    *parts, out_ref = refs
    start = 0
    for part in parts:
        out_ref[start : start + part.shape[0], :] = part[...]
        start += part.shape[0]


def stacked(parts):
    rows = sum(p.shape[0] for p in parts)
    return pl.pallas_call(
        stack_kernel,
        out_shape=jax.ShapeDtypeStruct((rows, parts[0].shape[1]), parts[0].dtype),
        in_specs=[WHOLE] * len(parts),
        out_specs=WHOLE,
        compiler_params=pltpu.CompilerParams(vmem_limit_bytes=16 * 1024 * 1024),
        cost_estimate=pl.CostEstimate(flops=1000, bytes_accessed=1000, transcendentals=0),
    )(*parts)


def gather(stack, have, groups, count):
    parts, places = [stack], [have]
    for k, group in enumerate(groups):
        if k > 0:
            stack = stacked(parts)
            have = [r for p in places for r in p]
        parts = [stack] + [swap(stack, "dp", count, m) for m in group]
        places = [have] + [[r ^ m for r in have] for m in group]
    return parts, places


def joined(parts, places):
    return stacked(parts), [r for p in places for r in p]


def two(parts, places):
    far = parts[1] if len(parts) == 2 else stacked(parts[1:])
    return (parts[0], far), places


def column_runs(places, order):
    found = []
    for have in places:
        runs = []
        for row, r in enumerate(have):
            col = order.index(r)
            if runs and runs[-1][0] + runs[-1][2] == col:
                runs[-1] = (runs[-1][0], runs[-1][1], runs[-1][2] + 1)
            else:
                runs.append((col, row, 1))
        found.append(runs)
    return found


def write_products(runs_of, block, lefts, rights, outs):
    start = 0
    for left, right in zip(lefts, rights):
        right_now = right[...]
        width = right_now.shape[1]
        for out, runs in zip(outs, runs_of):
            row = 0
            for col, n in runs:
                found = dot(left[:, col * block : (col + n) * block], right_now, 0, 0)
                out[row * block : (row + n) * block, start : start + width] = found.astype(out.dtype)
                row += n
        start += width


def products_kernel(runs_of, block, count, *refs):
    write_products(runs_of, block, refs[:count], refs[count : 2 * count], refs[2 * count :])


def plan(order, group):
    span = 0
    for m in group:
        span |= m
    stay = [r for r in order if r & span == 0]
    runs_of = []
    for blocks in [stay] + [[r ^ m for r in stay] for m in group]:
        runs = []
        for r in blocks:
            col = order.index(r)
            if runs and sum(runs[-1]) == col:
                runs[-1] = (runs[-1][0], runs[-1][1] + 1)
            else:
                runs.append((col, 1))
        runs_of.append(runs)
    return runs_of, stay


def product_shapes(stay, block, width, group):
    return [((len(stay) * block, width), FLOAT)] + [((len(stay) * block, width), BFLOAT)] * len(group)


def parted(pairs, order, group):
    block = pairs[0][0].shape[1] // len(order)
    runs_of, stay = plan(order, group)
    shape = (len(stay) * block, sum(right.shape[1] for _, right in pairs))
    kept, *sent = pl.pallas_call(
        functools.partial(products_kernel, runs_of, block, len(pairs)),
        out_shape=[jax.ShapeDtypeStruct(shape, FLOAT)]
        + [jax.ShapeDtypeStruct(shape, BFLOAT)] * len(group),
        in_specs=[WHOLE] * (2 * len(pairs)),
        out_specs=[WHOLE] * (1 + len(group)),
        compiler_params=pltpu.CompilerParams(vmem_limit_bytes=16 * 1024 * 1024),
        cost_estimate=pl.CostEstimate(flops=1000, bytes_accessed=1000, transcendentals=0),
    )(*[left for left, _ in pairs], *[right for _, right in pairs])
    return kept, sent, stay


def send(sent, group, count):
    return [swap(part, "dp", count, m) for m, part in zip(group, sent)]


def add(kept, got):
    for part in got:
        kept = kept + part.astype(FLOAT)
    return kept


def split(total, order, group, sizes):
    span = 0
    for m in group:
        span |= m
    stay = [r for r in order if r & span == 0]

    def rows(blocks):
        parts = []
        start = 0
        for size in sizes:
            parts += [total[start + order.index(r) * size :][:size] for r in blocks]
            start += size * len(order)
        return jnp.concatenate(parts, axis=0)

    return rows(stay), [rows([r ^ m for r in stay]).astype(BFLOAT) for m in group], stay


def add_split_kernel(spans, kept_ref, *refs):
    got, outs = refs[: len(refs) - len(spans)], refs[len(refs) - len(spans) :]
    for out, found in zip(outs, spans):
        row = 0
        for start, size in found:
            total = kept_ref[start : start + size, :]
            for part in got:
                total = total + part[start : start + size, :].astype(FLOAT)
            out[row : row + size, :] = total.astype(out.dtype)
            row += size


def add_split(kept, got, order, group, sizes):
    span = 0
    for m in group:
        span |= m
    stay = [r for r in order if r & span == 0]
    spans = []
    for blocks in [stay] + [[r ^ m for r in stay] for m in group]:
        start, found = 0, []
        for size in sizes:
            found += [(start + order.index(r) * size, size) for r in blocks]
            start += size * len(order)
        spans.append(found)
    shape = (sum(sizes) * len(stay), kept.shape[1])
    kept, *sent = pl.pallas_call(
        functools.partial(add_split_kernel, spans),
        out_shape=[jax.ShapeDtypeStruct(shape, FLOAT)]
        + [jax.ShapeDtypeStruct(shape, BFLOAT)] * len(group),
        in_specs=[WHOLE] * (1 + len(got)),
        out_specs=[WHOLE] * (1 + len(group)),
        compiler_params=pltpu.CompilerParams(vmem_limit_bytes=16 * 1024 * 1024),
        cost_estimate=pl.CostEstimate(flops=1000, bytes_accessed=1000, transcendentals=0),
    )(kept, *got)
    return kept, sent, stay


def finish(kept, got, order, groups, count, sizes=None):
    if sizes is None:
        sizes = [kept.shape[0] // len(order)]
    for group in groups:
        if min(sizes) % 16 == 0:
            kept, sent, order = add_split(kept, got, order, group, sizes)
        else:
            kept, sent, order = split(add(kept, got), order, group, sizes)
        got = send(sent, group, count)
    return kept, got


def dot(left, right, left_dim=1, right_dim=0):
    return lax.dot_general(
        left, right, (((left_dim,), (right_dim,)), ((), ())), preferred_element_type=FLOAT
    )


def exact_dot(left, right):
    return jnp.dot(left, right, precision=lax.Precision.HIGHEST, preferred_element_type=FLOAT)


def sigmoid(values):
    return 1.0 / (1.0 + jnp.exp(-values))


def softplus(values):
    return jnp.maximum(values, 0.0) + jnp.log1p(jnp.exp(-jnp.abs(values)))


def lanes_of(shape):
    return lax.broadcasted_iota(jnp.int32, shape, 1)


def same_document(seg_wide, offset):
    if offset == 0:
        return None
    row = lax.broadcasted_iota(jnp.int32, seg_wide.shape, 0)
    same = jnp.logical_and(pltpu.roll(seg_wide, offset, 0) == seg_wide, row >= offset)
    return jnp.where(same, 1.0, 0.0)


def square_mask(seg_wide, seg_row):
    length = seg_wide.shape[0]
    row = lax.broadcasted_iota(jnp.int32, (length, length), 0)
    col = lax.broadcasted_iota(jnp.int32, (length, length), 1)
    wide = jnp.concatenate([seg_wide] * (length // 128), axis=1)
    return jnp.logical_and(row >= col, wide == seg_row[0:1, :])


def triangle(length, flip):
    row = lax.broadcasted_iota(jnp.int32, (length, length), 0)
    col = lax.broadcasted_iota(jnp.int32, (length, length), 1)
    return jnp.where(row <= col if flip else row >= col, 1.0, 0.0)


def head_lanes(values, head, lane):
    return jnp.where((lane >= HDM) == (head == 1), values, jnp.zeros_like(values))


def softmax_of(queries, keys, mask, head, lane):
    scores = dot(head_lanes(queries, head, lane), keys, 1, 1) * (1.0 / math.sqrt(HD))
    masked = jnp.where(mask, scores, -1000000000.0)
    grown = jnp.exp(masked - jnp.max(masked, axis=-1, keepdims=True))
    return grown / jnp.sum(grown, axis=-1, keepdims=True)


def views(ref, widths):
    found = []
    start = 0
    for width in widths:
        found.append(ref.at[:, start : start + width])
        start += width
    return found


def kept_views(ref, width):
    return views(ref, (width + 256, width + 256, 128, 128, ref.shape[0]))


def low_views(ref, width):
    return views(ref, (width + 256, 128, 256))


def mixer_kernel(
    heads, owner_ref, normed_ref, near_ref, far_ref, shared_ref, taps_ref, head_ref, seg_ref, seg_row_ref,
    kept_ref, low_ref, pre_gate_ref, attn_ref,
):
    conv_in_ref, conv_pre_ref, step_ref, decay_ref, gram_ref = kept_views(kept_ref, pre_gate_ref.shape[1])
    conv_low_ref, query_ref, kv_ref = low_views(low_ref, pre_gate_ref.shape[1])
    length = normed_ref.shape[0]
    half = near_ref.shape[0]
    width = pre_gate_ref.shape[1]
    conv_width = conv_in_ref.shape[1]
    normed = normed_ref[...]
    taps = taps_ref[...]
    seg = seg_ref[...]
    mask = square_mask(seg, seg_row_ref[...])
    lead = dot(normed[:, :half], near_ref[:, 128:]) + dot(normed[:, half:], far_ref[:, 128:])
    x_raw = lead[:, 256:]
    shared = dot(normed, shared_ref[...]).astype(BFLOAT)
    queries = lead[:, :128].astype(BFLOAT)
    query_ref[...] = queries
    lane = lanes_of((length, 128))
    keep_half = (lane >= HD) == (owner_ref[0] == 1)
    shared_f = shared.astype(FLOAT)
    keys = jnp.where(keep_half, shared_f[:, :128], pltpu.roll(shared_f[:, :128], HD, 1)).astype(BFLOAT)
    values = jnp.where(keep_half, shared_f[:, 128:256], pltpu.roll(shared_f[:, 128:256], HD, 1)).astype(BFLOAT)
    kv_ref[:, :128] = keys
    kv_ref[:, 128:] = values
    outs = [dot(softmax_of(queries, keys, mask, h, lane).astype(BFLOAT), values) for h in range(2)]
    attn_ref[...] = jnp.where(lane < HD, outs[0], outs[1]).astype(BFLOAT)
    step_pre = lead[:, 128:256] + head_ref[0:1, :]
    step_ref[...] = step_pre
    step_size = softplus(step_pre)
    decay = exact_dot(triangle(length, False), step_size * -jnp.exp(head_ref[1:2, :]))
    decay_ref[...] = decay
    sames = [same_document(seg, o) for o in range(4)]
    for start in range(0, conv_width, 128):
        cols = slice(start, start + 128)
        if start < width:
            u = x_raw[:, cols]
        else:
            u = shared_f[:, 256 + start - width : 256 + start - width + 128]
        conv_in_ref[:, cols] = u
        pre = taps[4:5, cols] + taps[3:4, cols] * u
        for o in range(1, 4):
            pre = pre + taps[3 - o : 4 - o, cols] * (pltpu.roll(u, o, 0) * sames[o])
        conv_pre_ref[:, cols] = pre
        conv_low_ref[:, cols] = (pre * sigmoid(pre)).astype(BFLOAT)
    b_state = conv_low_ref[:, width : width + 128]
    c_state = conv_low_ref[:, width + 128 :]
    gram = dot(c_state, b_state, 1, 1)
    gram_ref[...] = gram
    step_rows, decay_rows = step_size.T, decay.T
    for pair in range(heads // 2):
        cols = slice(128 * pair, 128 * pair + 128)
        x_pair = conv_low_ref[:, cols]
        found = []
        for h in (2 * pair, 2 * pair + 1):
            gap = decay[:, h : h + 1] - decay_rows[h : h + 1, :]
            grown = jnp.where(mask, jnp.exp(jnp.where(mask, gap, 0.0)), 0.0)
            found.append(dot((gram * grown * step_rows[h : h + 1, :]).astype(BFLOAT), x_pair))
        y_pair = jnp.where(lane < HDM, found[0], found[1])
        pre_gate_ref[:, cols] = y_pair + taps[5:6, cols] * x_pair.astype(FLOAT)


def pieces_of(terms, at_core, axis):
    size = terms.shape[axis] // 4
    blocks = [lax.slice_in_dim(terms, k * size, (k + 1) * size, axis=axis) for k in range(4)]
    keep = [jnp.where(at_core, blocks[2 * y], blocks[2 * y + 1]) for y in range(2)]
    give = [jnp.where(at_core, blocks[2 * y + 1], blocks[2 * y]) for y in range(2)]
    return keep, give


def gate_kernel(
    core_ref, normed_ref, near_ref, far_ref, pre_gate_ref, attn_ref, gates_ref, mixed_ref, keep_ref, give_ref
):
    half = near_ref.shape[0]
    width = pre_gate_ref.shape[1]
    normed = normed_ref[...]
    gate_z = dot(normed[:, :half], near_ref[:, :width]) + dot(normed[:, half:], far_ref[:, :width])
    gates_ref[:, :width] = gate_z
    gates_ref[:, width:] = pre_gate_ref[...]
    gated = (pre_gate_ref[...] * (gate_z * sigmoid(gate_z))).astype(BFLOAT)
    mixed_ref[:, :width] = gated
    mixed_ref[:, width:] = attn_ref[...]
    mixed = mixed_ref[...]
    at_core = core_ref[0] == 0
    start = 0
    for part in (near_ref, far_ref):
        terms = dot(mixed, part[:, width:], 1, 1)
        cols = slice(start, start + part.shape[0])
        start += part.shape[0]
        keep, give = pieces_of(terms, at_core, 0)
        for y in range(2):
            keep_ref[y, :, cols] = keep[y]
            give_ref[y, :, cols] = give[y]


def input_back_kernel(
    core_ref, in_low_ref, zq_ref, block_ref, early_near_ref, early_far_ref, near_ref, far_ref,
    shared_ref, keep_ref, give_ref,
):
    width = zq_ref.shape[1] - 128
    x_low, step_low = in_low_ref[:, :width], in_low_ref[:, width:]
    z_low, query_low = zq_ref[:, :width], zq_ref[:, width:]
    block = block_ref[...]
    at_core = core_ref[0] == 0
    start = 0
    for early, part in ((early_near_ref, near_ref), (early_far_ref, far_ref)):
        cols = slice(start, start + part.shape[0])
        start += part.shape[0]
        terms = (
            dot(x_low, early[:, 384:], 1, 1)
            + dot(query_low, early[:, 128:256], 1, 1)
            + dot(step_low, early[:, 256:384], 1, 1)
            + dot(z_low, part[:, :width], 1, 1)
            + dot(block, shared_ref[cols, :], 1, 1)
        )
        keep, give = pieces_of(terms, at_core, 0)
        for y in range(2):
            keep_ref[y, :, cols] = keep[y]
            give_ref[y, :, cols] = give[y]


def gate_back_kernel(
    owner_ref, grad_ref, near_ref, far_ref, gates_ref, low_ref, seg_ref, seg_row_ref,
    zq_ref, pre_grad_ref, skip_ref, kv_grad_ref,
):
    half = near_ref.shape[0]
    width = pre_grad_ref.shape[1]
    conv_low_ref, query_ref, kv_ref = low_views(low_ref, width)
    grad = grad_ref[...]
    mixed_grad = dot(grad[:, :half], near_ref[:, width:]) + dot(grad[:, half:], far_ref[:, width:])
    gated_grad = mixed_grad[:, :width]
    gate_z = gates_ref[:, :width]
    s = sigmoid(gate_z)
    pre_grad = gated_grad * (gate_z * s)
    pre_grad_ref[...] = pre_grad
    zq_ref[:, :width] = (gated_grad * gates_ref[:, width:] * (s * (1.0 + gate_z * (1.0 - s)))).astype(BFLOAT)
    skip = jnp.sum(pre_grad * conv_low_ref[:, :width].astype(FLOAT), axis=0, keepdims=True)
    row = lax.broadcasted_iota(jnp.int32, (width, 128), 0)
    col = lax.broadcasted_iota(jnp.int32, (width, 128), 1)
    of_head = jnp.where(jnp.logical_and(row >= col * HDM, row < (col + 1) * HDM), 1.0, 0.0)
    skip_ref[...] = exact_dot(jnp.broadcast_to(skip, (8, width)), of_head)
    lane = lanes_of((grad.shape[0], 128))
    out_low = mixed_grad[:, width:].astype(BFLOAT)
    mask = square_mask(seg_ref[...], seg_row_ref[...])
    queries, keys, values = query_ref[...], kv_ref[:, :128], kv_ref[:, 128:]
    query_grads, key_sum, value_sum = [], 0.0, 0.0
    for h in range(2):
        probs = softmax_of(queries, keys, mask, h, lane)
        out_head = head_lanes(out_low, h, lane)
        prob_grad = dot(out_head, values, 1, 1)
        score = probs * (prob_grad - jnp.sum(probs * prob_grad, axis=-1, keepdims=True))
        score_low = score.astype(BFLOAT)
        query_grads.append(dot(score_low, keys))
        key_sum = key_sum + dot(score_low, head_lanes(queries, h, lane), 0, 0)
        value_sum = value_sum + dot(probs.astype(BFLOAT), out_head, 0, 0)
    scale = 1.0 / math.sqrt(HD)
    zq_ref[:, width:] = (jnp.where(lane < HD, query_grads[0], query_grads[1]) * scale).astype(BFLOAT)
    mine = (lane >= HD) == (owner_ref[0] == 1)
    for k, total in enumerate((key_sum * scale, value_sum)):
        both = total + pltpu.roll(total, HD, 1)
        kv_grad_ref[:, 128 * k : 128 * k + 128] = jnp.where(mine, both, 0.0)


def mixer_back_kernel(
    heads, owner_ref, pre_grad_ref, kept_ref, low_ref, kv_grad_ref, taps_ref, head_ref, seg_ref, seg_row_ref,
    in_low_ref, taps_grad_ref, head_grad_ref, share_ref, act_grad_ref,
):
    conv_in_ref, conv_pre_ref, step_ref, decay_ref, gram_ref = kept_views(kept_ref, pre_grad_ref.shape[1])
    conv_low_ref = low_views(low_ref, pre_grad_ref.shape[1])[0]
    length = pre_grad_ref.shape[0]
    width = pre_grad_ref.shape[1]
    conv_width = conv_in_ref.shape[1]
    taps = taps_ref[...]
    seg = seg_ref[...]
    mask = square_mask(seg, seg_row_ref[...])
    lane = lanes_of((length, 128))
    step_pre = step_ref[...]
    step_size = softplus(step_pre)
    decay = decay_ref[...]
    step_rows, decay_rows = step_size.T, decay.T
    gram = gram_ref[...]
    b_state = conv_low_ref[:, width : width + 128]
    c_state = conv_low_ref[:, width + 128 :]
    b_grad, c_grad = 0.0, 0.0
    step_grad_rows, row_sums = [], jnp.zeros((length, 128), FLOAT)
    for pair in range(heads // 2):
        cols = slice(128 * pair, 128 * pair + 128)
        x_pair = conv_low_ref[:, cols]
        pre_grad = pre_grad_ref[:, cols]
        y_pair = pre_grad.astype(BFLOAT)
        found = []
        for k in range(2):
            h = 2 * pair + k
            gap = decay[:, h : h + 1] - decay_rows[h : h + 1, :]
            grown = jnp.where(mask, jnp.exp(jnp.where(mask, gap, 0.0)), 0.0)
            step_row = step_rows[h : h + 1, :]
            y_head = head_lanes(y_pair, k, lane)
            weights_grad = dot(y_head, x_pair, 1, 1)
            shaped = weights_grad * grown
            gram_grad = (shaped * step_row).astype(BFLOAT)
            c_grad = c_grad + dot(gram_grad, b_state)
            b_grad = b_grad + dot(gram_grad, c_state, 0, 0)
            terms = shaped * gram
            step_grad_rows.append(jnp.sum(terms, axis=0, keepdims=True))
            sums = jnp.sum(terms * step_row, axis=1, keepdims=True)
            row_sums = jnp.where(lane == h, sums, row_sums)
            weights_low = (gram * grown * step_row).astype(BFLOAT)
            found.append(dot(weights_low, y_head, 0, 0))
        x_grad = pre_grad * taps[5:6, cols] + jnp.where(lane < HDM, found[0], found[1])
        act_grad_ref[:, cols] = x_grad
    act_grad_ref[:, width : width + 128] = b_grad
    act_grad_ref[:, width + 128 :] = c_grad
    step_grad = jnp.concatenate(
        step_grad_rows + [jnp.zeros((128 - heads, length), FLOAT)], axis=0
    ).T
    rate = -jnp.exp(head_ref[1:2, :])
    back_sum = exact_dot(triangle(length, True), row_sums - step_grad * step_size)
    raw_grad = (step_grad + rate * back_sum) * sigmoid(step_pre)
    raw_grad = jnp.where(lane < heads, raw_grad, 0.0)
    in_low_ref[:, width:] = raw_grad.astype(BFLOAT)
    head_grad_ref[0:1, :] = jnp.sum(raw_grad, axis=0, keepdims=True)
    head_grad_ref[1:2, :] = jnp.sum(rate * step_size * back_sum, axis=0, keepdims=True)
    head_grad_ref[2:8, :] = jnp.zeros((6, 128), FLOAT)
    sames = [same_document(seg, o) for o in range(4)]
    share_ref[:, :256] = kv_grad_ref[...]
    for start in range(0, conv_width, 128):
        cols = slice(start, start + 128)
        pre = conv_pre_ref[:, cols]
        s = sigmoid(pre)
        a = act_grad_ref[:, cols] * (s * (1.0 + pre * (1.0 - s)))
        u = conv_in_ref[:, cols]
        raw = taps[3:4, cols] * a
        taps_grad_ref[3:4, cols] = jnp.sum(a * u, axis=0, keepdims=True)
        taps_grad_ref[4:5, cols] = jnp.sum(a, axis=0, keepdims=True)
        for o in range(1, 4):
            masked = a * sames[o]
            raw = raw + taps[3 - o : 4 - o, cols] * pltpu.roll(masked, length - o, 0)
            taps_grad_ref[3 - o : 4 - o, cols] = jnp.sum(
                masked * pltpu.roll(u, o, 0), axis=0, keepdims=True
            )
        if start < width:
            in_low_ref[:, cols] = raw.astype(BFLOAT)
        else:
            share_ref[:, 256 + start - width : 256 + start - width + 128] = raw
    taps_grad_ref[5:8, :] = jnp.zeros((3, conv_width), FLOAT)


def call(kernel, outs, scalar, *arrays, scratch=()):
    return pl.pallas_call(
        kernel,
        out_shape=[jax.ShapeDtypeStruct(shape, dtype) for shape, dtype in outs],
        in_specs=[pl.BlockSpec(memory_space=pltpu.SMEM)]
        + [WHOLE] * len(arrays),
        out_specs=[WHOLE] * len(outs),
        scratch_shapes=list(scratch),
        compiler_params=pltpu.CompilerParams(vmem_limit_bytes=16 * 1024 * 1024),
        cost_estimate=pl.CostEstimate(flops=1000, bytes_accessed=1000, transcendentals=0),
    )(scalar, *arrays)


def finish_tensor(keep, give, index):
    sums = keep + swap(give, "tensor", 4, 1)
    half = index >> 1
    mine = jnp.where(half == 0, sums[0], sums[1])
    other = jnp.where(half == 0, sums[1], sums[0])
    return mine + swap(other.astype(BFLOAT), "tensor", 4, 2).astype(FLOAT)


def sum_tensor(partial, index):
    keep, give = pieces_of(partial, index & 1 == 0, 0)
    return finish_tensor(jnp.stack(keep), jnp.stack(give), index)


def ffn_kernel(
    gu_runs, down_runs, gu_plan, down_plan, core_ref, rows_ref, cot_ref, *refs
):
    gu_refs, refs = refs[: len(gu_runs)], refs[len(gu_runs) :]
    down_refs, refs = refs[: len(down_runs)], refs[len(down_runs) :]
    keep_ref, give_ref, out_keep_ref, out_give_ref, *refs = refs
    gu_outs, refs = refs[: len(gu_plan)], refs[len(gu_plan) :]
    down_outs, (gu_low_ref, act_ref) = refs[: len(down_plan)], refs[len(down_plan) :]
    width = act_ref.shape[1]
    block = sum(n for runs in gu_runs for _, _, n in runs)
    block = rows_ref.shape[1] // block

    def inner(left_ref, parts, found):
        total = 0.0
        for part, runs in zip(parts, found):
            for col, row, n in runs:
                total = total + dot(
                    left_ref[:, col * block : (col + n) * block], part[row * block : (row + n) * block, :]
                )
        return total

    def outer(left, parts, found, to_keep, to_give):
        for part, runs in zip(parts, found):
            for col, row, n in runs:
                terms = dot(left, part[row * block : (row + n) * block, :], 1, 1)
                keep, give = pieces_of(terms, at_core, 0)
                for y in range(2):
                    to_keep[y, :, col * block : (col + n) * block] = keep[y]
                    to_give[y, :, col * block : (col + n) * block] = give[y]

    at_core = core_ref[0] == 0
    gate_up = inner(rows_ref, gu_refs, gu_runs)
    gate_proj, up_proj = gate_up[:, :width], gate_up[:, width:]
    s = sigmoid(gate_proj)
    silu = gate_proj * s
    act = (silu * up_proj).astype(BFLOAT)
    act_ref[...] = act
    act_grad = inner(cot_ref, down_refs, down_runs)
    gu_low_ref[:, :width] = (act_grad * up_proj * (s * (1.0 + gate_proj * (1.0 - s)))).astype(BFLOAT)
    gu_low_ref[:, width:] = (act_grad * silu).astype(BFLOAT)
    outer(gu_low_ref[...], gu_refs, gu_runs, keep_ref, give_ref)
    outer(act, down_refs, down_runs, out_keep_ref, out_give_ref)
    write_products(gu_plan, block, [rows_ref], [gu_low_ref], gu_outs)
    write_products(down_plan, block, [cot_ref], [act_ref], down_outs)


def gather_tensor(values):
    return lax.all_gather(values, "tensor", axis=0, tiled=True)


def group_sum(values, axis, axis_count, bits):
    parts = [values] + [swap(values, axis, axis_count, m) for m in bits]
    while len(parts) > 1:
        parts = [parts[k] + parts[k + 1] for k in range(0, len(parts), 2)]
    return parts[0]


def per_device(
    count,
    tokens,
    segments,
    zx_weight,
    dt_weight,
    query_weight,
    ssm_out_weight,
    attn_out_weight,
    gate_up_weight,
    down_weight,
    shared_weight,
    norm_gains,
    conv_params,
    head_params,
    cotangent,
):
    shard_index = lax.axis_index("tensor")
    dp_index = lax.axis_index("dp")
    length = segments.shape[0]
    rows = zx_weight.shape[1]
    head_local = dt_weight.shape[1]
    width_local = zx_weight.shape[2]
    query_cols = query_weight.shape[1]
    query_local = query_cols // HD
    ff_local = down_weight.shape[0]
    share_rows = shared_weight.shape[0]
    share_cols = shared_weight.shape[1]

    token_rel, cot_local = relocate([tokens, cotangent], dp_index, count, True)
    token_f = token_rel.astype(FLOAT)
    gains = relocate([norm_gains], dp_index, count, True)[0]
    normed_one, norm_one_back = jax.vjp(rms_norm, token_f, gains[0])
    normed_rows = gather_tensor(normed_one.astype(BFLOAT))

    seg_wide = jnp.broadcast_to(segments.astype(FLOAT)[:, None], (length, 128))
    seg_row = jnp.broadcast_to(segments.astype(FLOAT)[None], (8, length))

    shared_pack = shared_weight.reshape(share_rows, 4, share_cols // 4)
    shared_pack = jnp.concatenate([shared_pack[:, k] for k in range(4)], axis=0)
    dt_pad = jnp.pad(dt_weight, ((0, 0), (0, 128 - head_local)))
    groups = stages_of(count)
    first, last = groups[:-1], groups[-1:]
    order = block_order(count)
    lead_piece = jnp.concatenate([shared_pack, query_weight, dt_pad, zx_weight[1]], axis=1)
    mid_piece = jnp.concatenate([zx_weight[0], ssm_out_weight.T, attn_out_weight.T], axis=1)
    gu_piece = jnp.concatenate([gate_up_weight[0], gate_up_weight[1]], axis=1)
    down_half, down_have = joined(*gather(down_weight.T, [0], last, count))
    early_half, have = joined(*gather(lead_piece, [0], first, count))
    early_half, down_half, mid_piece, normed_rows, seg_row = together(
        early_half, down_half, mid_piece, normed_rows, seg_row
    )
    cot_rows = gather_tensor(cot_local)
    (early_near, early_far), _ = two(*gather(early_half, have, last, count))
    mid_half, _ = joined(*gather(mid_piece, [0], first, count))
    mid_half, early_far, gu_piece, cot_rows, seg_row = together(
        mid_half, early_far, gu_piece, cot_rows, seg_row
    )
    (mid_near, mid_far), _ = two(*gather(mid_half, have, last, count))
    gu_first, gu_first_places = gather(gu_piece, [0], first, count)
    shared_got = jnp.concatenate([early_near[:, :128], early_far[:, :128]], axis=0)
    shared_got = shared_got.reshape(count, 4, share_rows, share_cols // 4)
    shared_got = jnp.concatenate([shared_got[:, k] for k in range(4)], axis=-1)
    near = jnp.stack([shared_got, swap(shared_got, "tensor", 4, 1)])
    both = jnp.stack([near, swap(near, "tensor", 4, 2)])
    both = jnp.where(shard_index >> 1 == 1, both[::-1], both)
    both = jnp.where(shard_index & 1 == 1, both[:, ::-1], both)
    shared_full = both.transpose(2, 0, 1, 3, 4).reshape(count * rows, share_cols)

    head_mine = lax.dynamic_slice_in_dim(head_params, shard_index * head_local, head_local, 1)
    bc_start = conv_params.shape[1] - 2 * NSTATE
    conv_mine = jnp.concatenate(
        [
            lax.dynamic_slice_in_dim(conv_params, shard_index * width_local, width_local, 1),
            conv_params[:, bc_start:],
        ],
        axis=1,
    )
    conv_width = width_local + 2 * NSTATE
    taps = jnp.concatenate([conv_mine, jnp.pad(jnp.repeat(head_mine[2], HDM), (0, 2 * NSTATE))[None]], axis=0)
    taps = jnp.pad(taps, ((0, 8 - taps.shape[0]), (0, 0)))
    head_pack = jnp.pad(head_mine, ((0, 5), (0, 128 - head_local)))
    core = (shard_index & 1)[None]
    owner = ((shard_index * query_local) // (QH // KVH))[None]
    width_full = count * rows
    kept_width = 2 * conv_width + 256 + length
    low_width = conv_width + 128 + 256
    mixer_kept, mixer_low, pre_gate, attn_low = call(
        functools.partial(mixer_kernel, head_local),
        [
            ((length, kept_width), FLOAT),
            ((length, low_width), BFLOAT),
            ((length, width_local), FLOAT),
            ((length, 128), BFLOAT),
        ],
        owner,
        normed_rows,
        early_near,
        early_far,
        shared_full,
        taps,
        head_pack,
        seg_wide,
        seg_row,
    )
    pre_gate, gu_first = together(pre_gate, gu_first)
    gu_half, _ = joined(gu_first, gu_first_places)
    gu_half, mid_far, down_half, seg_row = together(gu_half, mid_far, down_half, seg_row)
    gu_parts, gu_places = gather(gu_half, have, last, count)
    down_parts, down_places = gather(down_half, down_have, first, count)
    halves = ((2, length // 4, width_full), FLOAT)
    gates, mixed_low, keep, give = call(
        gate_kernel,
        [((length, 2 * width_local), FLOAT), ((length, width_local + 128), BFLOAT), halves, halves],
        core,
        normed_rows,
        mid_near,
        mid_far,
        pre_gate,
        attn_low,
    )
    hidden = token_f + finish_tensor(keep, give, shard_index)
    normed_two, norm_two_back = jax.vjp(rms_norm, hidden, gains[1])
    ffn_rows = gather_tensor(normed_two.astype(BFLOAT))
    last_group = last[0]
    back = groups[:-1][::-1]
    gu_plan, stay = plan(order, last_group)
    down_plan, down_stay = plan(order, back[0])
    keep, give, out_keep, out_give, *found = call(
        functools.partial(
            ffn_kernel, column_runs(gu_places, order), column_runs(down_places, order), gu_plan, down_plan
        ),
        [halves] * 4
        + product_shapes(stay, rows, 2 * ff_local, last_group)
        + product_shapes(down_stay, rows, ff_local, back[0]),
        core,
        ffn_rows,
        cot_rows,
        *gu_parts,
        *down_parts,
        scratch=[pltpu.VMEM((length, 2 * ff_local), BFLOAT), pltpu.VMEM((length, ff_local), BFLOAT)],
    )
    gu_found, down_found = found[: len(gu_plan)], found[len(gu_plan) :]
    gu_kept, gu_sent = gu_found[0], gu_found[1:]
    down_kept, down_sent = down_found[0], down_found[1:]
    gu_sent, down_sent, seg_row = together(gu_sent, down_sent, seg_row)
    gu_got = send(gu_sent, last_group, count)
    down_got = send(down_sent, back[0], count)
    normed_two_grad = finish_tensor(keep, give, shard_index)
    hidden_norm_grad, gain_two_grad = norm_two_back(normed_two_grad)
    hidden_grad = cot_local.astype(FLOAT) + hidden_norm_grad
    mix_grad_rows = gather_tensor(hidden_grad.astype(BFLOAT))
    gu_got, down_got, mix_grad_rows, seg_row = together(gu_got, down_got, mix_grad_rows, seg_row)
    if len(back) == 1 and rows % 16 == 0:
        gu_kept, gu_sent, _ = add_split(gu_kept, gu_got, stay, back[0], [rows])
        gu_sent, mix_grad_rows = together(gu_sent, mix_grad_rows)
        gu_got = send(gu_sent, back[0], count)
    else:
        gu_kept, gu_got = finish(gu_kept, gu_got, stay, back, count)
    zq_low, pre_grad, skip_lanes, kv_grad = call(
        gate_back_kernel,
        [
            ((length, width_local + 128), BFLOAT),
            ((length, width_local), FLOAT),
            ((8, 128), FLOAT),
            ((length, 256), FLOAT),
        ],
        owner,
        mix_grad_rows,
        mid_near,
        mid_far,
        gates,
        mixer_low,
        seg_wide,
        seg_row,
    )
    dt_start = width_local + query_cols
    mid_kept, mid_sent, _ = parted(
        [(normed_rows, zq_low), (mix_grad_rows, mixed_low)], order, last_group
    )
    mid_sent, seg_row = together(mid_sent, seg_row)
    mid_got = send(mid_sent, last_group, count)
    in_low, taps_grad, head_grad, share_terms = call(
        functools.partial(mixer_back_kernel, head_local),
        [
            ((length, width_local + 128), BFLOAT),
            ((8, conv_width), FLOAT),
            ((8, 128), FLOAT),
            ((length, share_cols), FLOAT),
        ],
        owner,
        pre_grad,
        mixer_kept,
        mixer_low,
        kv_grad,
        taps,
        head_pack,
        seg_wide,
        seg_row,
        scratch=[pltpu.VMEM((length, conv_width), FLOAT)],
    )
    share_terms = share_terms + swap(share_terms, "tensor", 4, 1)
    share_terms = share_terms + swap(share_terms.astype(BFLOAT), "tensor", 4, 2).astype(FLOAT)
    share_low = share_terms.astype(BFLOAT)
    block_width = share_cols // 4
    shared_mine = lax.dynamic_slice_in_dim(shared_full, shard_index * block_width, block_width, 1)
    block_low = lax.dynamic_slice_in_dim(share_low, shard_index * block_width, block_width, 1)
    share_grad = einsum_f32("ld,lk->dk", normed_rows, share_low).reshape(count, 4, share_rows, share_cols)
    share_grad = lax.dynamic_index_in_dim(share_grad, shard_index, 1, keepdims=False)
    share_grad = share_grad.reshape(count * share_rows, share_cols)
    in_kept, in_sent, _ = parted([(normed_rows, in_low)], order, last_group)
    share_kept, share_sent, _ = split(share_grad, order, last_group, [share_rows])
    in_kept = jnp.concatenate([in_kept, share_kept], axis=0)
    in_sent = [jnp.concatenate(pair, axis=0) for pair in zip(in_sent, share_sent)]
    mid_got, gu_got, block_low, in_sent = together(mid_got, gu_got, block_low, in_sent)
    gu_sum = add(gu_kept, gu_got)
    mid_kept, mid_got = finish(mid_kept, mid_got, stay, back, count)
    in_got = send(in_sent, last_group, count)
    keep, give = call(
        input_back_kernel,
        [halves, halves],
        core,
        in_low,
        zq_low,
        block_low,
        early_near,
        early_far,
        mid_near,
        mid_far,
        shared_mine,
    )
    normed_one_grad = finish_tensor(keep, give, shard_index)
    token_norm_grad, gain_one_grad = norm_one_back(normed_one_grad)
    conv_full = lax.dynamic_update_slice_in_dim(
        jnp.zeros_like(conv_params), taps_grad[:5, :width_local], shard_index * width_local, 1
    )
    conv_full = conv_full.at[:, bc_start:].set(taps_grad[:5, width_local:])
    head_full = lax.dynamic_update_slice_in_dim(
        jnp.zeros_like(head_params),
        jnp.concatenate([head_grad[:2, :head_local], skip_lanes[:1, :head_local]], axis=0),
        shard_index * head_local,
        1,
    )
    wide = conv_params.shape[1]
    features, head_count = gains.shape[1], head_params.shape[1]
    gains_grad = relocate([jnp.stack([gain_one_grad, gain_two_grad])], dp_index, count, False)[0]
    small = jnp.concatenate(
        [
            jnp.pad(
                jnp.concatenate([gains_grad, head_full[:2]], axis=1),
                ((0, 0), (0, wide - features - head_count)),
            ),
            conv_full,
            jnp.pad(head_full[2:], ((0, 0), (0, wide - head_count))),
        ],
        axis=0,
    )
    for bits in (1, 2):
        small = group_sum(small, "tensor", 4, [bits])
    in_got, mid_got, down_got, out_give, small = together(in_got, mid_got, down_got, out_give, small)
    mid_sum = add(mid_kept, mid_got)
    in_sum = add(*finish(in_kept, in_got, stay, back, count, [rows, share_rows]))
    down_sum = add(*finish(down_kept, down_got, down_stay, back[1:] + last, count))
    ffn_sum = finish_tensor(out_keep, out_give, shard_index)
    output = (hidden + ffn_sum).astype(BFLOAT)
    z_sum = mid_sum[:, :dt_start]
    out_sum = mid_sum[:, dt_start:]
    small = group_sum(small, "dp", count, last_group)
    small, in_sum, output = together(small, in_sum, output)
    for group in first:
        small = group_sum(small, "dp", count, group)
    shared_sum = in_sum[rows:]
    in_sum = in_sum[:rows]
    return (
        *relocate([output, hidden_grad + token_norm_grad], dp_index, count, False),
        jnp.stack([z_sum[:, :width_local], in_sum[:, :width_local]]),
        in_sum[:, width_local : width_local + head_local],
        z_sum[:, width_local:],
        out_sum[:, :width_local].T,
        out_sum[:, width_local:].T,
        jnp.stack([gu_sum[:, :ff_local], gu_sum[:, ff_local:]]),
        down_sum.T,
        shared_sum,
        small[:2, :features],
        small[2:7],
        jnp.concatenate(
            [small[:2, features : features + head_count], small[7:, :head_count]], axis=0
        ),
    )


def solution(mesh):
    count = mesh.shape["dp"]
    placed = (
        P(("dp", "tensor"), None),
        P("dp"),
        P(None, "dp", "tensor"),
        P("dp", "tensor"),
        P("dp", "tensor"),
        P("tensor", "dp"),
        P("tensor", "dp"),
        P(None, "dp", "tensor"),
        P("tensor", "dp"),
        P(("dp", "tensor"), None),
        P(),
        P(),
        P(),
        P(("dp", "tensor"), None),
    )

    def body(*arrays):
        return per_device(count, *arrays)

    return jax.shard_map(
        body,
        mesh=mesh,
        in_specs=placed,
        out_specs=(
            P(("dp", "tensor"), None),
            P(("dp", "tensor"), None),
            P(None, "dp", "tensor"),
            P("dp", "tensor"),
            P("dp", "tensor"),
            P("tensor", "dp"),
            P("tensor", "dp"),
            P(None, "dp", "tensor"),
            P("tensor", "dp"),
            P(("dp", "tensor"), None),
            P(),
            P(),
            P(),
        ),
        check_vma=False,
    )
```

```python
import functools
import math

import jax
import jax.numpy as jnp
from jax import lax
from jax.experimental import pallas as pl
from jax.experimental.pallas import tpu as pltpu
from jax.sharding import PartitionSpec as P

HDM = 64
NSTATE = 128
QH = 8
KVH = 2
HD = 64


EPSILON = 1e-05
FLOAT = jnp.float32
BFLOAT = jnp.bfloat16
WHOLE = pl.BlockSpec()


def rms_norm(values, scale_vec):
    return (
        values * lax.rsqrt(jnp.mean(values * values, axis=-1, keepdims=True) + EPSILON) * scale_vec
    )


def einsum_f32(pattern, op_left, op_right):
    return jnp.einsum(pattern, op_left, op_right, preferred_element_type=jnp.float32)


def silu_gate(gate_proj, up_proj):
    return jax.nn.silu(gate_proj) * up_proj


def swap(values, axis, count, bits):
    return lax.ppermute(values, axis, [(i, i ^ bits) for i in range(count)])


def stages_of(count):
    top = count.bit_length() - 1
    groups = []
    while top > 0:
        low = max(0, top - 2)
        groups.append([m << low for m in range(1, 1 << (top - low))])
        top = low
    return groups


def block_order(count):
    order = [0]
    for group in stages_of(count):
        order = order + [r ^ m for m in group for r in order]
    return order


def relocate_kernel(order, to_relative, index_ref, *refs):
    for source, target in zip(refs[: len(refs) // 2], refs[len(refs) // 2 :]):
        block = source.shape[1] // len(order)
        for k, r in enumerate(order):
            here = slice(k * block, (k + 1) * block)
            there = pl.ds(pl.multiple_of((index_ref[0] ^ r) * block, block), block)
            if to_relative:
                target[:, here] = source[:, there]
            else:
                target[:, there] = source[:, here]


def relocate(arrays, index, count, to_relative):
    order = block_order(count)
    if arrays[0].shape[1] // count % 128 == 0:
        return call(
            functools.partial(relocate_kernel, order, to_relative),
            [(a.shape, a.dtype) for a in arrays],
            index[None],
            *arrays,
        )
    places = jnp.array(order, jnp.int32) ^ index
    if not to_relative:
        places = jnp.argsort(places)
    moved = [a.reshape(a.shape[0], count, -1)[:, places].reshape(a.shape) for a in arrays]
    return moved


def together(*values):
    return lax.optimization_barrier(values)


def stack_kernel(*refs):
    *parts, out_ref = refs
    start = 0
    for part in parts:
        out_ref[start : start + part.shape[0], :] = part[...]
        start += part.shape[0]


def stacked(parts):
    rows = sum(p.shape[0] for p in parts)
    return pl.pallas_call(
        stack_kernel,
        out_shape=jax.ShapeDtypeStruct((rows, parts[0].shape[1]), parts[0].dtype),
        in_specs=[WHOLE] * len(parts),
        out_specs=WHOLE,
        compiler_params=pltpu.CompilerParams(vmem_limit_bytes=16 * 1024 * 1024),
        cost_estimate=pl.CostEstimate(flops=1000, bytes_accessed=1000, transcendentals=0),
    )(*parts)


def gather(stack, have, groups, count):
    parts, places = [stack], [have]
    for k, group in enumerate(groups):
        if k > 0:
            stack = stacked(parts)
            have = [r for p in places for r in p]
        parts = [stack] + [swap(stack, "dp", count, m) for m in group]
        places = [have] + [[r ^ m for r in have] for m in group]
    return parts, places


def joined(parts, places):
    return stacked(parts), [r for p in places for r in p]


def two(parts, places):
    far = parts[1] if len(parts) == 2 else stacked(parts[1:])
    return (parts[0], far), places


def column_runs(places, order):
    found = []
    for have in places:
        runs = []
        for row, r in enumerate(have):
            col = order.index(r)
            if runs and runs[-1][0] + runs[-1][2] == col:
                runs[-1] = (runs[-1][0], runs[-1][1], runs[-1][2] + 1)
            else:
                runs.append((col, row, 1))
        found.append(runs)
    return found


def write_products(runs_of, block, lefts, rights, outs):
    start = 0
    for left, right in zip(lefts, rights):
        right_now = right[...]
        width = right_now.shape[1]
        for out, runs in zip(outs, runs_of):
            row = 0
            for col, n in runs:
                found = dot(left[:, col * block : (col + n) * block], right_now, 0, 0)
                out[row * block : (row + n) * block, start : start + width] = found.astype(out.dtype)
                row += n
        start += width


def products_kernel(runs_of, block, count, *refs):
    write_products(runs_of, block, refs[:count], refs[count : 2 * count], refs[2 * count :])


def plan(order, group):
    span = 0
    for m in group:
        span |= m
    stay = [r for r in order if r & span == 0]
    runs_of = []
    for blocks in [stay] + [[r ^ m for r in stay] for m in group]:
        runs = []
        for r in blocks:
            col = order.index(r)
            if runs and sum(runs[-1]) == col:
                runs[-1] = (runs[-1][0], runs[-1][1] + 1)
            else:
                runs.append((col, 1))
        runs_of.append(runs)
    return runs_of, stay


def product_shapes(stay, block, width, group):
    return [((len(stay) * block, width), FLOAT)] + [((len(stay) * block, width), BFLOAT)] * len(group)


def parted(pairs, order, group):
    block = pairs[0][0].shape[1] // len(order)
    runs_of, stay = plan(order, group)
    shape = (len(stay) * block, sum(right.shape[1] for _, right in pairs))
    kept, *sent = pl.pallas_call(
        functools.partial(products_kernel, runs_of, block, len(pairs)),
        out_shape=[jax.ShapeDtypeStruct(shape, FLOAT)]
        + [jax.ShapeDtypeStruct(shape, BFLOAT)] * len(group),
        in_specs=[WHOLE] * (2 * len(pairs)),
        out_specs=[WHOLE] * (1 + len(group)),
        compiler_params=pltpu.CompilerParams(vmem_limit_bytes=16 * 1024 * 1024),
        cost_estimate=pl.CostEstimate(flops=1000, bytes_accessed=1000, transcendentals=0),
    )(*[left for left, _ in pairs], *[right for _, right in pairs])
    return kept, sent, stay


def send(sent, group, count):
    return [swap(part, "dp", count, m) for m, part in zip(group, sent)]


def add(kept, got):
    for part in got:
        kept = kept + part.astype(FLOAT)
    return kept


def split(total, order, group, sizes):
    span = 0
    for m in group:
        span |= m
    stay = [r for r in order if r & span == 0]

    def rows(blocks):
        parts = []
        start = 0
        for size in sizes:
            parts += [total[start + order.index(r) * size :][:size] for r in blocks]
            start += size * len(order)
        return jnp.concatenate(parts, axis=0)

    return rows(stay), [rows([r ^ m for r in stay]).astype(BFLOAT) for m in group], stay


def add_split_kernel(spans, kept_ref, *refs):
    got, outs = refs[: len(refs) - len(spans)], refs[len(refs) - len(spans) :]
    for out, found in zip(outs, spans):
        row = 0
        for start, size in found:
            total = kept_ref[start : start + size, :]
            for part in got:
                total = total + part[start : start + size, :].astype(FLOAT)
            out[row : row + size, :] = total.astype(out.dtype)
            row += size


def add_split(kept, got, order, group, sizes):
    span = 0
    for m in group:
        span |= m
    stay = [r for r in order if r & span == 0]
    spans = []
    for blocks in [stay] + [[r ^ m for r in stay] for m in group]:
        start, found = 0, []
        for size in sizes:
            found += [(start + order.index(r) * size, size) for r in blocks]
            start += size * len(order)
        spans.append(found)
    shape = (sum(sizes) * len(stay), kept.shape[1])
    kept, *sent = pl.pallas_call(
        functools.partial(add_split_kernel, spans),
        out_shape=[jax.ShapeDtypeStruct(shape, FLOAT)]
        + [jax.ShapeDtypeStruct(shape, BFLOAT)] * len(group),
        in_specs=[WHOLE] * (1 + len(got)),
        out_specs=[WHOLE] * (1 + len(group)),
        compiler_params=pltpu.CompilerParams(vmem_limit_bytes=16 * 1024 * 1024),
        cost_estimate=pl.CostEstimate(flops=1000, bytes_accessed=1000, transcendentals=0),
    )(kept, *got)
    return kept, sent, stay


def finish(kept, got, order, groups, count, sizes=None):
    if sizes is None:
        sizes = [kept.shape[0] // len(order)]
    for group in groups:
        if min(sizes) % 16 == 0:
            kept, sent, order = add_split(kept, got, order, group, sizes)
        else:
            kept, sent, order = split(add(kept, got), order, group, sizes)
        got = send(sent, group, count)
    return kept, got


def dot(left, right, left_dim=1, right_dim=0):
    return lax.dot_general(
        left, right, (((left_dim,), (right_dim,)), ((), ())), preferred_element_type=FLOAT
    )


def exact_dot(left, right):
    return jnp.dot(left, right, precision=lax.Precision.HIGHEST, preferred_element_type=FLOAT)


def sigmoid(values):
    return 1.0 / (1.0 + jnp.exp(-values))


def softplus(values):
    return jnp.maximum(values, 0.0) + jnp.log1p(jnp.exp(-jnp.abs(values)))


def lanes_of(shape):
    return lax.broadcasted_iota(jnp.int32, shape, 1)


def same_document(seg_wide, offset):
    if offset == 0:
        return None
    row = lax.broadcasted_iota(jnp.int32, seg_wide.shape, 0)
    same = jnp.logical_and(pltpu.roll(seg_wide, offset, 0) == seg_wide, row >= offset)
    return jnp.where(same, 1.0, 0.0)


def square_mask(seg_wide, seg_row):
    length = seg_wide.shape[0]
    row = lax.broadcasted_iota(jnp.int32, (length, length), 0)
    col = lax.broadcasted_iota(jnp.int32, (length, length), 1)
    wide = jnp.concatenate([seg_wide] * (length // 128), axis=1)
    return jnp.logical_and(row >= col, wide == seg_row[0:1, :])


def triangle(length, flip):
    row = lax.broadcasted_iota(jnp.int32, (length, length), 0)
    col = lax.broadcasted_iota(jnp.int32, (length, length), 1)
    return jnp.where(row <= col if flip else row >= col, 1.0, 0.0)


def head_lanes(values, head, lane):
    return jnp.where((lane >= HDM) == (head == 1), values, jnp.zeros_like(values))


def softmax_of(queries, keys, mask, head, lane):
    scores = dot(head_lanes(queries, head, lane), keys, 1, 1) * (1.0 / math.sqrt(HD))
    masked = jnp.where(mask, scores, -1000000000.0)
    grown = jnp.exp(masked - jnp.max(masked, axis=-1, keepdims=True))
    return grown / jnp.sum(grown, axis=-1, keepdims=True)


def views(ref, widths):
    found = []
    start = 0
    for width in widths:
        found.append(ref.at[:, start : start + width])
        start += width
    return found


def kept_views(ref, width):
    return views(ref, (width + 256, width + 256, 128, 128, ref.shape[0]))


def low_views(ref, width):
    return views(ref, (width + 256, 128, 256))


def mixer_kernel(
    heads, owner_ref, normed_ref, near_ref, far_ref, shared_ref, taps_ref, head_ref, seg_ref, seg_row_ref,
    kept_ref, low_ref, pre_gate_ref, attn_ref,
):
    conv_in_ref, conv_pre_ref, step_ref, decay_ref, gram_ref = kept_views(kept_ref, pre_gate_ref.shape[1])
    conv_low_ref, query_ref, kv_ref = low_views(low_ref, pre_gate_ref.shape[1])
    length = normed_ref.shape[0]
    half = near_ref.shape[0]
    width = pre_gate_ref.shape[1]
    conv_width = conv_in_ref.shape[1]
    normed = normed_ref[...]
    taps = taps_ref[...]
    seg = seg_ref[...]
    mask = square_mask(seg, seg_row_ref[...])
    lead = dot(normed[:, :half], near_ref[:, 128:]) + dot(normed[:, half:], far_ref[:, 128:])
    x_raw = lead[:, 256:]
    shared = dot(normed, shared_ref[...]).astype(BFLOAT)
    queries = lead[:, :128].astype(BFLOAT)
    query_ref[...] = queries
    lane = lanes_of((length, 128))
    keep_half = (lane >= HD) == (owner_ref[0] == 1)
    shared_f = shared.astype(FLOAT)
    keys = jnp.where(keep_half, shared_f[:, :128], pltpu.roll(shared_f[:, :128], HD, 1)).astype(BFLOAT)
    values = jnp.where(keep_half, shared_f[:, 128:256], pltpu.roll(shared_f[:, 128:256], HD, 1)).astype(BFLOAT)
    kv_ref[:, :128] = keys
    kv_ref[:, 128:] = values
    outs = [dot(softmax_of(queries, keys, mask, h, lane).astype(BFLOAT), values) for h in range(2)]
    attn_ref[...] = jnp.where(lane < HD, outs[0], outs[1]).astype(BFLOAT)
    step_pre = lead[:, 128:256] + head_ref[0:1, :]
    step_ref[...] = step_pre
    step_size = softplus(step_pre)
    decay = exact_dot(triangle(length, False), step_size * -jnp.exp(head_ref[1:2, :]))
    decay_ref[...] = decay
    sames = [same_document(seg, o) for o in range(4)]
    for start in range(0, conv_width, 128):
        cols = slice(start, start + 128)
        if start < width:
            u = x_raw[:, cols]
        else:
            u = shared_f[:, 256 + start - width : 256 + start - width + 128]
        conv_in_ref[:, cols] = u
        pre = taps[4:5, cols] + taps[3:4, cols] * u
        for o in range(1, 4):
            pre = pre + taps[3 - o : 4 - o, cols] * (pltpu.roll(u, o, 0) * sames[o])
        conv_pre_ref[:, cols] = pre
        conv_low_ref[:, cols] = (pre * sigmoid(pre)).astype(BFLOAT)
    b_state = conv_low_ref[:, width : width + 128]
    c_state = conv_low_ref[:, width + 128 :]
    gram = dot(c_state, b_state, 1, 1)
    gram_ref[...] = gram
    step_rows, decay_rows = step_size.T, decay.T
    for pair in range(heads // 2):
        cols = slice(128 * pair, 128 * pair + 128)
        x_pair = conv_low_ref[:, cols]
        found = []
        for h in (2 * pair, 2 * pair + 1):
            gap = decay[:, h : h + 1] - decay_rows[h : h + 1, :]
            grown = jnp.where(mask, jnp.exp(jnp.where(mask, gap, 0.0)), 0.0)
            found.append(dot((gram * grown * step_rows[h : h + 1, :]).astype(BFLOAT), x_pair))
        y_pair = jnp.where(lane < HDM, found[0], found[1])
        pre_gate_ref[:, cols] = y_pair + taps[5:6, cols] * x_pair.astype(FLOAT)


def pieces_of(terms, at_core, axis):
    size = terms.shape[axis] // 4
    blocks = [lax.slice_in_dim(terms, k * size, (k + 1) * size, axis=axis) for k in range(4)]
    keep = [jnp.where(at_core, blocks[2 * y], blocks[2 * y + 1]) for y in range(2)]
    give = [jnp.where(at_core, blocks[2 * y + 1], blocks[2 * y]) for y in range(2)]
    return keep, give


def gate_kernel(
    core_ref, normed_ref, near_ref, far_ref, pre_gate_ref, attn_ref, gates_ref, mixed_ref, keep_ref, give_ref
):
    half = near_ref.shape[0]
    width = pre_gate_ref.shape[1]
    normed = normed_ref[...]
    gate_z = dot(normed[:, :half], near_ref[:, :width]) + dot(normed[:, half:], far_ref[:, :width])
    gates_ref[:, :width] = gate_z
    gates_ref[:, width:] = pre_gate_ref[...]
    gated = (pre_gate_ref[...] * (gate_z * sigmoid(gate_z))).astype(BFLOAT)
    mixed_ref[:, :width] = gated
    mixed_ref[:, width:] = attn_ref[...]
    mixed = mixed_ref[...]
    at_core = core_ref[0] == 0
    start = 0
    for part in (near_ref, far_ref):
        terms = dot(mixed, part[:, width:], 1, 1)
        cols = slice(start, start + part.shape[0])
        start += part.shape[0]
        keep, give = pieces_of(terms, at_core, 0)
        for y in range(2):
            keep_ref[y, :, cols] = keep[y]
            give_ref[y, :, cols] = give[y]


def input_back_kernel(
    core_ref, in_low_ref, zq_ref, block_ref, early_near_ref, early_far_ref, near_ref, far_ref,
    shared_ref, keep_ref, give_ref,
):
    width = zq_ref.shape[1] - 128
    x_low, step_low = in_low_ref[:, :width], in_low_ref[:, width:]
    z_low, query_low = zq_ref[:, :width], zq_ref[:, width:]
    block = block_ref[...]
    at_core = core_ref[0] == 0
    start = 0
    for early, part in ((early_near_ref, near_ref), (early_far_ref, far_ref)):
        cols = slice(start, start + part.shape[0])
        start += part.shape[0]
        terms = (
            dot(x_low, early[:, 384:], 1, 1)
            + dot(query_low, early[:, 128:256], 1, 1)
            + dot(step_low, early[:, 256:384], 1, 1)
            + dot(z_low, part[:, :width], 1, 1)
            + dot(block, shared_ref[cols, :], 1, 1)
        )
        keep, give = pieces_of(terms, at_core, 0)
        for y in range(2):
            keep_ref[y, :, cols] = keep[y]
            give_ref[y, :, cols] = give[y]


def gate_back_kernel(
    owner_ref, grad_ref, near_ref, far_ref, gates_ref, low_ref, seg_ref, seg_row_ref,
    zq_ref, pre_grad_ref, skip_ref, kv_grad_ref,
):
    half = near_ref.shape[0]
    width = pre_grad_ref.shape[1]
    conv_low_ref, query_ref, kv_ref = low_views(low_ref, width)
    grad = grad_ref[...]
    mixed_grad = dot(grad[:, :half], near_ref[:, width:]) + dot(grad[:, half:], far_ref[:, width:])
    gated_grad = mixed_grad[:, :width]
    gate_z = gates_ref[:, :width]
    s = sigmoid(gate_z)
    pre_grad = gated_grad * (gate_z * s)
    pre_grad_ref[...] = pre_grad
    zq_ref[:, :width] = (gated_grad * gates_ref[:, width:] * (s * (1.0 + gate_z * (1.0 - s)))).astype(BFLOAT)
    skip = jnp.sum(pre_grad * conv_low_ref[:, :width].astype(FLOAT), axis=0, keepdims=True)
    row = lax.broadcasted_iota(jnp.int32, (width, 128), 0)
    col = lax.broadcasted_iota(jnp.int32, (width, 128), 1)
    of_head = jnp.where(jnp.logical_and(row >= col * HDM, row < (col + 1) * HDM), 1.0, 0.0)
    skip_ref[...] = exact_dot(jnp.broadcast_to(skip, (8, width)), of_head)
    lane = lanes_of((grad.shape[0], 128))
    out_low = mixed_grad[:, width:].astype(BFLOAT)
    mask = square_mask(seg_ref[...], seg_row_ref[...])
    queries, keys, values = query_ref[...], kv_ref[:, :128], kv_ref[:, 128:]
    query_grads, key_sum, value_sum = [], 0.0, 0.0
    for h in range(2):
        probs = softmax_of(queries, keys, mask, h, lane)
        out_head = head_lanes(out_low, h, lane)
        prob_grad = dot(out_head, values, 1, 1)
        score = probs * (prob_grad - jnp.sum(probs * prob_grad, axis=-1, keepdims=True))
        score_low = score.astype(BFLOAT)
        query_grads.append(dot(score_low, keys))
        key_sum = key_sum + dot(score_low, head_lanes(queries, h, lane), 0, 0)
        value_sum = value_sum + dot(probs.astype(BFLOAT), out_head, 0, 0)
    scale = 1.0 / math.sqrt(HD)
    zq_ref[:, width:] = (jnp.where(lane < HD, query_grads[0], query_grads[1]) * scale).astype(BFLOAT)
    mine = (lane >= HD) == (owner_ref[0] == 1)
    for k, total in enumerate((key_sum * scale, value_sum)):
        both = total + pltpu.roll(total, HD, 1)
        kv_grad_ref[:, 128 * k : 128 * k + 128] = jnp.where(mine, both, 0.0)


def mixer_back_kernel(
    heads, owner_ref, pre_grad_ref, kept_ref, low_ref, kv_grad_ref, taps_ref, head_ref, seg_ref, seg_row_ref,
    in_low_ref, taps_grad_ref, head_grad_ref, share_ref, act_grad_ref,
):
    conv_in_ref, conv_pre_ref, step_ref, decay_ref, gram_ref = kept_views(kept_ref, pre_grad_ref.shape[1])
    conv_low_ref = low_views(low_ref, pre_grad_ref.shape[1])[0]
    length = pre_grad_ref.shape[0]
    width = pre_grad_ref.shape[1]
    conv_width = conv_in_ref.shape[1]
    taps = taps_ref[...]
    seg = seg_ref[...]
    mask = square_mask(seg, seg_row_ref[...])
    lane = lanes_of((length, 128))
    step_pre = step_ref[...]
    step_size = softplus(step_pre)
    decay = decay_ref[...]
    step_rows, decay_rows = step_size.T, decay.T
    gram = gram_ref[...]
    b_state = conv_low_ref[:, width : width + 128]
    c_state = conv_low_ref[:, width + 128 :]
    b_grad, c_grad = 0.0, 0.0
    step_grad_rows, row_sums = [], jnp.zeros((length, 128), FLOAT)
    for pair in range(heads // 2):
        cols = slice(128 * pair, 128 * pair + 128)
        x_pair = conv_low_ref[:, cols]
        pre_grad = pre_grad_ref[:, cols]
        y_pair = pre_grad.astype(BFLOAT)
        found = []
        for k in range(2):
            h = 2 * pair + k
            gap = decay[:, h : h + 1] - decay_rows[h : h + 1, :]
            grown = jnp.where(mask, jnp.exp(jnp.where(mask, gap, 0.0)), 0.0)
            step_row = step_rows[h : h + 1, :]
            y_head = head_lanes(y_pair, k, lane)
            weights_grad = dot(y_head, x_pair, 1, 1)
            shaped = weights_grad * grown
            gram_grad = (shaped * step_row).astype(BFLOAT)
            c_grad = c_grad + dot(gram_grad, b_state)
            b_grad = b_grad + dot(gram_grad, c_state, 0, 0)
            terms = shaped * gram
            step_grad_rows.append(jnp.sum(terms, axis=0, keepdims=True))
            sums = jnp.sum(terms * step_row, axis=1, keepdims=True)
            row_sums = jnp.where(lane == h, sums, row_sums)
            weights_low = (gram * grown * step_row).astype(BFLOAT)
            found.append(dot(weights_low, y_head, 0, 0))
        x_grad = pre_grad * taps[5:6, cols] + jnp.where(lane < HDM, found[0], found[1])
        act_grad_ref[:, cols] = x_grad
    act_grad_ref[:, width : width + 128] = b_grad
    act_grad_ref[:, width + 128 :] = c_grad
    step_grad = jnp.concatenate(
        step_grad_rows + [jnp.zeros((128 - heads, length), FLOAT)], axis=0
    ).T
    rate = -jnp.exp(head_ref[1:2, :])
    back_sum = exact_dot(triangle(length, True), row_sums - step_grad * step_size)
    raw_grad = (step_grad + rate * back_sum) * sigmoid(step_pre)
    raw_grad = jnp.where(lane < heads, raw_grad, 0.0)
    in_low_ref[:, width:] = raw_grad.astype(BFLOAT)
    head_grad_ref[0:1, :] = jnp.sum(raw_grad, axis=0, keepdims=True)
    head_grad_ref[1:2, :] = jnp.sum(rate * step_size * back_sum, axis=0, keepdims=True)
    head_grad_ref[2:8, :] = jnp.zeros((6, 128), FLOAT)
    sames = [same_document(seg, o) for o in range(4)]
    share_ref[:, :256] = kv_grad_ref[...]
    for start in range(0, conv_width, 128):
        cols = slice(start, start + 128)
        pre = conv_pre_ref[:, cols]
        s = sigmoid(pre)
        a = act_grad_ref[:, cols] * (s * (1.0 + pre * (1.0 - s)))
        u = conv_in_ref[:, cols]
        raw = taps[3:4, cols] * a
        taps_grad_ref[3:4, cols] = jnp.sum(a * u, axis=0, keepdims=True)
        taps_grad_ref[4:5, cols] = jnp.sum(a, axis=0, keepdims=True)
        for o in range(1, 4):
            masked = a * sames[o]
            raw = raw + taps[3 - o : 4 - o, cols] * pltpu.roll(masked, length - o, 0)
            taps_grad_ref[3 - o : 4 - o, cols] = jnp.sum(
                masked * pltpu.roll(u, o, 0), axis=0, keepdims=True
            )
        if start < width:
            in_low_ref[:, cols] = raw.astype(BFLOAT)
        else:
            share_ref[:, 256 + start - width : 256 + start - width + 128] = raw
    taps_grad_ref[5:8, :] = jnp.zeros((3, conv_width), FLOAT)


def call(kernel, outs, scalar, *arrays, scratch=()):
    return pl.pallas_call(
        kernel,
        out_shape=[jax.ShapeDtypeStruct(shape, dtype) for shape, dtype in outs],
        in_specs=[pl.BlockSpec(memory_space=pltpu.SMEM)]
        + [WHOLE] * len(arrays),
        out_specs=[WHOLE] * len(outs),
        scratch_shapes=list(scratch),
        compiler_params=pltpu.CompilerParams(vmem_limit_bytes=16 * 1024 * 1024),
        cost_estimate=pl.CostEstimate(flops=1000, bytes_accessed=1000, transcendentals=0),
    )(scalar, *arrays)


def finish_tensor(keep, give, index):
    sums = keep + swap(give, "tensor", 4, 1)
    half = index >> 1
    mine = jnp.where(half == 0, sums[0], sums[1])
    other = jnp.where(half == 0, sums[1], sums[0])
    return mine + swap(other.astype(BFLOAT), "tensor", 4, 2).astype(FLOAT)


def sum_tensor(partial, index):
    keep, give = pieces_of(partial, index & 1 == 0, 0)
    return finish_tensor(jnp.stack(keep), jnp.stack(give), index)


def ffn_kernel(
    gu_runs, down_runs, gu_plan, down_plan, core_ref, rows_ref, cot_ref, *refs
):
    gu_refs, refs = refs[: len(gu_runs)], refs[len(gu_runs) :]
    down_refs, refs = refs[: len(down_runs)], refs[len(down_runs) :]
    keep_ref, give_ref, out_keep_ref, out_give_ref, *refs = refs
    gu_outs, refs = refs[: len(gu_plan)], refs[len(gu_plan) :]
    down_outs, (gu_low_ref, act_ref) = refs[: len(down_plan)], refs[len(down_plan) :]
    width = act_ref.shape[1]
    block = sum(n for runs in gu_runs for _, _, n in runs)
    block = rows_ref.shape[1] // block

    def inner(left_ref, parts, found):
        total = 0.0
        for part, runs in zip(parts, found):
            for col, row, n in runs:
                total = total + dot(
                    left_ref[:, col * block : (col + n) * block], part[row * block : (row + n) * block, :]
                )
        return total

    def outer(left, parts, found, to_keep, to_give):
        for part, runs in zip(parts, found):
            for col, row, n in runs:
                terms = dot(left, part[row * block : (row + n) * block, :], 1, 1)
                keep, give = pieces_of(terms, at_core, 0)
                for y in range(2):
                    to_keep[y, :, col * block : (col + n) * block] = keep[y]
                    to_give[y, :, col * block : (col + n) * block] = give[y]

    at_core = core_ref[0] == 0
    gate_up = inner(rows_ref, gu_refs, gu_runs)
    gate_proj, up_proj = gate_up[:, :width], gate_up[:, width:]
    s = sigmoid(gate_proj)
    silu = gate_proj * s
    act = (silu * up_proj).astype(BFLOAT)
    act_ref[...] = act
    act_grad = inner(cot_ref, down_refs, down_runs)
    gu_low_ref[:, :width] = (act_grad * up_proj * (s * (1.0 + gate_proj * (1.0 - s)))).astype(BFLOAT)
    gu_low_ref[:, width:] = (act_grad * silu).astype(BFLOAT)
    outer(gu_low_ref[...], gu_refs, gu_runs, keep_ref, give_ref)
    outer(act, down_refs, down_runs, out_keep_ref, out_give_ref)
    write_products(gu_plan, block, [rows_ref], [gu_low_ref], gu_outs)
    write_products(down_plan, block, [cot_ref], [act_ref], down_outs)


def gather_tensor(values):
    return lax.all_gather(values, "tensor", axis=0, tiled=True)


def group_sum(values, axis, axis_count, bits):
    parts = [values] + [swap(values, axis, axis_count, m) for m in bits]
    while len(parts) > 1:
        parts = [parts[k] + parts[k + 1] for k in range(0, len(parts), 2)]
    return parts[0]


def per_device(
    count,
    tokens,
    segments,
    zx_weight,
    dt_weight,
    query_weight,
    ssm_out_weight,
    attn_out_weight,
    gate_up_weight,
    down_weight,
    shared_weight,
    norm_gains,
    conv_params,
    head_params,
    cotangent,
):
    shard_index = lax.axis_index("tensor")
    dp_index = lax.axis_index("dp")
    length = segments.shape[0]
    rows = zx_weight.shape[1]
    head_local = dt_weight.shape[1]
    width_local = zx_weight.shape[2]
    query_cols = query_weight.shape[1]
    query_local = query_cols // HD
    ff_local = down_weight.shape[0]
    share_rows = shared_weight.shape[0]
    share_cols = shared_weight.shape[1]

    token_rel, cot_local = relocate([tokens, cotangent], dp_index, count, True)
    token_f = token_rel.astype(FLOAT)
    gains = relocate([norm_gains], dp_index, count, True)[0]
    normed_one, norm_one_back = jax.vjp(rms_norm, token_f, gains[0])
    normed_rows = gather_tensor(normed_one.astype(BFLOAT))

    seg_wide = jnp.broadcast_to(segments.astype(FLOAT)[:, None], (length, 128))
    seg_row = jnp.broadcast_to(segments.astype(FLOAT)[None], (8, length))

    shared_pack = shared_weight.reshape(share_rows, 4, share_cols // 4)
    shared_pack = jnp.concatenate([shared_pack[:, k] for k in range(4)], axis=0)
    dt_pad = jnp.pad(dt_weight, ((0, 0), (0, 128 - head_local)))
    groups = stages_of(count)
    first, last = groups[:-1], groups[-1:]
    order = block_order(count)
    lead_piece = jnp.concatenate([shared_pack, query_weight, dt_pad, zx_weight[1]], axis=1)
    mid_piece = jnp.concatenate([zx_weight[0], ssm_out_weight.T, attn_out_weight.T], axis=1)
    gu_piece = jnp.concatenate([gate_up_weight[0], gate_up_weight[1]], axis=1)
    down_half, down_have = joined(*gather(down_weight.T, [0], last, count))
    early_half, have = joined(*gather(lead_piece, [0], first, count))
    early_half, down_half, mid_piece, normed_rows, seg_row = together(
        early_half, down_half, mid_piece, normed_rows, seg_row
    )
    cot_rows = gather_tensor(cot_local)
    (early_near, early_far), _ = two(*gather(early_half, have, last, count))
    mid_half, _ = joined(*gather(mid_piece, [0], first, count))
    mid_half, early_far, gu_piece, cot_rows, seg_row = together(
        mid_half, early_far, gu_piece, cot_rows, seg_row
    )
    (mid_near, mid_far), _ = two(*gather(mid_half, have, last, count))
    gu_first, gu_first_places = gather(gu_piece, [0], first, count)
    shared_got = jnp.concatenate([early_near[:, :128], early_far[:, :128]], axis=0)
    shared_got = shared_got.reshape(count, 4, share_rows, share_cols // 4)
    shared_got = jnp.concatenate([shared_got[:, k] for k in range(4)], axis=-1)
    near = jnp.stack([shared_got, swap(shared_got, "tensor", 4, 1)])
    both = jnp.stack([near, swap(near, "tensor", 4, 2)])
    both = jnp.where(shard_index >> 1 == 1, both[::-1], both)
    both = jnp.where(shard_index & 1 == 1, both[:, ::-1], both)
    shared_full = both.transpose(2, 0, 1, 3, 4).reshape(count * rows, share_cols)

    head_mine = lax.dynamic_slice_in_dim(head_params, shard_index * head_local, head_local, 1)
    bc_start = conv_params.shape[1] - 2 * NSTATE
    conv_mine = jnp.concatenate(
        [
            lax.dynamic_slice_in_dim(conv_params, shard_index * width_local, width_local, 1),
            conv_params[:, bc_start:],
        ],
        axis=1,
    )
    conv_width = width_local + 2 * NSTATE
    taps = jnp.concatenate([conv_mine, jnp.pad(jnp.repeat(head_mine[2], HDM), (0, 2 * NSTATE))[None]], axis=0)
    taps = jnp.pad(taps, ((0, 8 - taps.shape[0]), (0, 0)))
    head_pack = jnp.pad(head_mine, ((0, 5), (0, 128 - head_local)))
    core = (shard_index & 1)[None]
    owner = ((shard_index * query_local) // (QH // KVH))[None]
    width_full = count * rows
    kept_width = 2 * conv_width + 256 + length
    low_width = conv_width + 128 + 256
    mixer_kept, mixer_low, pre_gate, attn_low = call(
        functools.partial(mixer_kernel, head_local),
        [
            ((length, kept_width), FLOAT),
            ((length, low_width), BFLOAT),
            ((length, width_local), FLOAT),
            ((length, 128), BFLOAT),
        ],
        owner,
        normed_rows,
        early_near,
        early_far,
        shared_full,
        taps,
        head_pack,
        seg_wide,
        seg_row,
    )
    pre_gate, gu_first = together(pre_gate, gu_first)
    gu_half, _ = joined(gu_first, gu_first_places)
    gu_half, mid_far, down_half, seg_row = together(gu_half, mid_far, down_half, seg_row)
    gu_parts, gu_places = gather(gu_half, have, last, count)
    down_parts, down_places = gather(down_half, down_have, first, count)
    halves = ((2, length // 4, width_full), FLOAT)
    gates, mixed_low, keep, give = call(
        gate_kernel,
        [((length, 2 * width_local), FLOAT), ((length, width_local + 128), BFLOAT), halves, halves],
        core,
        normed_rows,
        mid_near,
        mid_far,
        pre_gate,
        attn_low,
    )
    hidden = token_f + finish_tensor(keep, give, shard_index)
    normed_two, norm_two_back = jax.vjp(rms_norm, hidden, gains[1])
    ffn_rows = gather_tensor(normed_two.astype(BFLOAT))
    last_group = last[0]
    back = groups[:-1][::-1]
    gu_plan, stay = plan(order, last_group)
    down_plan, down_stay = plan(order, back[0])
    keep, give, out_keep, out_give, *found = call(
        functools.partial(
            ffn_kernel, column_runs(gu_places, order), column_runs(down_places, order), gu_plan, down_plan
        ),
        [halves] * 4
        + product_shapes(stay, rows, 2 * ff_local, last_group)
        + product_shapes(down_stay, rows, ff_local, back[0]),
        core,
        ffn_rows,
        cot_rows,
        *gu_parts,
        *down_parts,
        scratch=[pltpu.VMEM((length, 2 * ff_local), BFLOAT), pltpu.VMEM((length, ff_local), BFLOAT)],
    )
    gu_found, down_found = found[: len(gu_plan)], found[len(gu_plan) :]
    gu_kept, gu_sent = gu_found[0], gu_found[1:]
    down_kept, down_sent = down_found[0], down_found[1:]
    gu_sent, down_sent, seg_row = together(gu_sent, down_sent, seg_row)
    gu_got = send(gu_sent, last_group, count)
    down_got = send(down_sent, back[0], count)
    normed_two_grad = finish_tensor(keep, give, shard_index)
    hidden_norm_grad, gain_two_grad = norm_two_back(normed_two_grad)
    hidden_grad = cot_local.astype(FLOAT) + hidden_norm_grad
    mix_grad_rows = gather_tensor(hidden_grad.astype(BFLOAT))
    gu_got, down_got, mix_grad_rows, seg_row = together(gu_got, down_got, mix_grad_rows, seg_row)
    if len(back) == 1 and rows % 16 == 0:
        gu_kept, gu_sent, _ = add_split(gu_kept, gu_got, stay, back[0], [rows])
        gu_sent, mix_grad_rows = together(gu_sent, mix_grad_rows)
        gu_got = send(gu_sent, back[0], count)
    else:
        gu_kept, gu_got = finish(gu_kept, gu_got, stay, back, count)
    zq_low, pre_grad, skip_lanes, kv_grad = call(
        gate_back_kernel,
        [
            ((length, width_local + 128), BFLOAT),
            ((length, width_local), FLOAT),
            ((8, 128), FLOAT),
            ((length, 256), FLOAT),
        ],
        owner,
        mix_grad_rows,
        mid_near,
        mid_far,
        gates,
        mixer_low,
        seg_wide,
        seg_row,
    )
    dt_start = width_local + query_cols
    mid_kept, mid_sent, _ = parted(
        [(normed_rows, zq_low), (mix_grad_rows, mixed_low)], order, last_group
    )
    mid_sent, seg_row = together(mid_sent, seg_row)
    mid_got = send(mid_sent, last_group, count)
    in_low, taps_grad, head_grad, share_terms = call(
        functools.partial(mixer_back_kernel, head_local),
        [
            ((length, width_local + 128), BFLOAT),
            ((8, conv_width), FLOAT),
            ((8, 128), FLOAT),
            ((length, share_cols), FLOAT),
        ],
        owner,
        pre_grad,
        mixer_kept,
        mixer_low,
        kv_grad,
        taps,
        head_pack,
        seg_wide,
        seg_row,
        scratch=[pltpu.VMEM((length, conv_width), FLOAT)],
    )
    share_terms = share_terms + swap(share_terms, "tensor", 4, 1)
    share_terms = share_terms + swap(share_terms.astype(BFLOAT), "tensor", 4, 2).astype(FLOAT)
    share_low = share_terms.astype(BFLOAT)
    block_width = share_cols // 4
    shared_mine = lax.dynamic_slice_in_dim(shared_full, shard_index * block_width, block_width, 1)
    block_low = lax.dynamic_slice_in_dim(share_low, shard_index * block_width, block_width, 1)
    share_grad = einsum_f32("ld,lk->dk", normed_rows, share_low).reshape(count, 4, share_rows, share_cols)
    share_grad = lax.dynamic_index_in_dim(share_grad, shard_index, 1, keepdims=False)
    share_grad = share_grad.reshape(count * share_rows, share_cols)
    in_kept, in_sent, _ = parted([(normed_rows, in_low)], order, last_group)
    share_kept, share_sent, _ = split(share_grad, order, last_group, [share_rows])
    in_kept = jnp.concatenate([in_kept, share_kept], axis=0)
    in_sent = [jnp.concatenate(pair, axis=0) for pair in zip(in_sent, share_sent)]
    mid_got, gu_got, block_low, in_sent = together(mid_got, gu_got, block_low, in_sent)
    gu_sum = add(gu_kept, gu_got)
    mid_kept, mid_got = finish(mid_kept, mid_got, stay, back, count)
    in_got = send(in_sent, last_group, count)
    keep, give = call(
        input_back_kernel,
        [halves, halves],
        core,
        in_low,
        zq_low,
        block_low,
        early_near,
        early_far,
        mid_near,
        mid_far,
        shared_mine,
    )
    normed_one_grad = finish_tensor(keep, give, shard_index)
    token_norm_grad, gain_one_grad = norm_one_back(normed_one_grad)
    conv_full = lax.dynamic_update_slice_in_dim(
        jnp.zeros_like(conv_params), taps_grad[:5, :width_local], shard_index * width_local, 1
    )
    conv_full = conv_full.at[:, bc_start:].set(taps_grad[:5, width_local:])
    head_full = lax.dynamic_update_slice_in_dim(
        jnp.zeros_like(head_params),
        jnp.concatenate([head_grad[:2, :head_local], skip_lanes[:1, :head_local]], axis=0),
        shard_index * head_local,
        1,
    )
    wide = conv_params.shape[1]
    features, head_count = gains.shape[1], head_params.shape[1]
    gains_grad = relocate([jnp.stack([gain_one_grad, gain_two_grad])], dp_index, count, False)[0]
    small = jnp.concatenate(
        [
            jnp.pad(
                jnp.concatenate([gains_grad, head_full[:2]], axis=1),
                ((0, 0), (0, wide - features - head_count)),
            ),
            conv_full,
            jnp.pad(head_full[2:], ((0, 0), (0, wide - head_count))),
        ],
        axis=0,
    )
    for bits in (1, 2):
        small = group_sum(small, "tensor", 4, [bits])
    in_got, mid_got, down_got, out_give, small = together(in_got, mid_got, down_got, out_give, small)
    if len(back) == 1 and share_rows % 16 == 0:
        in_kept, in_sent, _ = add_split(in_kept, in_got, stay, back[0], [rows, share_rows])
        in_sent, mid_kept, mid_got, down_kept, down_got, out_give = together(
            in_sent, mid_kept, mid_got, down_kept, down_got, out_give
        )
        in_sum = add(in_kept, send(in_sent, back[0], count))
    else:
        in_sum = add(*finish(in_kept, in_got, stay, back, count, [rows, share_rows]))
    mid_sum = add(mid_kept, mid_got)
    down_sum = add(*finish(down_kept, down_got, down_stay, back[1:] + last, count))
    ffn_sum = finish_tensor(out_keep, out_give, shard_index)
    output = (hidden + ffn_sum).astype(BFLOAT)
    z_sum = mid_sum[:, :dt_start]
    out_sum = mid_sum[:, dt_start:]
    small = group_sum(small, "dp", count, last_group)
    small, in_sum, output = together(small, in_sum, output)
    for group in first:
        small = group_sum(small, "dp", count, group)
    shared_sum = in_sum[rows:]
    in_sum = in_sum[:rows]
    return (
        *relocate([output, hidden_grad + token_norm_grad], dp_index, count, False),
        jnp.stack([z_sum[:, :width_local], in_sum[:, :width_local]]),
        in_sum[:, width_local : width_local + head_local],
        z_sum[:, width_local:],
        out_sum[:, :width_local].T,
        out_sum[:, width_local:].T,
        jnp.stack([gu_sum[:, :ff_local], gu_sum[:, ff_local:]]),
        down_sum.T,
        shared_sum,
        small[:2, :features],
        small[2:7],
        jnp.concatenate(
            [small[:2, features : features + head_count], small[7:, :head_count]], axis=0
        ),
    )


def solution(mesh):
    count = mesh.shape["dp"]
    placed = (
        P(("dp", "tensor"), None),
        P("dp"),
        P(None, "dp", "tensor"),
        P("dp", "tensor"),
        P("dp", "tensor"),
        P("tensor", "dp"),
        P("tensor", "dp"),
        P(None, "dp", "tensor"),
        P("tensor", "dp"),
        P(("dp", "tensor"), None),
        P(),
        P(),
        P(),
        P(("dp", "tensor"), None),
    )

    def body(*arrays):
        return per_device(count, *arrays)

    return jax.shard_map(
        body,
        mesh=mesh,
        in_specs=placed,
        out_specs=(
            P(("dp", "tensor"), None),
            P(("dp", "tensor"), None),
            P(None, "dp", "tensor"),
            P("dp", "tensor"),
            P("dp", "tensor"),
            P("tensor", "dp"),
            P("tensor", "dp"),
            P(None, "dp", "tensor"),
            P("tensor", "dp"),
            P(("dp", "tensor"), None),
            P(),
            P(),
            P(),
        ),
        check_vma=False,
    )
```
